32 devices in a mesh: grp: 2 (over x), tm: 16 (over z, y, core).
Axes of the slice: x: 2, y: 2, z: 4, core: 2. Of those that a mesh axis runs over, the one named last changes fastest.
Arguments:
- inputs: bfloat16 [2, 2048, 1536], P('grp', 'tm'), may hold values from -16 to 16
- norm_gain: float32 [1536], replicated, may hold values from 0.1 to 1.9
- query_weight: bfloat16 [1536, 768], P('tm', 'grp'), may hold values from -0.15625 to 0.15625
- key_weight: bfloat16 [1536, 768], P('tm', 'grp'), may hold values from -0.15625 to 0.15625
- value_weight: bfloat16 [1536, 768], P('tm', 'grp'), may hold values from -0.15625 to 0.15625
- output_weight: bfloat16 [1536, 768], P('tm', 'grp'), may hold values from -0.5 to 0.5
- content_bias: float32 [768], replicated, may hold values from -4 to 4
- position_bias: float32 [768], replicated, may hold values from -4 to 4
- position_keys: bfloat16 [256, 768], replicated, may hold values from -6 to 6
- start_flags: int32 [2, 16], P('grp', 'tm'), may hold values from 0 to 1, as said below
- cotangent: bfloat16 [2, 2048, 1536], P('grp', 'tm'), may hold values from -6 to 6
Outputs:
- layer_out: bfloat16 [2, 2048, 1536], P('grp', 'tm')
- input_grad: bfloat16 [2, 2048, 1536], P('grp', 'tm')
The draws below stay inside these ranges and needn't reach their ends.
Inputs may be any that keep to these rules, and one draw needn't show every extreme that they name: start_flags[r, 0] is 1 for every recording r.
All inputs are finite; a program needn't handle non-finite values.
Results may differ from the reference program's by a relative error of at most 0.013.
Values may be sent and summed in bfloat16 or wider, within the bound.
No kernel may reach another device: no remote copies, remote signals or barrier semaphores. Data moves between devices by JAX's collectives and lax.ppermute only.
A program may use at most 64 MiB of HBM per device.

```python
import jax
import jax.numpy as jnp
from jax import lax

D = 1536
H = 6
DH = 128
HD = 768
SEG = 128
NREC = 2
NSEG = 16
TOKENS = 2048
KEYS = 256


def draw_inputs(key, part):
    key = jax.random.fold_in(key, 3)
    base_key = jax.random.fold_in(key, 2)
    result = jnp.clip(jax.random.normal(base_key, (NREC, TOKENS, D), jnp.float32), -6.0, 6.0)
    return result.astype(jnp.bfloat16)


def draw_position_bias(key, part):
    key = jax.random.fold_in(key, 11)
    result = jnp.clip(0.5 * jax.random.normal(key, (HD,), jnp.float32), -2.0, 2.0)
    return result


def draw_position_keys(key, part):
    key = jax.random.fold_in(key, 13)
    result = jnp.clip(jax.random.normal(key, (KEYS, HD), jnp.float32), -4.0, 4.0)
    return result.astype(jnp.bfloat16)


def draw_start_flags(key, part):
    key = jax.random.fold_in(key, 7)
    raw_draw = jax.random.randint(key, (NREC, NSEG), 0, 8)
    flags_drawn = (raw_draw == 0).astype(jnp.int32)
    column = jnp.arange(NSEG)[None, :]
    return jnp.where(column == 0, 1, flags_drawn).astype(jnp.int32)


def steps_of(rng, dims, shards, smallest, top_value):
    loudness, own = 1.0, jax.random.fold_in(rng, 6)
    for dim, shards_of in shards:
        draws = jnp.exp(jax.random.uniform(jax.random.fold_in(own, dim), (shards_of,), jnp.float32, smallest / len(shards), top_value / len(shards)))
        loudness = loudness * jnp.repeat(draws, dims[dim] // shards_of).reshape([-1 if axis == dim else 1 for axis in range(len(dims))])
    return loudness


def normal_values(own_key, extent, scale, bound, shards=(), kind=jnp.bfloat16):
    entries = scale * jax.random.normal(own_key, extent, jnp.float32)
    if shards:
        entries = entries * steps_of(own_key, extent, shards, -0.22, 0.18)
    return jnp.clip(entries, -bound, bound).astype(kind)


def setup_inputs(seed: int = 0) -> dict:
    arg_keys = jax.random.split(jax.random.key(seed), 12)
    return {
        "inputs": draw_inputs(jax.random.fold_in(arg_keys[11], 71), 0),
        "norm_gain": jnp.clip(1.0 + 0.18 * jax.random.normal(arg_keys[1], (D,), jnp.float32), 0.1, 1.9),
        "query_weight": normal_values(arg_keys[2], (D, HD), D ** -0.5, 0.15625, ((0, 16), (1, 2))),
        "key_weight": normal_values(arg_keys[3], (D, HD), D ** -0.5, 0.15625, ((0, 16), (1, 2))),
        "value_weight": normal_values(arg_keys[4], (D, HD), D ** -0.5, 0.15625, ((0, 16), (1, 2))),
        "output_weight": normal_values(arg_keys[5], (D, HD), DH ** -0.5, 0.5, ((0, 16), (1, 2))),
        "content_bias": normal_values(arg_keys[6], (HD,), 0.5, 4.0, (), jnp.float32),
        "position_bias": draw_position_bias(jax.random.fold_in(arg_keys[11], 71), 0),
        "position_keys": draw_position_keys(jax.random.fold_in(arg_keys[11], 71), 0),
        "start_flags": draw_start_flags(jax.random.fold_in(arg_keys[11], 71), 0),
        "cotangent": normal_values(arg_keys[10], (NREC, TOKENS, D), 1.0, 6.0, ((0, 2), (1, 16))),
    }


epsilon = 1e-05

def normalize_project(inputs, norm_gain, query_weight, key_weight, value_weight, content_bias, position_bias):
    widened = inputs.astype(jnp.float32)
    center = lax.optimization_barrier(jnp.mean(widened, axis=-1, keepdims=True))
    spread = lax.optimization_barrier(jnp.mean(jnp.square(widened - center), axis=-1, keepdims=True))
    normed = ((widened - center) * lax.rsqrt(spread + epsilon) * norm_gain).astype(jnp.bfloat16)
    projected = jnp.dot(normed, query_weight, preferred_element_type=jnp.float32)
    content_query = (projected + content_bias).astype(jnp.bfloat16)
    position_query = (projected + position_bias).astype(jnp.bfloat16)
    key_rows = jnp.dot(normed, key_weight, preferred_element_type=jnp.float32).astype(jnp.bfloat16)
    value_rows = jnp.dot(normed, value_weight, preferred_element_type=jnp.float32).astype(jnp.bfloat16)
    return (content_query, position_query, key_rows, value_rows)

def attend(content_query, position_query, key_rows, value_rows, memory_keys, memory_values, position_keys, keep_memory):
    length = content_query.shape[0]
    all_keys = jnp.concatenate([memory_keys, key_rows], axis=0).reshape(2 * length, H, DH)
    all_values = jnp.concatenate([memory_values, value_rows], axis=0).reshape(2 * length, H, DH)
    content = content_query.reshape(length, H, DH)
    located = position_query.reshape(length, H, DH)
    distance_keys = position_keys[::-1].reshape(2 * length, H, DH)
    direct = jnp.einsum('ihd,jhd->hij', content.astype(jnp.float32), all_keys.astype(jnp.float32))
    relative = jnp.einsum('ihd,jhd->hij', located.astype(jnp.float32), distance_keys.astype(jnp.float32))
    padded = jnp.pad(relative, ((0, 0), (0, 0), (0, 1)))
    skewed = padded.reshape(H, length * (2 * length + 1))[:, length - 1:length - 1 + 2 * length * length]
    skewed = skewed.reshape(H, length, 2 * length)
    scores = (direct + skewed) * DH ** (-0.5)
    key_index = lax.broadcasted_iota(jnp.int32, (length, 2 * length), 1)
    query_index = lax.broadcasted_iota(jnp.int32, (length, 2 * length), 0)
    allowed = (key_index <= query_index + length) & (keep_memory | (key_index >= length))
    scores = jnp.where(allowed[None], scores, -jnp.inf)
    row_peak = lax.stop_gradient(lax.optimization_barrier(jnp.max(scores, axis=-1, keepdims=True)))
    raised = jnp.exp(scores - row_peak)
    attention = (raised / lax.optimization_barrier(jnp.sum(raised, axis=-1, keepdims=True))).astype(jnp.bfloat16)
    gathered = jnp.einsum('hij,jhd->ihd', attention.astype(jnp.float32), all_values.astype(jnp.float32))
    return gathered.reshape(length, H * DH).astype(jnp.bfloat16)

def finish(inputs, context, output_weight):
    update = lax.dot_general(context, output_weight, (((context.ndim - 1,), (1,)), ((), ())), preferred_element_type=jnp.float32)
    return (inputs.astype(jnp.float32) + update).astype(jnp.bfloat16)

def reference(inputs, norm_gain, query_weight, key_weight, value_weight, output_weight, content_bias, position_bias, position_keys, start_flags, cotangent):

    def forward(whole_inputs):
        content_query, position_query, key_rows, value_rows = normalize_project(whole_inputs, norm_gain, query_weight, key_weight, value_weight, content_bias, position_bias)

        def per_segment(array):
            return array.reshape(NREC * NSEG, SEG, HD)
        key_blocks = key_rows.reshape(NREC, NSEG, SEG, HD)
        value_blocks = value_rows.reshape(NREC, NSEG, SEG, HD)
        memory_keys = jnp.concatenate([jnp.zeros_like(key_blocks[:, :1]), key_blocks[:, :-1]], axis=1)
        memory_values = jnp.concatenate([jnp.zeros_like(value_blocks[:, :1]), value_blocks[:, :-1]], axis=1)
        keep_memory = (start_flags == 0).reshape(NREC * NSEG)

        def one_segment(pieces):
            return attend(pieces[0], pieces[1], pieces[2], pieces[3], pieces[4], pieces[5], position_keys, pieces[6])
        context = lax.map(jax.checkpoint(one_segment), (per_segment(content_query), per_segment(position_query), per_segment(key_rows), per_segment(value_rows), per_segment(memory_keys), per_segment(memory_values), keep_memory))
        context = context.reshape(NREC, TOKENS, HD)
        return finish(whole_inputs, context, output_weight)
    layer_out, pullback = jax.vjp(forward, inputs)
    input_grad, = pullback(cotangent)
    return (layer_out, input_grad)
```

```python
import jax
import jax.numpy as jnp
from jax import lax
from jax.experimental import pallas as pl
from jax.experimental.pallas import tpu as pltpu
from jax.sharding import PartitionSpec as P

H = 6
DH = 128
epsilon = 1e-05

F32 = jnp.float32
BF16 = jnp.bfloat16
SEG = 128
D = 1536
HALF = 384
HEADS = HALF // DH
ROWS = 96
ZS = 4
BLK = 4 * ROWS
NT = (((1,), (1,)), ((), ()))
TN = (((0,), (0,)), ((), ()))
VMEM_LIMIT = 48 * 1024 * 1024


def dot(a, b, dims=(((1,), (0,)), ((), ()))):
    return lax.dot_general(a, b, dims, preferred_element_type=F32)


def place():
    t = lax.axis_index("tm")
    return t // 4, (t // 2) % 2, t % 2


def plane_columns(z, r):
    return pl.ds(pl.multiple_of(lax.rem(z - r + ZS, ZS) * BLK, 128), BLK)


def normalize_kernel(x_ref, gain_ref, flag_ref, out_ref, held):
    z, _, _ = place()
    x = x_ref[...].astype(F32)
    center = jnp.mean(x, axis=-1, keepdims=True)
    moved = x - center
    spread = jnp.mean(jnp.square(moved), axis=-1, keepdims=True)
    held[...] = (moved * lax.rsqrt(spread + epsilon) * gain_ref[...]).astype(BF16)
    for r in range(ZS):
        out_ref[0:SEG, r * BLK : (r + 1) * BLK] = held[:, plane_columns(z, r)]
    flag = flag_ref[0, 0].astype(F32)
    out_ref[SEG:, :] = jnp.full((16, D), flag, F32).astype(BF16)


def shard_rows(j):
    _, y, c = place()
    yy = 1 - y if j % 2 else y
    cc = 1 - c if j // 2 else c
    return (2 * yy + cc) * ROWS


def fetch_qkv(pieces, weights, sems):
    copies = []
    for r in range(ZS):
        for j in range(4):
            rows = pl.ds(pl.multiple_of(r * BLK + shard_rows(j), 16), ROWS)
            for w in range(3):
                n = (r * 4 + j) * 3 + w
                copies.append(
                    pltpu.make_async_copy(
                        pieces[r * 4 + j].at[w],
                        weights.at[rows, pl.ds(w * HALF, HALF)],
                        sems.at[n],
                    )
                )
    for copy in copies:
        copy.start()
    return copies


def project_kernel(own_ref, oth_ref, cb_ref, pb_ref, *rest):
    pieces, (kv_ref, cq_ref, pq_ref, flags), (weights, xs, sems) = rest[:16], rest[16:20], rest[20:]
    flags[0] = own_ref[SEG:, :DH]
    flags[1] = oth_ref[SEG:, :DH]
    copies = fetch_qkv(pieces, weights, sems)
    xs[0:SEG, :] = own_ref[0:SEG, :]
    xs[SEG:, :] = oth_ref[0:SEG, :]
    total = None
    for half in range(2):
        for copy in copies[half * 24 : half * 24 + 24]:
            copy.wait()
        rows = slice(half * 2 * BLK, (half + 1) * 2 * BLK)
        part = dot(xs[:, rows], weights[rows, :])
        total = part if total is None else total + part
    for rec in range(2):
        rows = slice(rec * SEG, (rec + 1) * SEG)
        kv_ref[rec] = total[rows, 0 : 2 * HALF].astype(BF16)
        q = total[rows, 2 * HALF :]
        cq_ref[rec] = (q + cb_ref[...]).astype(BF16)
        pq_ref[rec] = (q + pb_ref[...]).astype(BF16)


def attend_kernel(flags, cq_ref, pq_ref, kv_ref, mem_ref, pk_ref, p_ref, ctx_ref):
    row = lax.broadcasted_iota(jnp.int32, (SEG, SEG), 0)
    col = lax.broadcasted_iota(jnp.int32, (SEG, SEG), 1)
    scale = DH**-0.5
    for rec in range(2):
        flag = flags[rec, 0:1, :].astype(F32)
        for h in range(HEADS):
            f = slice(h * DH, (h + 1) * DH)
            fv = slice(HALF + h * DH, HALF + (h + 1) * DH)
            cq = cq_ref[rec, :, f]
            rel = dot(pq_ref[rec, :, f], pk_ref[:, f], NT)
            rel = pltpu.roll(rel, SEG + 1, 1, stride=1, stride_axis=0)
            s_mem = (dot(cq, mem_ref[rec, :, f], NT) + rel[:, :SEG]) * scale
            s_own = (dot(cq, kv_ref[rec, :, f], NT) + rel[:, SEG:]) * scale
            s_mem = jnp.where(flag == 0, s_mem, -jnp.inf)
            s_own = jnp.where(col <= row, s_own, -jnp.inf)
            peak = jnp.maximum(
                jnp.max(s_mem, axis=-1, keepdims=True), jnp.max(s_own, axis=-1, keepdims=True)
            )
            e_mem = jnp.exp(s_mem - peak)
            e_own = jnp.exp(s_own - peak)
            norm = 1.0 / (
                jnp.sum(e_mem, axis=-1, keepdims=True) + jnp.sum(e_own, axis=-1, keepdims=True)
            )
            p_mem = (e_mem * norm).astype(BF16)
            p_own = (e_own * norm).astype(BF16)
            p_ref[rec, h, :, :SEG] = p_mem
            p_ref[rec, h, :, SEG:] = p_own
            ctx = dot(p_mem, mem_ref[rec, :, fv]) + dot(p_own, kv_ref[rec, :, fv])
            ctx_ref[rec, :, f] = ctx.astype(BF16)


def back_kernel(
    x_ref, cot_own, cot_oth, p_ref, ctx_ref, cq_ref, kv_ref, mem_ref, pk_ref, *rest
):
    pieces = rest[:8]
    lo_own, lo_oth, d_ref, dmem_ref = rest[8:12]
    wo, cots, cg, sems = rest[12:]
    z, _, _ = place()
    copies = []
    for r in range(ZS):
        for j in range(4):
            rows = pl.ds(pl.multiple_of(r * BLK + shard_rows(j), 16), ROWS)
            src = pieces[r * 2 + j // 2].at[j % 2]
            copies.append(pltpu.make_async_copy(src, wo.at[rows, :], sems.at[r * 4 + j]))
    for copy in copies:
        copy.start()
    for r in range(ZS):
        cots[0:SEG, r * BLK : (r + 1) * BLK] = cot_own[:, plane_columns(z, r)]
        cots[SEG:, r * BLK : (r + 1) * BLK] = cot_oth[:, plane_columns(z, r)]
    for copy in copies:
        copy.wait()
    cg[...] = dot(cots[...], wo[...]).astype(BF16)
    lo_oth[...] = dot(ctx_ref[1], wo[...], NT).astype(BF16)
    lo = dot(ctx_ref[0], wo[...], NT)
    for r in range(ZS):
        lo_own[:, plane_columns(z, r)] = (
            x_ref[:, plane_columns(z, r)].astype(F32) + lo[:, r * BLK : (r + 1) * BLK]
        )
    row = lax.broadcasted_iota(jnp.int32, (SEG, SEG), 0)
    col = lax.broadcasted_iota(jnp.int32, (SEG, SEG), 1)
    flip = jnp.where(row + col == SEG - 1, 1.0, 0.0).astype(BF16)
    scale = DH**-0.5
    for rec in range(2):
        for h in range(HEADS):
            f = slice(h * DH, (h + 1) * DH)
            fv = slice(HALF + h * DH, HALF + (h + 1) * DH)
            fq = slice(2 * HALF + h * DH, 2 * HALF + (h + 1) * DH)
            g = cg[rec * SEG : (rec + 1) * SEG, f]
            cq = cq_ref[rec, :, f]
            k_mem, k_own = mem_ref[rec, :, f], kv_ref[rec, :, f]
            p_mem, p_own = p_ref[rec, h, :, :SEG], p_ref[rec, h, :, SEG:]
            dp_mem = dot(g, mem_ref[rec, :, fv], NT)
            dp_own = dot(g, kv_ref[rec, :, fv], NT)
            a_mem, a_own = p_mem.astype(F32), p_own.astype(F32)
            inner = jnp.sum(a_mem * dp_mem + a_own * dp_own, axis=-1, keepdims=True)
            ds_mem = a_mem * (dp_mem - inner) * scale
            ds_own = a_own * (dp_own - inner) * scale
            b_mem, b_own = ds_mem.astype(BF16), ds_own.astype(BF16)
            rel = dot(flip, jnp.concatenate([b_mem, b_own], axis=1))
            rel = pltpu.roll(rel, 0, 1, stride=1, stride_axis=0).astype(BF16)
            rel = dot(flip, rel).astype(BF16)
            dq = dot(b_mem, k_mem) + dot(b_own, k_own) + dot(rel, pk_ref[:, f])
            d_ref[rec, :, f] = dot(b_own, cq, TN).astype(BF16)
            d_ref[rec, :, fv] = dot(p_own, g, TN).astype(BF16)
            d_ref[rec, :, fq] = dq.astype(BF16)
            dmem_ref[rec, :, f] = dot(b_mem, cq, TN).astype(BF16)
            dmem_ref[rec, :, fv] = dot(p_mem, g, TN).astype(BF16)


def unproject_kernel(d_ref, ret_ref, *rest):
    pieces, (np_own, np_oth), (weights, ds, sems) = rest[:16], rest[16:18], rest[18:]
    copies = fetch_qkv(pieces, weights, sems)
    for rec in range(2):
        rows = slice(rec * SEG, (rec + 1) * SEG)
        kv = d_ref[rec, :, : 2 * HALF].astype(F32) + ret_ref[rec].astype(F32)
        ds[rows, : 2 * HALF] = kv.astype(BF16)
        ds[rows, 2 * HALF :] = d_ref[rec, :, 2 * HALF :]
    for half in range(2):
        for copy in copies[half * 24 : half * 24 + 24]:
            copy.wait()
        rows = slice(half * 2 * BLK, (half + 1) * 2 * BLK)
        part = dot(ds[...], weights[rows, :], NT)
        np_own[:, rows] = part[:SEG]
        np_oth[:, rows] = part[SEG:].astype(BF16)


def finish_kernel(
    x_ref, gain_ref, cot_ref, np_own, np_ret, lo_own, lo_ret, out_ref, grad_ref, total
):
    z, _, _ = place()
    for r in range(ZS):
        cols = slice(r * BLK, (r + 1) * BLK)
        there = plane_columns(z, r)
        total[:, there] = np_own[:, cols] + np_ret[:, cols].astype(F32)
        out_ref[:, there] = (lo_own[:, there] + lo_ret[:, cols].astype(F32)).astype(BF16)
    x = x_ref[...].astype(F32)
    center = jnp.mean(x, axis=-1, keepdims=True)
    moved = x - center
    spread = jnp.mean(jnp.square(moved), axis=-1, keepdims=True)
    rstd = lax.rsqrt(spread + epsilon)
    hat = moved * rstd
    g = total[...] * gain_ref[...]
    mean_g = jnp.mean(g, axis=-1, keepdims=True)
    mean_gh = jnp.mean(g * hat, axis=-1, keepdims=True)
    grad = (rstd * (g - mean_g - hat * mean_gh)).astype(BF16)
    grad_ref[...] = cot_ref[...] + grad


def call(kernel, outs, scratch=(), in_specs=None, flops=0, nbytes=0):
    return pl.pallas_call(
        kernel,
        out_shape=outs,
        in_specs=in_specs,
        out_specs=jax.tree.map(lambda _: pl.BlockSpec(memory_space=pltpu.VMEM), outs),
        scratch_shapes=list(scratch),
        compiler_params=pltpu.CompilerParams(vmem_limit_bytes=VMEM_LIMIT),
        cost_estimate=pl.CostEstimate(flops=flops, bytes_accessed=nbytes, transcendentals=0),
    )


def shape(*dims, dtype=BF16):
    return jax.ShapeDtypeStruct(dims, dtype)


VM = pl.BlockSpec(memory_space=pltpu.VMEM)
SM = pl.BlockSpec(memory_space=pltpu.SMEM)
ANY = pl.BlockSpec(memory_space=pl.ANY)


def moved_by(f):
    route = []
    for z in range(ZS):
        for y in range(2):
            for c in range(2):
                zz, yy, cc = f(z, y, c)
                route.append((4 * z + 2 * y + c, 4 * zz + 2 * yy + cc))
    return lambda block: lax.ppermute(block, "tm", route)


up = moved_by(lambda z, y, c: ((z + 1) % ZS, y, c))
down = moved_by(lambda z, y, c: ((z - 1) % ZS, y, c))
across = moved_by(lambda z, y, c: (z, 1 - y, c))
sibling = moved_by(lambda z, y, c: (z, y, 1 - c))


def other(block):
    return lax.ppermute(block, "grp", [(0, 1), (1, 0)])


def split_heads(
    inputs,
    norm_gain,
    query_weight,
    key_weight,
    value_weight,
    output_weight,
    content_bias,
    position_bias,
    position_keys,
    start_flags,
    cotangent,
):
    g = lax.axis_index("grp")
    x, cot = inputs[0], cotangent[0]
    gain = norm_gain[None]
    cb = lax.dynamic_slice_in_dim(content_bias, g * HALF, HALF)[None]
    pb = lax.dynamic_slice_in_dim(position_bias, g * HALF, HALF)[None]
    pk = lax.dynamic_slice_in_dim(position_keys, g * HALF, HALF, axis=1)[::-1]

    shard = jnp.stack([key_weight, value_weight, query_weight, output_weight])
    qkv = shard[:3]
    normed = call(
        normalize_kernel,
        shape(SEG + 16, D),
        [pltpu.VMEM((SEG, D), BF16)],
        [VM, VM, SM],
    )(x, gain, start_flags)
    normed_oth = other(normed)
    cot_oth = other(cot)

    shard_y = across(shard)
    a1, a3 = up(qkv), down(qkv)
    a2 = up(a1)
    a1y, a3y, a2y = across(a1), across(a3), across(a2)
    b0 = jnp.stack([output_weight, shard_y[3]])
    b1, b3 = up(b0), down(b0)
    b2 = up(b1)
    qkv_y = shard_y[:3]
    here = [qkv, qkv_y, a1, a1y, a2, a2y, a3, a3y]
    there = [sibling(p) for p in here]
    pieces = []
    for r in range(ZS):
        pieces += here[2 * r : 2 * r + 2] + there[2 * r : 2 * r + 2]
    out_here = [b0, b1, b2, b3]
    out_there = [sibling(p) for p in out_here]
    out_pieces = []
    for r in range(ZS):
        out_pieces += [out_here[r], out_there[r]]

    kv, cq, pq, flags = call(
        project_kernel,
        (
            shape(2, SEG, 2 * HALF),
            shape(2, SEG, HALF),
            shape(2, SEG, HALF),
            shape(2, 16, DH),
        ),
        [
            pltpu.VMEM((D, 3 * HALF), BF16),
            pltpu.VMEM((2 * SEG, D), BF16),
            pltpu.SemaphoreType.DMA((48,)),
        ],
        [VM, VM, VM, VM] + [ANY] * 16,
    )(normed, normed_oth, cb, pb, *pieces)

    steps = lax.axis_size("tm")
    mem = lax.ppermute(kv, "tm", [(i, i + 1) for i in range(steps - 1)])
    p, ctx = call(
        attend_kernel,
        (shape(2, HEADS, SEG, 2 * SEG), shape(2, SEG, HALF)),
        (),
        [VM] * 6,
    )(flags, cq, pq, kv, mem, pk)

    lo_own, lo_oth, d, dmem = call(
        back_kernel,
        (
            shape(SEG, D, dtype=F32),
            shape(SEG, D),
            shape(2, SEG, 3 * HALF),
            shape(2, SEG, 2 * HALF),
        ),
        [
            pltpu.VMEM((D, HALF), BF16),
            pltpu.VMEM((2 * SEG, D), BF16),
            pltpu.VMEM((2 * SEG, HALF), BF16),
            pltpu.SemaphoreType.DMA((16,)),
        ],
        [VM] * 9 + [ANY] * 8,
    )(x, cot, cot_oth, p, ctx, cq, kv, mem, pk, *out_pieces)
    lo_ret = other(lo_oth)
    ret = lax.ppermute(dmem, "tm", [(i + 1, i) for i in range(steps - 1)])
    np_own, np_oth = call(
        unproject_kernel,
        (shape(SEG, D, dtype=F32), shape(SEG, D)),
        [
            pltpu.VMEM((D, 3 * HALF), BF16),
            pltpu.VMEM((2 * SEG, 3 * HALF), BF16),
            pltpu.SemaphoreType.DMA((48,)),
        ],
        [VM, VM] + [ANY] * 16,
    )(d, ret, *pieces)
    np_ret = other(np_oth)
    layer_out, input_grad = call(
        finish_kernel,
        (shape(SEG, D), shape(SEG, D)),
        [pltpu.VMEM((SEG, D), F32)],
        [VM] * 7,
    )(x, gain, cot, np_own, np_ret, lo_own, lo_ret)
    return (layer_out[None], input_grad[None])


def from_behind(block, axis, distance):
    devices = range(lax.axis_size(axis))
    route = [(i - distance, i) for i in devices if i - distance in devices]
    return lax.ppermute(block, axis, route)


def normalize_project(
    inputs, norm_gain, query_weight, key_weight, value_weight, content_bias, position_bias
):
    widened = inputs.astype(jnp.float32)
    center = jnp.mean(widened, axis=-1, keepdims=True)
    spread = jnp.mean(jnp.square(widened - center), axis=-1, keepdims=True)
    normed = ((widened - center) * lax.rsqrt(spread + epsilon) * norm_gain).astype(jnp.bfloat16)
    projected = jnp.dot(normed, query_weight, preferred_element_type=jnp.float32)
    content_query = (projected + content_bias).astype(jnp.bfloat16)
    position_query = (projected + position_bias).astype(jnp.bfloat16)
    key_rows = jnp.dot(normed, key_weight, preferred_element_type=jnp.float32).astype(jnp.bfloat16)
    value_rows = jnp.dot(normed, value_weight, preferred_element_type=jnp.float32).astype(
        jnp.bfloat16
    )
    return (content_query, position_query, key_rows, value_rows)


def attend(
    content_query,
    position_query,
    key_rows,
    value_rows,
    memory_keys,
    memory_values,
    position_keys,
    keep_memory,
):
    length = content_query.shape[0]
    all_keys = jnp.concatenate([memory_keys, key_rows], axis=0).reshape(2 * length, H, DH)
    all_values = jnp.concatenate([memory_values, value_rows], axis=0).reshape(2 * length, H, DH)
    content = content_query.reshape(length, H, DH)
    located = position_query.reshape(length, H, DH)
    distance_keys = position_keys[::-1].reshape(2 * length, H, DH)
    direct = jnp.einsum("ihd,jhd->hij", content, all_keys, preferred_element_type=jnp.float32)
    relative = jnp.einsum(
        "ihd,jhd->hij", located, distance_keys, preferred_element_type=jnp.float32
    )
    padded = jnp.pad(relative, ((0, 0), (0, 0), (0, 1)))
    skewed = padded.reshape(H, length * (2 * length + 1))[
        :, length - 1 : length - 1 + 2 * length * length
    ]
    skewed = skewed.reshape(H, length, 2 * length)
    scores = (direct + skewed) * DH ** (-0.5)
    key_index = lax.broadcasted_iota(jnp.int32, (length, 2 * length), 1)
    query_index = lax.broadcasted_iota(jnp.int32, (length, 2 * length), 0)
    allowed = (key_index <= query_index + length) & (keep_memory | (key_index >= length))
    scores = jnp.where(allowed[None], scores, -jnp.inf)
    row_peak = lax.stop_gradient(jnp.max(scores, axis=-1, keepdims=True))
    raised = jnp.exp(scores - row_peak)
    attention = (raised / jnp.sum(raised, axis=-1, keepdims=True)).astype(jnp.bfloat16)
    gathered = jnp.einsum("hij,jhd->ihd", attention, all_values, preferred_element_type=jnp.float32)
    return gathered.reshape(length, H * DH).astype(jnp.bfloat16)


def finish(inputs, context, output_weight):
    update = lax.dot_general(
        context,
        output_weight,
        (((context.ndim - 1,), (1,)), ((), ())),
        preferred_element_type=jnp.float32,
    )
    return (inputs.astype(jnp.float32) + update).astype(jnp.bfloat16)


def shards(
    inputs,
    norm_gain,
    query_weight,
    key_weight,
    value_weight,
    output_weight,
    content_bias,
    position_bias,
    position_keys,
    start_flags,
    cotangent,
):
    partial_weights = (
        lax.all_gather(query_weight, "grp", axis=1, tiled=True),
        lax.all_gather(key_weight, "grp", axis=1, tiled=True),
        lax.all_gather(value_weight, "grp", axis=1, tiled=True),
        lax.all_gather(output_weight, "grp", axis=1, tiled=True),
    )
    full_weights = (
        lax.all_gather(partial_weights[0], "tm", axis=0, tiled=True),
        lax.all_gather(partial_weights[1], "tm", axis=0, tiled=True),
        lax.all_gather(partial_weights[2], "tm", axis=0, tiled=True),
        lax.all_gather(partial_weights[3], "tm", axis=0, tiled=True),
    )
    query_full, key_full, value_full, output_full = full_weights
    own_inputs = inputs[0]
    own_cotangent = cotangent[0]
    keep_memory = start_flags[0, 0] == 0

    def project(local_inputs):
        return normalize_project(
            local_inputs, norm_gain, query_full, key_full, value_full, content_bias, position_bias
        )

    projections, project_back = jax.vjp(project, own_inputs)
    content_query, position_query, key_rows, value_rows = projections
    memory_keys, memory_values = from_behind((key_rows, value_rows), "tm", 1)

    def attend_local(
        local_content, local_position, local_keys, local_values, prior_keys, prior_values
    ):
        return attend(
            local_content,
            local_position,
            local_keys,
            local_values,
            prior_keys,
            prior_values,
            position_keys,
            keep_memory,
        )

    context, attend_back = jax.vjp(
        attend_local,
        content_query,
        position_query,
        key_rows,
        value_rows,
        memory_keys,
        memory_values,
    )

    def combine(local_inputs, local_context):
        return finish(local_inputs, local_context, output_full)

    layer_out, finish_back = jax.vjp(combine, own_inputs, context)
    residual_grad, context_grad = finish_back(own_cotangent)
    attend_grads = attend_back(context_grad)
    returned_keys, returned_values = from_behind((attend_grads[4], attend_grads[5]), "tm", -1)
    key_grad = attend_grads[2] + returned_keys
    value_grad = attend_grads[3] + returned_values
    (norm_grad,) = project_back((attend_grads[0], attend_grads[1], key_grad, value_grad))
    input_grad = residual_grad + norm_grad
    return (layer_out[None], input_grad[None])


def solution(mesh):
    in_specs = (
        P("grp", "tm", None),
        P(),
        P("tm", "grp"),
        P("tm", "grp"),
        P("tm", "grp"),
        P("tm", "grp"),
        P(),
        P(),
        P(),
        P("grp", "tm"),
        P("grp", "tm", None),
    )
    out_specs = (P("grp", "tm", None), P("grp", "tm", None))
    split = dict(mesh.shape) == {"grp": 2, "tm": 4 * ZS}
    body = split_heads if split else shards
    return jax.shard_map(body, mesh=mesh, in_specs=in_specs, out_specs=out_specs, check_vma=False)
```

```python
import jax
import jax.numpy as jnp
from jax import lax
from jax.experimental import pallas as pl
from jax.experimental.pallas import tpu as pltpu
from jax.sharding import PartitionSpec as P

H = 6
DH = 128
epsilon = 1e-05

F32 = jnp.float32
BF16 = jnp.bfloat16
SEG = 128
D = 1536
HALF = 384
HEADS = HALF // DH
ROWS = 96
ZS = 4
BLK = 4 * ROWS
NT = (((1,), (1,)), ((), ()))
TN = (((0,), (0,)), ((), ()))
VMEM_LIMIT = 24 * 1024 * 1024


def dot(a, b, dims=(((1,), (0,)), ((), ()))):
    return lax.dot_general(a, b, dims, preferred_element_type=F32)


def place():
    t = lax.axis_index("tm")
    return t // 4, (t // 2) % 2, t % 2


def plane_columns(z, r):
    return pl.ds(pl.multiple_of(lax.rem(z - r + ZS, ZS) * BLK, 128), BLK)


def pack_kernel(k_ref, v_ref, q_ref, o_ref, out_ref, sems):
    copies = [
        pltpu.make_async_copy(ref, out_ref.at[i], sems.at[i])
        for i, ref in enumerate((k_ref, v_ref, q_ref, o_ref))
    ]
    for copy in copies:
        copy.start()
    for copy in copies:
        copy.wait()


def normalize_kernel(
    x_ref, gain_ref, flag_ref, cb_ref, pb_ref, pk_ref, out_ref, biases, pk_out, held
):
    z, _, _ = place()
    x = x_ref[...].astype(F32)
    center = jnp.mean(x, axis=-1, keepdims=True)
    moved = x - center
    spread = jnp.mean(jnp.square(moved), axis=-1, keepdims=True)
    held[...] = (moved * lax.rsqrt(spread + epsilon) * gain_ref[...]).astype(BF16)
    for r in range(ZS):
        out_ref[0:SEG, r * BLK : (r + 1) * BLK] = held[:, plane_columns(z, r)]
    flag = flag_ref[0, 0].astype(F32)
    out_ref[SEG:, :] = jnp.full((16, D), flag, F32).astype(BF16)
    own = pl.ds(pl.multiple_of(lax.axis_index("grp") * HALF, 128), HALF)
    biases[0:1, :] = cb_ref[:, own]
    biases[1:2, :] = pb_ref[:, own]
    row = lax.broadcasted_iota(jnp.int32, (2 * SEG, 2 * SEG), 0)
    col = lax.broadcasted_iota(jnp.int32, (2 * SEG, 2 * SEG), 1)
    flip = jnp.where(row + col == 2 * SEG - 1, 1.0, 0.0).astype(BF16)
    pk_out[...] = dot(flip, pk_ref[:, own]).astype(BF16)


def shard_rows(r, j):
    _, y, c = place()
    yy = 1 - y if j % 2 else y
    cc = 1 - c if j // 2 else c
    return pl.ds(pl.multiple_of(r * BLK + (2 * yy + cc) * ROWS, 16), ROWS)


def fetch(pieces, which, weights, sems):
    copies = []
    for n in range(4 * ZS):
        for w in range(2):
            copies.append(
                pltpu.make_async_copy(
                    pieces[n].at[which[n] + w],
                    weights.at[shard_rows(n // 4, n % 4), pl.ds(w * HALF, HALF)],
                    sems.at[2 * n + w],
                )
            )
    for copy in copies:
        copy.start()
    return copies


def accumulate(x, weights, copies, columns):
    total = None
    for half in range(2):
        for copy in copies[half * 16 : half * 16 + 16]:
            copy.wait()
        rows = slice(half * 2 * BLK, (half + 1) * 2 * BLK)
        part = dot(x[:, rows], weights[rows, columns])
        total = part if total is None else total + part
    return total


def key_value_kernel(own_ref, oth_ref, *rest):
    pieces, (weights, kv_ref, xs, flags), sems = rest[:16], rest[16:20], rest[20]
    copies = fetch(pieces, (0,) * 16, weights, sems)
    flags[0] = own_ref[SEG:, :DH]
    flags[1] = oth_ref[SEG:, :DH]
    xs[0:SEG, :] = own_ref[0:SEG, :]
    xs[SEG:, :] = oth_ref[0:SEG, :]
    total = accumulate(xs, weights, copies, slice(0, 2 * HALF))
    kv_ref[0] = total[:SEG].astype(BF16)
    kv_ref[1] = total[SEG:].astype(BF16)


QO_PLACES = (2,) * 9 + (0,) + (2,) + (0,) + (2,) * 4


def query_kernel(xs, cot_own, cot_oth, biases, kv_ref, pk_ref, *rest):
    pieces = rest[:16]
    weights, cq_ref, cg_ref, rel_ref, own_ref, dp_ref = rest[16:22]
    cots, sems = rest[22:]
    z, _, _ = place()
    copies = fetch(pieces, QO_PLACES, weights, sems)
    for r in range(ZS):
        cots[0:SEG, r * BLK : (r + 1) * BLK] = cot_own[:, plane_columns(z, r)]
        cots[SEG:, r * BLK : (r + 1) * BLK] = cot_oth[:, plane_columns(z, r)]
    q = accumulate(xs, weights, copies, slice(0, HALF))
    cq = (q + biases[0:1, :]).astype(BF16)
    pq = (q + biases[1:2, :]).astype(BF16)
    cg = dot(cots[...], weights[:, HALF:]).astype(BF16)
    row = lax.broadcasted_iota(jnp.int32, (SEG, SEG), 0)
    col = lax.broadcasted_iota(jnp.int32, (SEG, SEG), 1)
    for rec in range(2):
        rows = slice(rec * SEG, (rec + 1) * SEG)
        cq_ref[rec] = cq[rows]
        cg_ref[rec] = cg[rows]
        for h in range(HEADS):
            f, fv = head(h), head(HEADS + h)
            rel = dot(pq[rows, f], pk_ref[:, f], NT)
            rel = pltpu.roll(rel, SEG + 1, 1, stride=1, stride_axis=0)
            rel_ref[rec, h] = rel[:, :SEG]
            s_own = (dot(cq[rows, f], kv_ref[rec, :, f], NT) + rel[:, SEG:]) * SCALE
            own_ref[rec, h] = jnp.where(col <= row, s_own, -jnp.inf)
            dp_ref[rec, h] = dot(cg[rows, f], kv_ref[rec, :, fv], NT)


SCALE = DH**-0.5


def head(i):
    return slice(i * DH, (i + 1) * DH)


def memory_kernel(
    flags, cq_ref, cg_ref, rel_ref, own_ref, dp_ref, mem_ref, p_ref, ds_ref, dmem_ref
):
    for rec in range(2):
        flag = flags[rec, 0:1, :].astype(F32)
        for h in range(HEADS):
            f, fv = head(h), head(HEADS + h)
            cq, g = cq_ref[rec, :, f], cg_ref[rec, :, f]
            s_own = own_ref[rec, h]
            s_mem = (dot(cq, mem_ref[rec, :, f], NT) + rel_ref[rec, h]) * SCALE
            s_mem = jnp.where(flag == 0, s_mem, -jnp.inf)
            dp_mem = dot(g, mem_ref[rec, :, fv], NT)
            peak = jnp.max(jnp.maximum(s_mem, s_own), axis=-1, keepdims=True)
            e_mem = jnp.exp(s_mem - peak)
            e_own = jnp.exp(s_own - peak)
            norm = 1.0 / jnp.sum(e_mem + e_own, axis=-1, keepdims=True)
            a_mem, a_own = e_mem * norm, e_own * norm
            dp_own = dp_ref[rec, h]
            inner = jnp.sum(a_mem * dp_mem + a_own * dp_own, axis=-1, keepdims=True)
            p_mem = a_mem.astype(BF16)
            ds_mem = (a_mem * (dp_mem - inner) * SCALE).astype(BF16)
            p_ref[rec, h, :, :SEG] = p_mem
            p_ref[rec, h, :, SEG:] = a_own.astype(BF16)
            ds_ref[rec, h, :, :SEG] = ds_mem
            ds_ref[rec, h, :, SEG:] = (a_own * (dp_own - inner) * SCALE).astype(BF16)
            dmem_ref[rec, :, f] = dot(ds_mem, cq, TN).astype(BF16)
            dmem_ref[rec, :, fv] = dot(p_mem, g, TN).astype(BF16)


def context_kernel(p_ref, kv_ref, mem_ref, wqo, ctx_ref, lo_oth):
    for rec in range(2):
        for h in range(HEADS):
            f, fv = head(h), head(HEADS + h)
            ctx = dot(p_ref[rec, h, :, :SEG], mem_ref[rec, :, fv])
            ctx += dot(p_ref[rec, h, :, SEG:], kv_ref[rec, :, fv])
            ctx_ref[rec, :, f] = ctx.astype(BF16)
    lo_oth[...] = dot(ctx_ref[1], wqo[:, HALF:], NT).astype(BF16)


def own_grad_kernel(
    x_ref, ctx_ref, p_ref, ds_ref, cq_ref, cg_ref, kv_ref, mem_ref, pk_ref, wkv, wqo,
    lo_own, np_ref, dq, dkv,
):
    z, _, _ = place()
    row = lax.broadcasted_iota(jnp.int32, (SEG, SEG), 0)
    col = lax.broadcasted_iota(jnp.int32, (SEG, SEG), 1)
    flip = jnp.where(row + col == SEG - 1, 1.0, 0.0).astype(BF16)
    for rec in range(2):
        rows = slice(rec * SEG, (rec + 1) * SEG)
        for h in range(HEADS):
            f, fv = head(h), head(HEADS + h)
            ds = ds_ref[rec, h]
            rel = pltpu.roll(dot(flip, ds), 0, 1, stride=1, stride_axis=0).astype(BF16)
            rel = dot(flip, rel).astype(BF16)
            total = dot(ds[:, :SEG], mem_ref[rec, :, f]) + dot(ds[:, SEG:], kv_ref[rec, :, f])
            dq[rows, f] = (total + dot(rel, pk_ref[:, f])).astype(BF16)
            dkv[rows, f] = dot(ds[:, SEG:], cq_ref[rec, :, f], TN).astype(BF16)
            dkv[rows, fv] = dot(p_ref[rec, h, :, SEG:], cg_ref[rec, :, f], TN).astype(BF16)
    np_ref[...] = dot(dq[...], wqo[:, :HALF], NT) + dot(dkv[...], wkv[...], NT)
    lo = dot(ctx_ref[0], wqo[:, HALF:], NT)
    for r in range(ZS):
        there = plane_columns(z, r)
        lo_own[:, there] = x_ref[:, there].astype(F32) + lo[:, r * BLK : (r + 1) * BLK]


def returned_kernel(np_ref, ret_ref, wkv, np_oth):
    np_oth[...] = (np_ref[SEG:, :] + dot(ret_ref[1], wkv[...], NT)).astype(BF16)


def returned_own_kernel(np_ref, ret_ref, wkv, lo_own, lo_ret, np_own, out_ref):
    z, _, _ = place()
    np_own[...] = np_ref[:SEG, :] + dot(ret_ref[0], wkv[...], NT)
    for r in range(ZS):
        there = plane_columns(z, r)
        lo = lo_own[:, there] + lo_ret[:, r * BLK : (r + 1) * BLK].astype(F32)
        out_ref[:, there] = lo.astype(BF16)


def finish_kernel(x_ref, gain_ref, cot_ref, np_own, np_ret, grad_ref, total):
    z, _, _ = place()
    for r in range(ZS):
        cols = slice(r * BLK, (r + 1) * BLK)
        total[:, plane_columns(z, r)] = np_own[:, cols] + np_ret[:, cols].astype(F32)
    x = x_ref[...].astype(F32)
    center = jnp.mean(x, axis=-1, keepdims=True)
    moved = x - center
    spread = jnp.mean(jnp.square(moved), axis=-1, keepdims=True)
    rstd = lax.rsqrt(spread + epsilon)
    hat = moved * rstd
    g = total[...] * gain_ref[...]
    mean_g = jnp.mean(g, axis=-1, keepdims=True)
    mean_gh = jnp.mean(g * hat, axis=-1, keepdims=True)
    grad = (rstd * (g - mean_g - hat * mean_gh)).astype(BF16)
    grad_ref[...] = cot_ref[...] + grad


def call(kernel, outs, scratch=(), in_specs=None, us=1.0):
    return pl.pallas_call(
        kernel,
        out_shape=outs,
        in_specs=in_specs,
        out_specs=jax.tree.map(lambda _: VM, outs),
        scratch_shapes=list(scratch),
        compiler_params=pltpu.CompilerParams(vmem_limit_bytes=VMEM_LIMIT),
        cost_estimate=pl.CostEstimate(
            flops=0, bytes_accessed=int(us * 3.0e6), transcendentals=0
        ),
    )


def shape(*dims, dtype=BF16):
    return jax.ShapeDtypeStruct(dims, dtype)


VM = pl.BlockSpec(memory_space=pltpu.VMEM)
SM = pl.BlockSpec(memory_space=pltpu.SMEM)
ANY = pl.BlockSpec(memory_space=pl.ANY)


def moved_by(f):
    route = []
    for z in range(ZS):
        for y in range(2):
            for c in range(2):
                zz, yy, cc = f(z, y, c)
                route.append((4 * z + 2 * y + c, 4 * zz + 2 * yy + cc))
    return lambda block: lax.ppermute(block, "tm", route)


up = moved_by(lambda z, y, c: ((z + 1) % ZS, y, c))
down = moved_by(lambda z, y, c: ((z - 1) % ZS, y, c))
across = moved_by(lambda z, y, c: (z, 1 - y, c))
sibling = moved_by(lambda z, y, c: (z, y, 1 - c))


def other(block):
    return lax.ppermute(block, "grp", [(0, 1), (1, 0)])


def split_heads(
    inputs,
    norm_gain,
    query_weight,
    key_weight,
    value_weight,
    output_weight,
    content_bias,
    position_bias,
    position_keys,
    start_flags,
    cotangent,
):
    x, cot = inputs[0], cotangent[0]
    gain = norm_gain[None]
    w0 = call(
        pack_kernel, shape(4, ROWS, HALF), [pltpu.SemaphoreType.DMA((4,))], [ANY] * 4, 0.5
    )(key_weight, value_weight, query_weight, output_weight)
    normed, biases, pk = call(
        normalize_kernel,
        (shape(SEG + 16, D), shape(2, HALF, dtype=F32), shape(2 * SEG, HALF)),
        [pltpu.VMEM((SEG, D), BF16)],
        [VM, VM, SM, VM, VM, VM],
        0.5,
    )(x, gain, start_flags, content_bias[None], position_bias[None], position_keys)
    normed_oth = other(normed)
    cot_oth = other(cot)

    w0y = across(w0)
    w1, w3 = up(w0), down(w0)
    w2 = up(w1)
    w1y, w3y = across(w1), across(w3)
    w2y_kv = up(w1y[:2])
    w2y_qo = across(w2[2:])
    here = [w0, w0y, w1, w1y, w2, w2y_kv, w3, w3y]
    there = [sibling(p) for p in here]
    w2y_qo_there = sibling(w2y_qo)
    kv_pieces, qo_pieces = [], []
    for r in range(ZS):
        kv_pieces += here[2 * r : 2 * r + 2] + there[2 * r : 2 * r + 2]
        if r == 2:
            qo_pieces += [w2, w2y_qo, there[4], w2y_qo_there]
        else:
            qo_pieces += here[2 * r : 2 * r + 2] + there[2 * r : 2 * r + 2]

    wkv, kv, xs, flags = call(
        key_value_kernel,
        (
            shape(D, 2 * HALF),
            shape(2, SEG, 2 * HALF),
            shape(2 * SEG, D),
            shape(2, 16, DH),
        ),
        [pltpu.SemaphoreType.DMA((32,))],
        [VM, VM] + [ANY] * 16,
        2.0,
    )(normed, normed_oth, *kv_pieces)
    steps = lax.axis_size("tm")
    mem = lax.ppermute(kv, "tm", [(i, i + 1) for i in range(steps - 1)])

    blocks = shape(2, HEADS, SEG, SEG, dtype=F32)
    wqo, cq, cg, rel, s_own, dp_own = call(
        query_kernel,
        (shape(D, 2 * HALF), shape(2, SEG, HALF), shape(2, SEG, HALF), blocks, blocks, blocks),
        [pltpu.VMEM((2 * SEG, D), BF16), pltpu.SemaphoreType.DMA((32,))],
        [VM] * 6 + [ANY] * 16,
        3.0,
    )(xs, cot, cot_oth, biases, kv, pk, *qo_pieces)

    p, ds, dmem = call(
        memory_kernel,
        (
            shape(2, HEADS, SEG, 2 * SEG),
            shape(2, HEADS, SEG, 2 * SEG),
            shape(2, SEG, 2 * HALF),
        ),
        (),
        [VM] * 7,
        3.0,
    )(flags, cq, cg, rel, s_own, dp_own, mem)
    ret = lax.ppermute(dmem, "tm", [(i + 1, i) for i in range(steps - 1)])

    ctx, lo_oth = call(
        context_kernel, (shape(2, SEG, HALF), shape(SEG, D)), (), [VM] * 4, 1.5
    )(p, kv, mem, wqo)
    lo_ret = other(lo_oth)
    lo_own, partial = call(
        own_grad_kernel,
        (shape(SEG, D, dtype=F32), shape(2 * SEG, D, dtype=F32)),
        [pltpu.VMEM((2 * SEG, HALF), BF16), pltpu.VMEM((2 * SEG, 2 * HALF), BF16)],
        [VM] * 11,
        5.0,
    )(x, ctx, p, ds, cq, cg, kv, mem, pk, wkv, wqo)
    np_oth = call(returned_kernel, shape(SEG, D), (), [VM] * 3, 1.0)(partial, ret, wkv)
    np_ret = other(np_oth)
    np_own, layer_out = call(
        returned_own_kernel, (shape(SEG, D, dtype=F32), shape(SEG, D)), (), [VM] * 5, 1.0
    )(partial, ret, wkv, lo_own, lo_ret)
    input_grad = call(
        finish_kernel, shape(SEG, D), [pltpu.VMEM((SEG, D), F32)], [VM] * 5, 1.0
    )(x, gain, cot, np_own, np_ret)
    return (layer_out[None], input_grad[None])


def from_behind(block, axis, distance):
    devices = range(lax.axis_size(axis))
    route = [(i - distance, i) for i in devices if i - distance in devices]
    return lax.ppermute(block, axis, route)


def normalize_project(
    inputs, norm_gain, query_weight, key_weight, value_weight, content_bias, position_bias
):
    widened = inputs.astype(jnp.float32)
    center = jnp.mean(widened, axis=-1, keepdims=True)
    spread = jnp.mean(jnp.square(widened - center), axis=-1, keepdims=True)
    normed = ((widened - center) * lax.rsqrt(spread + epsilon) * norm_gain).astype(jnp.bfloat16)
    projected = jnp.dot(normed, query_weight, preferred_element_type=jnp.float32)
    content_query = (projected + content_bias).astype(jnp.bfloat16)
    position_query = (projected + position_bias).astype(jnp.bfloat16)
    key_rows = jnp.dot(normed, key_weight, preferred_element_type=jnp.float32).astype(jnp.bfloat16)
    value_rows = jnp.dot(normed, value_weight, preferred_element_type=jnp.float32).astype(
        jnp.bfloat16
    )
    return (content_query, position_query, key_rows, value_rows)


def attend(
    content_query,
    position_query,
    key_rows,
    value_rows,
    memory_keys,
    memory_values,
    position_keys,
    keep_memory,
):
    length = content_query.shape[0]
    all_keys = jnp.concatenate([memory_keys, key_rows], axis=0).reshape(2 * length, H, DH)
    all_values = jnp.concatenate([memory_values, value_rows], axis=0).reshape(2 * length, H, DH)
    content = content_query.reshape(length, H, DH)
    located = position_query.reshape(length, H, DH)
    distance_keys = position_keys[::-1].reshape(2 * length, H, DH)
    direct = jnp.einsum("ihd,jhd->hij", content, all_keys, preferred_element_type=jnp.float32)
    relative = jnp.einsum(
        "ihd,jhd->hij", located, distance_keys, preferred_element_type=jnp.float32
    )
    padded = jnp.pad(relative, ((0, 0), (0, 0), (0, 1)))
    skewed = padded.reshape(H, length * (2 * length + 1))[
        :, length - 1 : length - 1 + 2 * length * length
    ]
    skewed = skewed.reshape(H, length, 2 * length)
    scores = (direct + skewed) * DH ** (-0.5)
    key_index = lax.broadcasted_iota(jnp.int32, (length, 2 * length), 1)
    query_index = lax.broadcasted_iota(jnp.int32, (length, 2 * length), 0)
    allowed = (key_index <= query_index + length) & (keep_memory | (key_index >= length))
    scores = jnp.where(allowed[None], scores, -jnp.inf)
    row_peak = lax.stop_gradient(jnp.max(scores, axis=-1, keepdims=True))
    raised = jnp.exp(scores - row_peak)
    attention = (raised / jnp.sum(raised, axis=-1, keepdims=True)).astype(jnp.bfloat16)
    gathered = jnp.einsum("hij,jhd->ihd", attention, all_values, preferred_element_type=jnp.float32)
    return gathered.reshape(length, H * DH).astype(jnp.bfloat16)


def finish(inputs, context, output_weight):
    update = lax.dot_general(
        context,
        output_weight,
        (((context.ndim - 1,), (1,)), ((), ())),
        preferred_element_type=jnp.float32,
    )
    return (inputs.astype(jnp.float32) + update).astype(jnp.bfloat16)


def shards(
    inputs,
    norm_gain,
    query_weight,
    key_weight,
    value_weight,
    output_weight,
    content_bias,
    position_bias,
    position_keys,
    start_flags,
    cotangent,
):
    partial_weights = (
        lax.all_gather(query_weight, "grp", axis=1, tiled=True),
        lax.all_gather(key_weight, "grp", axis=1, tiled=True),
        lax.all_gather(value_weight, "grp", axis=1, tiled=True),
        lax.all_gather(output_weight, "grp", axis=1, tiled=True),
    )
    full_weights = (
        lax.all_gather(partial_weights[0], "tm", axis=0, tiled=True),
        lax.all_gather(partial_weights[1], "tm", axis=0, tiled=True),
        lax.all_gather(partial_weights[2], "tm", axis=0, tiled=True),
        lax.all_gather(partial_weights[3], "tm", axis=0, tiled=True),
    )
    query_full, key_full, value_full, output_full = full_weights
    own_inputs = inputs[0]
    own_cotangent = cotangent[0]
    keep_memory = start_flags[0, 0] == 0

    def project(local_inputs):
        return normalize_project(
            local_inputs, norm_gain, query_full, key_full, value_full, content_bias, position_bias
        )

    projections, project_back = jax.vjp(project, own_inputs)
    content_query, position_query, key_rows, value_rows = projections
    memory_keys, memory_values = from_behind((key_rows, value_rows), "tm", 1)

    def attend_local(
        local_content, local_position, local_keys, local_values, prior_keys, prior_values
    ):
        return attend(
            local_content,
            local_position,
            local_keys,
            local_values,
            prior_keys,
            prior_values,
            position_keys,
            keep_memory,
        )

    context, attend_back = jax.vjp(
        attend_local,
        content_query,
        position_query,
        key_rows,
        value_rows,
        memory_keys,
        memory_values,
    )

    def combine(local_inputs, local_context):
        return finish(local_inputs, local_context, output_full)

    layer_out, finish_back = jax.vjp(combine, own_inputs, context)
    residual_grad, context_grad = finish_back(own_cotangent)
    attend_grads = attend_back(context_grad)
    returned_keys, returned_values = from_behind((attend_grads[4], attend_grads[5]), "tm", -1)
    key_grad = attend_grads[2] + returned_keys
    value_grad = attend_grads[3] + returned_values
    (norm_grad,) = project_back((attend_grads[0], attend_grads[1], key_grad, value_grad))
    input_grad = residual_grad + norm_grad
    return (layer_out[None], input_grad[None])


def solution(mesh):
    in_specs = (
        P("grp", "tm", None),
        P(),
        P("tm", "grp"),
        P("tm", "grp"),
        P("tm", "grp"),
        P("tm", "grp"),
        P(),
        P(),
        P(),
        P("grp", "tm"),
        P("grp", "tm", None),
    )
    out_specs = (P("grp", "tm", None), P("grp", "tm", None))
    split = dict(mesh.shape) == {"grp": 2, "tm": 4 * ZS}
    body = split_heads if split else shards
    return jax.shard_map(body, mesh=mesh, in_specs=in_specs, out_specs=out_specs, check_vma=False)
```

```python
import functools

import jax
import jax.numpy as jnp
from jax import lax
from jax.experimental import pallas as pl
from jax.experimental.pallas import tpu as pltpu
from jax.sharding import PartitionSpec as P

H = 6
DH = 128
epsilon = 1e-05

F32 = jnp.float32
BF16 = jnp.bfloat16
SEG = 128
D = 1536
HALF = 384
HEADS = HALF // DH
ROWS = 96
ZS = 4
BLK = 4 * ROWS
NT = (((1,), (1,)), ((), ()))
TN = (((0,), (0,)), ((), ()))


def dot(a, b, dims=(((1,), (0,)), ((), ()))):
    return lax.dot_general(a, b, dims, preferred_element_type=F32)


def place():
    t = lax.axis_index("tm")
    return t // 4, (t // 2) % 2, t % 2


def plane_columns(z, r):
    return pl.ds(pl.multiple_of(lax.rem(z - r + ZS, ZS) * BLK, 128), BLK)


def lanes(ref):
    return jnp.concatenate([ref[i : i + 1, :] for i in range(ref.shape[0])], axis=1)


def prepare_kernel(
    k_ref, v_ref, q_ref, o_ref, x_ref, gain_ref, pk_ref, flag_ref,
    shard, out_ref, pk_out, held, x_in, gain_in, pk_in, sems,
):
    z, _, _ = place()
    own = pl.ds(pl.multiple_of(lax.axis_index("grp") * HALF, 128), HALF)
    copies = [
        pltpu.make_async_copy(x_ref.at[0], x_in, sems.at[0]),
        pltpu.make_async_copy(gain_ref, gain_in, sems.at[1]),
        pltpu.make_async_copy(pk_ref.at[:, own], pk_in, sems.at[2]),
    ] + [
        pltpu.make_async_copy(ref, shard.at[i], sems.at[3 + i])
        for i, ref in enumerate((k_ref, v_ref, q_ref, o_ref))
    ]
    for copy in copies:
        copy.start()
    for copy in copies:
        copy.wait()
    x = x_in[...].astype(F32)
    center = jnp.mean(x, axis=-1, keepdims=True)
    moved = x - center
    spread = jnp.mean(jnp.square(moved), axis=-1, keepdims=True)
    held[...] = (moved * lax.rsqrt(spread + epsilon) * lanes(gain_in)).astype(BF16)
    for r in range(ZS):
        out_ref[0:SEG, r * BLK : (r + 1) * BLK] = held[:, plane_columns(z, r)]
    flag = flag_ref[0, 0].astype(F32)
    out_ref[SEG:, :] = jnp.full((16, D), flag, F32).astype(BF16)
    row = lax.broadcasted_iota(jnp.int32, (2 * SEG, 2 * SEG), 0)
    col = lax.broadcasted_iota(jnp.int32, (2 * SEG, 2 * SEG), 1)
    flip = jnp.where(row + col == 2 * SEG - 1, 1.0, 0.0).astype(BF16)
    pk_out[...] = dot(flip, pk_in[...]).astype(BF16)


def stage_kernel(shard_ref, normed_ref, shard, normed):
    shard[...] = shard_ref[...]
    normed[...] = normed_ref[...]


def shard_rows(r, j):
    _, y, c = place()
    yy = 1 - y if j % 2 else y
    cc = 1 - c if j // 2 else c
    return pl.ds(pl.multiple_of(r * BLK + (2 * yy + cc) * ROWS, 16), ROWS)


def fetch(pieces, first, weights, sems):
    copies = []
    for n in range(4 * ZS):
        for w in range(2):
            copies.append(
                pltpu.make_async_copy(
                    pieces[n].at[first[n] + w],
                    weights.at[shard_rows(n // 4, n % 4), pl.ds(w * HALF, HALF)],
                    sems.at[2 * n + w],
                )
            )
    for copy in copies:
        copy.start()
    return copies


def accumulate(x, weights, copies, columns):
    total = None
    for half in range(2):
        for copy in copies[half * 16 : half * 16 + 16]:
            copy.wait()
        rows = slice(half * 2 * BLK, (half + 1) * 2 * BLK)
        part = dot(x[:, rows], weights[rows, columns])
        total = part if total is None else total + part
    return total


def key_value_kernel(own_ref, oth_ref, *rest):
    pieces, (weights, kv_own, kv_oth, xs, flags, sems) = rest[:16], rest[16:]
    copies = fetch(pieces, (0,) * 16, weights, sems)
    flags[0] = own_ref[SEG:, :DH]
    flags[1] = oth_ref[SEG:, :DH]
    xs[0:SEG, :] = own_ref[0:SEG, :]
    xs[SEG:, :] = oth_ref[0:SEG, :]
    total = accumulate(xs, weights, copies, slice(0, 2 * HALF))
    kv_own[...] = total[:SEG].astype(BF16)
    kv_oth[...] = total[SEG:].astype(BF16)


SCALE = DH**-0.5
QO_PLACES = (2,) * 9 + (0,) + (2,) + (0,) + (2,) * 4


def head(i):
    return slice(i * DH, (i + 1) * DH)


def own_half(ref):
    g = lax.axis_index("grp")
    parts = [jnp.where(g == 0, ref[h : h + 1], ref[HEADS + h : HEADS + h + 1]) for h in range(HEADS)]
    return jnp.concatenate(parts, axis=1)


def query_kernel(xs, cot_own, cot_oth, cb_ref, pb_ref, kv_own, kv_oth, pk_ref, *rest):
    pieces = rest[:16]
    weights, cq_ref, cg_ref, rel_ref, own_ref, dp_ref = rest[16:22]
    cots, sems = rest[22:]
    z, _, _ = place()
    copies = fetch(pieces, QO_PLACES, weights, sems)
    for r in range(ZS):
        cots[0:SEG, r * BLK : (r + 1) * BLK] = cot_own[:, plane_columns(z, r)]
        cots[SEG:, r * BLK : (r + 1) * BLK] = cot_oth[:, plane_columns(z, r)]
    q = accumulate(xs, weights, copies, slice(0, HALF))
    cq = (q + own_half(cb_ref)).astype(BF16)
    pq = (q + own_half(pb_ref)).astype(BF16)
    cg = dot(cots[...], weights[:, HALF:]).astype(BF16)
    row = lax.broadcasted_iota(jnp.int32, (SEG, SEG), 0)
    col = lax.broadcasted_iota(jnp.int32, (SEG, SEG), 1)
    for rec in range(2):
        rows = slice(rec * SEG, (rec + 1) * SEG)
        kv_ref = (kv_own, kv_oth)[rec]
        cq_ref[rec] = cq[rows]
        cg_ref[rec] = cg[rows]
        for h in range(HEADS):
            f, fv = head(h), head(HEADS + h)
            rel = dot(pq[rows, f], pk_ref[:, f], NT)
            rel = pltpu.roll(rel, SEG + 1, 1, stride=1, stride_axis=0)
            rel_ref[rec, h] = rel[:, :SEG]
            s_own = (dot(cq[rows, f], kv_ref[:, f], NT) + rel[:, SEG:]) * SCALE
            own_ref[rec, h] = jnp.where(col <= row, s_own, -jnp.inf)
            dp_ref[rec, h] = dot(cg[rows, f], kv_ref[:, fv], NT)


def memory_kernel(
    rec, flags, cq_ref, cg_ref, rel_ref, own_ref, dp_ref, kv_ref, mem_ref,
    p_ref, ds_ref, dmem_ref, ctx_ref,
):
    flag = flags[rec, 0:1, :].astype(F32)
    for h in range(HEADS):
        f, fv = head(h), head(HEADS + h)
        cq, g = cq_ref[rec, :, f], cg_ref[rec, :, f]
        s_own = own_ref[rec, h]
        s_mem = (dot(cq, mem_ref[:, f], NT) + rel_ref[rec, h]) * SCALE
        s_mem = jnp.where(flag == 0, s_mem, -jnp.inf)
        dp_mem = dot(g, mem_ref[:, fv], NT)
        peak = jnp.max(jnp.maximum(s_mem, s_own), axis=-1, keepdims=True)
        e_mem = jnp.exp(s_mem - peak)
        e_own = jnp.exp(s_own - peak)
        norm = 1.0 / jnp.sum(e_mem + e_own, axis=-1, keepdims=True)
        a_mem, a_own = e_mem * norm, e_own * norm
        dp_own = dp_ref[rec, h]
        inner = jnp.sum(a_mem * dp_mem + a_own * dp_own, axis=-1, keepdims=True)
        p_mem, p_own = a_mem.astype(BF16), a_own.astype(BF16)
        ctx = dot(p_mem, mem_ref[:, fv]) + dot(p_own, kv_ref[:, fv])
        ctx_ref[:, f] = ctx.astype(BF16)
        ds_mem = (a_mem * (dp_mem - inner) * SCALE).astype(BF16)
        p_ref[h] = p_own
        ds_ref[h, :, :SEG] = ds_mem
        ds_ref[h, :, SEG:] = (a_own * (dp_own - inner) * SCALE).astype(BF16)
        dmem_ref[:, f] = dot(ds_mem, cq, TN).astype(BF16)
        dmem_ref[:, fv] = dot(p_mem, g, TN).astype(BF16)


def grad_kernel(
    rec, p_ref, ds_ref, cq_ref, cg_ref, kv_ref, mem_ref, pk_ref, wkv, wqo, np_ref, dq, dkv
):
    row = lax.broadcasted_iota(jnp.int32, (SEG, SEG), 0)
    col = lax.broadcasted_iota(jnp.int32, (SEG, SEG), 1)
    flip = jnp.where(row + col == SEG - 1, 1.0, 0.0).astype(BF16)
    for h in range(HEADS):
        f, fv = head(h), head(HEADS + h)
        ds = ds_ref[h]
        rel = pltpu.roll(dot(flip, ds), 0, 1, stride=1, stride_axis=0).astype(BF16)
        rel = dot(flip, rel).astype(BF16)
        total = dot(ds[:, :SEG], mem_ref[:, f]) + dot(ds[:, SEG:], kv_ref[:, f])
        dq[:, f] = (total + dot(rel, pk_ref[:, f])).astype(BF16)
        dkv[:, f] = dot(ds[:, SEG:], cq_ref[rec, :, f], TN).astype(BF16)
        dkv[:, fv] = dot(p_ref[h], cg_ref[rec, :, f], TN).astype(BF16)
    np_ref[...] = dot(dq[...], wqo[:, :HALF], NT) + dot(dkv[...], wkv[...], NT)


def returned_kernel(np_ref, ret_ref, wkv, out_ref):
    out_ref[...] = (np_ref[...] + dot(ret_ref[...], wkv[...], NT)).astype(out_ref.dtype)


def partial_output_kernel(ctx_ref, wqo, out_ref):
    out_ref[...] = dot(ctx_ref[...], wqo[:, HALF:], NT).astype(BF16)


def output_kernel(x_ref, ctx_ref, wqo, lo_ret, out_ref, held):
    z, _, _ = place()
    held[...] = dot(ctx_ref[...], wqo[:, HALF:], NT)
    for r in range(ZS):
        cols, there = slice(r * BLK, (r + 1) * BLK), plane_columns(z, r)
        total = held[:, cols] + lo_ret[:, cols].astype(F32)
        out_ref[0, :, there] = (x_ref[0, :, there].astype(F32) + total).astype(BF16)


def finish_kernel(x_ref, gain_ref, cot_ref, np_own, np_ret, grad_ref, total):
    z, _, _ = place()
    for r in range(ZS):
        cols = slice(r * BLK, (r + 1) * BLK)
        total[:, plane_columns(z, r)] = np_own[:, cols] + np_ret[:, cols].astype(F32)
    x = x_ref[0].astype(F32)
    center = jnp.mean(x, axis=-1, keepdims=True)
    moved = x - center
    spread = jnp.mean(jnp.square(moved), axis=-1, keepdims=True)
    rstd = lax.rsqrt(spread + epsilon)
    hat = moved * rstd
    g = total[...] * lanes(gain_ref)
    mean_g = jnp.mean(g, axis=-1, keepdims=True)
    mean_gh = jnp.mean(g * hat, axis=-1, keepdims=True)
    grad = (rstd * (g - mean_g - hat * mean_gh)).astype(BF16)
    grad_ref[0] = cot_ref[...] + grad


def call(kernel, outs, scratch=(), in_specs=None, mib=24):
    return pl.pallas_call(
        kernel,
        out_shape=outs,
        in_specs=in_specs,
        out_specs=jax.tree.map(lambda _: VM, outs),
        scratch_shapes=list(scratch),
        compiler_params=pltpu.CompilerParams(vmem_limit_bytes=mib * 1024 * 1024),
        cost_estimate=pl.CostEstimate(
            flops=0, bytes_accessed=1024, transcendentals=0
        ),
    )


def shape(*dims, dtype=BF16):
    return jax.ShapeDtypeStruct(dims, dtype)


VM = pl.BlockSpec(memory_space=pltpu.VMEM)
SM = pl.BlockSpec(memory_space=pltpu.SMEM)
ANY = pl.BlockSpec(memory_space=pl.ANY)


def moved_by(f):
    route = []
    for z in range(ZS):
        for y in range(2):
            for c in range(2):
                zz, yy, cc = f(z, y, c)
                route.append((4 * z + 2 * y + c, 4 * zz + 2 * yy + cc))
    return lambda block: lax.ppermute(block, "tm", route)


up = moved_by(lambda z, y, c: ((z + 1) % ZS, y, c))
down = moved_by(lambda z, y, c: ((z - 1) % ZS, y, c))
across = moved_by(lambda z, y, c: (z, 1 - y, c))
sibling = moved_by(lambda z, y, c: (z, y, 1 - c))


def after(block, *earlier):
    return lax.optimization_barrier((block, *earlier))[0]


def other(block):
    return lax.ppermute(block, "grp", [(0, 1), (1, 0)])


def split_heads(
    inputs,
    norm_gain,
    query_weight,
    key_weight,
    value_weight,
    output_weight,
    content_bias,
    position_bias,
    position_keys,
    start_flags,
    cotangent,
):
    cot = cotangent[0]
    gain = norm_gain.reshape(D // 128, 128)
    w0, normed, pk = call(
        prepare_kernel,
        (shape(4, ROWS, HALF), shape(SEG + 16, D), shape(2 * SEG, HALF)),
        [
            pltpu.VMEM((SEG, D), BF16),
            pltpu.VMEM((SEG, D), BF16),
            pltpu.VMEM((D // 128, 128), F32),
            pltpu.VMEM((2 * SEG, HALF), BF16),
            pltpu.SemaphoreType.DMA((7,)),
        ],
        [ANY] * 7 + [SM],
        62,
    )(
        key_weight, value_weight, query_weight, output_weight, inputs, gain, position_keys,
        start_flags,
    )
    normed_oth = other(normed)
    w1 = up(w0)
    w0y = across(w0)
    w3 = down(w0)
    w0_near, normed = call(
        stage_kernel, (shape(4, ROWS, HALF), shape(SEG + 16, D)), (), [VM] * 2
    )(w0, normed)
    w1 = after(w1, w0_near)
    cot_oth = other(after(cot, w1))
    w1y = across(w1)
    w2 = up(w1)
    w3y = across(w3)
    w2y_kv = up(after(w1y, w3)[:2])
    w2y_qo = across(after(w2, w3)[2:])
    here = [w0_near, w0y, w1, w1y, w2, w2y_kv, w3, w3y]
    there = [sibling(p) for p in [w0] + here[1:]]
    w2y_qo_there = sibling(w2y_qo)
    kv_pieces = []
    for r in range(ZS):
        kv_pieces += here[2 * r : 2 * r + 2] + there[2 * r : 2 * r + 2]
    qo_pieces = list(kv_pieces)
    qo_pieces[9], qo_pieces[11] = w2y_qo, w2y_qo_there

    half = shape(SEG, 2 * HALF)
    wkv, kv, kv_oth, xs, flags = call(
        key_value_kernel,
        (
            shape(D, 2 * HALF),
            half,
            half,
            shape(2 * SEG, D),
            shape(2, 16, DH),
        ),
        [pltpu.SemaphoreType.DMA((32,))],
        [VM, VM] + [ANY] * 16,
    )(after(normed, w2y_qo, cot_oth), normed_oth, *kv_pieces)
    steps = lax.axis_size("tm")
    onward = [(i, i + 1) for i in range(steps - 1)]
    back = [(i + 1, i) for i in range(steps - 1)]
    mem_oth = lax.ppermute(kv_oth, "tm", onward)
    mem = lax.ppermute(kv, "tm", onward)
    blocks = shape(2, HEADS, SEG, SEG, dtype=F32)
    wqo, cq, cg, rel, s_own, dp_own = call(
        query_kernel,
        (shape(D, 2 * HALF), shape(2, SEG, HALF), shape(2, SEG, HALF), blocks, blocks, blocks),
        [pltpu.VMEM((2 * SEG, D), BF16), pltpu.SemaphoreType.DMA((32,))],
        [VM] * 8 + [ANY] * 16,
    )(
        xs, cot, cot_oth, content_bias.reshape(H, DH), position_bias.reshape(H, DH),
        kv, kv_oth, pk, *qo_pieces,
    )

    def memory(rec, kv_rows, mem_rows):
        return call(
            functools.partial(memory_kernel, rec),
            (shape(HEADS, SEG, SEG), shape(HEADS, SEG, 2 * SEG), half, shape(SEG, HALF)),
            (),
            [VM] * 8,
        )(flags, cq, cg, rel, s_own, dp_own, kv_rows, mem_rows)

    def grads(rec, p, ds, kv_rows, mem_rows):
        return call(
            functools.partial(grad_kernel, rec),
            shape(SEG, D, dtype=F32),
            [pltpu.VMEM((SEG, HALF), BF16), pltpu.VMEM((SEG, 2 * HALF), BF16)],
            [VM] * 9,
        )(p, ds, cq, cg, kv_rows, mem_rows, pk, wkv, wqo)

    p_oth, ds_oth, dmem_oth, ctx_oth = memory(1, kv_oth, mem_oth)
    ret_oth = lax.ppermute(dmem_oth, "tm", back)
    lo_oth = call(partial_output_kernel, shape(SEG, D), (), [VM] * 2)(ctx_oth, wqo)
    lo_ret = other(lo_oth)
    p, ds, dmem, ctx = memory(0, kv, after(mem, lo_oth))
    ret = lax.ppermute(dmem, "tm", back)
    partial_oth = grads(1, after(p_oth, dmem), ds_oth, kv_oth, mem_oth)
    np_oth = call(returned_kernel, shape(SEG, D), (), [VM] * 3)(partial_oth, ret_oth, wkv)
    np_ret = other(np_oth)
    partial = grads(0, after(p, np_oth), ds, kv, mem)
    np_own = call(returned_kernel, shape(SEG, D, dtype=F32), (), [VM] * 3)(partial, ret, wkv)
    layer_out = call(
        output_kernel, shape(1, SEG, D), [pltpu.VMEM((SEG, D), F32)], [VM] * 4
    )(inputs, after(ctx, np_own), wqo, lo_ret)
    input_grad = call(
        finish_kernel, shape(1, SEG, D), [pltpu.VMEM((SEG, D), F32)], [VM] * 5
    )(inputs, gain, cot, after(np_own, layer_out), np_ret)
    return (layer_out, input_grad)


def from_behind(block, axis, distance):
    devices = range(lax.axis_size(axis))
    route = [(i - distance, i) for i in devices if i - distance in devices]
    return lax.ppermute(block, axis, route)


def normalize_project(
    inputs, norm_gain, query_weight, key_weight, value_weight, content_bias, position_bias
):
    widened = inputs.astype(jnp.float32)
    center = jnp.mean(widened, axis=-1, keepdims=True)
    spread = jnp.mean(jnp.square(widened - center), axis=-1, keepdims=True)
    normed = ((widened - center) * lax.rsqrt(spread + epsilon) * norm_gain).astype(jnp.bfloat16)
    projected = jnp.dot(normed, query_weight, preferred_element_type=jnp.float32)
    content_query = (projected + content_bias).astype(jnp.bfloat16)
    position_query = (projected + position_bias).astype(jnp.bfloat16)
    key_rows = jnp.dot(normed, key_weight, preferred_element_type=jnp.float32).astype(jnp.bfloat16)
    value_rows = jnp.dot(normed, value_weight, preferred_element_type=jnp.float32).astype(
        jnp.bfloat16
    )
    return (content_query, position_query, key_rows, value_rows)


def attend(
    content_query,
    position_query,
    key_rows,
    value_rows,
    memory_keys,
    memory_values,
    position_keys,
    keep_memory,
):
    length = content_query.shape[0]
    all_keys = jnp.concatenate([memory_keys, key_rows], axis=0).reshape(2 * length, H, DH)
    all_values = jnp.concatenate([memory_values, value_rows], axis=0).reshape(2 * length, H, DH)
    content = content_query.reshape(length, H, DH)
    located = position_query.reshape(length, H, DH)
    distance_keys = position_keys[::-1].reshape(2 * length, H, DH)
    direct = jnp.einsum("ihd,jhd->hij", content, all_keys, preferred_element_type=jnp.float32)
    relative = jnp.einsum(
        "ihd,jhd->hij", located, distance_keys, preferred_element_type=jnp.float32
    )
    padded = jnp.pad(relative, ((0, 0), (0, 0), (0, 1)))
    skewed = padded.reshape(H, length * (2 * length + 1))[
        :, length - 1 : length - 1 + 2 * length * length
    ]
    skewed = skewed.reshape(H, length, 2 * length)
    scores = (direct + skewed) * DH ** (-0.5)
    key_index = lax.broadcasted_iota(jnp.int32, (length, 2 * length), 1)
    query_index = lax.broadcasted_iota(jnp.int32, (length, 2 * length), 0)
    allowed = (key_index <= query_index + length) & (keep_memory | (key_index >= length))
    scores = jnp.where(allowed[None], scores, -jnp.inf)
    row_peak = lax.stop_gradient(jnp.max(scores, axis=-1, keepdims=True))
    raised = jnp.exp(scores - row_peak)
    attention = (raised / jnp.sum(raised, axis=-1, keepdims=True)).astype(jnp.bfloat16)
    gathered = jnp.einsum("hij,jhd->ihd", attention, all_values, preferred_element_type=jnp.float32)
    return gathered.reshape(length, H * DH).astype(jnp.bfloat16)


def finish(inputs, context, output_weight):
    update = lax.dot_general(
        context,
        output_weight,
        (((context.ndim - 1,), (1,)), ((), ())),
        preferred_element_type=jnp.float32,
    )
    return (inputs.astype(jnp.float32) + update).astype(jnp.bfloat16)


def shards(
    inputs,
    norm_gain,
    query_weight,
    key_weight,
    value_weight,
    output_weight,
    content_bias,
    position_bias,
    position_keys,
    start_flags,
    cotangent,
):
    partial_weights = (
        lax.all_gather(query_weight, "grp", axis=1, tiled=True),
        lax.all_gather(key_weight, "grp", axis=1, tiled=True),
        lax.all_gather(value_weight, "grp", axis=1, tiled=True),
        lax.all_gather(output_weight, "grp", axis=1, tiled=True),
    )
    full_weights = (
        lax.all_gather(partial_weights[0], "tm", axis=0, tiled=True),
        lax.all_gather(partial_weights[1], "tm", axis=0, tiled=True),
        lax.all_gather(partial_weights[2], "tm", axis=0, tiled=True),
        lax.all_gather(partial_weights[3], "tm", axis=0, tiled=True),
    )
    query_full, key_full, value_full, output_full = full_weights
    own_inputs = inputs[0]
    own_cotangent = cotangent[0]
    keep_memory = start_flags[0, 0] == 0

    def project(local_inputs):
        return normalize_project(
            local_inputs, norm_gain, query_full, key_full, value_full, content_bias, position_bias
        )

    projections, project_back = jax.vjp(project, own_inputs)
    content_query, position_query, key_rows, value_rows = projections
    memory_keys, memory_values = from_behind((key_rows, value_rows), "tm", 1)

    def attend_local(
        local_content, local_position, local_keys, local_values, prior_keys, prior_values
    ):
        return attend(
            local_content,
            local_position,
            local_keys,
            local_values,
            prior_keys,
            prior_values,
            position_keys,
            keep_memory,
        )

    context, attend_back = jax.vjp(
        attend_local,
        content_query,
        position_query,
        key_rows,
        value_rows,
        memory_keys,
        memory_values,
    )

    def combine(local_inputs, local_context):
        return finish(local_inputs, local_context, output_full)

    layer_out, finish_back = jax.vjp(combine, own_inputs, context)
    residual_grad, context_grad = finish_back(own_cotangent)
    attend_grads = attend_back(context_grad)
    returned_keys, returned_values = from_behind((attend_grads[4], attend_grads[5]), "tm", -1)
    key_grad = attend_grads[2] + returned_keys
    value_grad = attend_grads[3] + returned_values
    (norm_grad,) = project_back((attend_grads[0], attend_grads[1], key_grad, value_grad))
    input_grad = residual_grad + norm_grad
    return (layer_out[None], input_grad[None])


def solution(mesh):
    in_specs = (
        P("grp", "tm", None),
        P(),
        P("tm", "grp"),
        P("tm", "grp"),
        P("tm", "grp"),
        P("tm", "grp"),
        P(),
        P(),
        P(),
        P("grp", "tm"),
        P("grp", "tm", None),
    )
    out_specs = (P("grp", "tm", None), P("grp", "tm", None))
    split = dict(mesh.shape) == {"grp": 2, "tm": 4 * ZS}
    body = split_heads if split else shards
    return jax.shard_map(body, mesh=mesh, in_specs=in_specs, out_specs=out_specs, check_vma=False)
```

```python
import functools

import jax
import jax.numpy as jnp
from jax import lax
from jax.experimental import pallas as pl
from jax.experimental.pallas import tpu as pltpu
from jax.sharding import PartitionSpec as P

H = 6
DH = 128
epsilon = 1e-05

F32 = jnp.float32
BF16 = jnp.bfloat16
SEG = 128
D = 1536
HALF = 384
HEADS = HALF // DH
ROWS = 96
ZS = 4
BLK = 4 * ROWS
NT = (((1,), (1,)), ((), ()))
TN = (((0,), (0,)), ((), ()))


def dot(a, b, dims=(((1,), (0,)), ((), ()))):
    return lax.dot_general(a, b, dims, preferred_element_type=F32)


def place():
    t = lax.axis_index("tm")
    return t // 4, (t // 2) % 2, t % 2


def plane_columns(z, r):
    return pl.ds(pl.multiple_of(lax.rem(z - r + ZS, ZS) * BLK, 128), BLK)


def lanes(ref):
    return jnp.concatenate([ref[i : i + 1, :] for i in range(ref.shape[0])], axis=1)


def prepare_kernel(
    k_ref, v_ref, q_ref, o_ref, x_ref, gain_ref, pk_ref, flag_ref,
    shard, out_ref, pk_out, held, x_in, gain_in, pk_in, sems,
):
    z, _, _ = place()
    own = pl.ds(pl.multiple_of(lax.axis_index("grp") * HALF, 128), HALF)
    copies = [
        pltpu.make_async_copy(x_ref.at[0], x_in, sems.at[0]),
        pltpu.make_async_copy(gain_ref, gain_in, sems.at[1]),
        pltpu.make_async_copy(pk_ref.at[:, own], pk_in, sems.at[2]),
    ] + [
        pltpu.make_async_copy(ref, shard.at[i], sems.at[3 + i])
        for i, ref in enumerate((k_ref, v_ref, q_ref, o_ref))
    ]
    for copy in copies:
        copy.start()
    for copy in copies:
        copy.wait()
    x = x_in[...].astype(F32)
    center = jnp.mean(x, axis=-1, keepdims=True)
    moved = x - center
    spread = jnp.mean(jnp.square(moved), axis=-1, keepdims=True)
    held[...] = (moved * lax.rsqrt(spread + epsilon) * lanes(gain_in)).astype(BF16)
    for r in range(ZS):
        out_ref[0:SEG, r * BLK : (r + 1) * BLK] = held[:, plane_columns(z, r)]
    flag = flag_ref[0, 0].astype(F32)
    out_ref[SEG:, :] = jnp.full((16, D), flag, F32).astype(BF16)
    row = lax.broadcasted_iota(jnp.int32, (2 * SEG, 2 * SEG), 0)
    col = lax.broadcasted_iota(jnp.int32, (2 * SEG, 2 * SEG), 1)
    flip = jnp.where(row + col == 2 * SEG - 1, 1.0, 0.0).astype(BF16)
    pk_out[...] = dot(flip, pk_in[...]).astype(BF16)


def stage_kernel(shard_ref, normed_ref, shard, normed):
    shard[...] = shard_ref[...]
    normed[...] = normed_ref[...]


def shard_rows(r, j):
    _, y, c = place()
    yy = 1 - y if j % 2 else y
    cc = 1 - c if j // 2 else c
    return pl.ds(pl.multiple_of(r * BLK + (2 * yy + cc) * ROWS, 16), ROWS)


def fetch(pieces, first, weights, sems):
    copies = []
    for n in range(4 * ZS):
        for w in range(2):
            copies.append(
                pltpu.make_async_copy(
                    pieces[n].at[first[n] + w],
                    weights.at[shard_rows(n // 4, n % 4), pl.ds(w * HALF, HALF)],
                    sems.at[2 * n + w],
                )
            )
    for copy in copies:
        copy.start()
    return copies


def accumulate(x, weights, copies, columns):
    total = None
    for half in range(2):
        for copy in copies[half * 16 : half * 16 + 16]:
            copy.wait()
        rows = slice(half * 2 * BLK, (half + 1) * 2 * BLK)
        part = dot(x[:, rows], weights[rows, columns])
        total = part if total is None else total + part
    return total


def key_value_kernel(own_ref, oth_ref, *rest):
    pieces, (weights, kv_ref, xs, flags, sems) = rest[:16], rest[16:]
    copies = fetch(pieces, (0,) * 16, weights, sems)
    flags[0] = own_ref[SEG:, :DH]
    flags[1] = oth_ref[SEG:, :DH]
    xs[0:SEG, :] = own_ref[0:SEG, :]
    xs[SEG:, :] = oth_ref[0:SEG, :]
    total = accumulate(xs, weights, copies, slice(0, 2 * HALF))
    kv_ref[0] = total[:SEG].astype(BF16)
    kv_ref[1] = total[SEG:].astype(BF16)


SCALE = DH**-0.5
QO_PLACES = (2,) * 9 + (0,) + (2,) + (0,) + (2,) * 4


def head(i):
    return slice(i * DH, (i + 1) * DH)


def own_half(ref):
    g = lax.axis_index("grp")
    parts = [jnp.where(g == 0, ref[h : h + 1], ref[HEADS + h : HEADS + h + 1]) for h in range(HEADS)]
    return jnp.concatenate(parts, axis=1)


def query_kernel(xs, cot_own, cot_oth, cb_ref, pb_ref, kv_ref, pk_ref, *rest):
    pieces = rest[:16]
    weights, cq_ref, cg_ref, rel_ref, own_ref, dp_ref = rest[16:22]
    cots, sems = rest[22:]
    z, _, _ = place()
    copies = fetch(pieces, QO_PLACES, weights, sems)
    for r in range(ZS):
        cots[0:SEG, r * BLK : (r + 1) * BLK] = cot_own[:, plane_columns(z, r)]
        cots[SEG:, r * BLK : (r + 1) * BLK] = cot_oth[:, plane_columns(z, r)]
    q = accumulate(xs, weights, copies, slice(0, HALF))
    cq = (q + own_half(cb_ref)).astype(BF16)
    pq = (q + own_half(pb_ref)).astype(BF16)
    cg = dot(cots[...], weights[:, HALF:]).astype(BF16)
    row = lax.broadcasted_iota(jnp.int32, (SEG, SEG), 0)
    col = lax.broadcasted_iota(jnp.int32, (SEG, SEG), 1)
    for rec in range(2):
        rows = slice(rec * SEG, (rec + 1) * SEG)
        cq_ref[rec] = cq[rows]
        cg_ref[rec] = cg[rows]
        for h in range(HEADS):
            f, fv = head(h), head(HEADS + h)
            rel = dot(pq[rows, f], pk_ref[:, f], NT)
            rel = pltpu.roll(rel, SEG + 1, 1, stride=1, stride_axis=0)
            rel_ref[rec, h] = rel[:, :SEG]
            s_own = (dot(cq[rows, f], kv_ref[rec, :, f], NT) + rel[:, SEG:]) * SCALE
            own_ref[rec, h] = jnp.where(col <= row, s_own, -jnp.inf)
            dp_ref[rec, h] = dot(cg[rows, f], kv_ref[rec, :, fv], NT)


def memory_kernel(
    rec, flags, cq_ref, cg_ref, rel_ref, own_ref, dp_ref, kv_ref, mem_ref,
    p_ref, ds_ref, dmem_ref, ctx_ref,
):
    flag = flags[rec, 0:1, :].astype(F32)
    for h in range(HEADS):
        f, fv = head(h), head(HEADS + h)
        cq, g = cq_ref[rec, :, f], cg_ref[rec, :, f]
        s_own = own_ref[rec, h]
        s_mem = (dot(cq, mem_ref[rec, :, f], NT) + rel_ref[rec, h]) * SCALE
        s_mem = jnp.where(flag == 0, s_mem, -jnp.inf)
        dp_mem = dot(g, mem_ref[rec, :, fv], NT)
        peak = jnp.max(jnp.maximum(s_mem, s_own), axis=-1, keepdims=True)
        e_mem = jnp.exp(s_mem - peak)
        e_own = jnp.exp(s_own - peak)
        norm = 1.0 / jnp.sum(e_mem + e_own, axis=-1, keepdims=True)
        a_mem, a_own = e_mem * norm, e_own * norm
        dp_own = dp_ref[rec, h]
        inner = jnp.sum(a_mem * dp_mem + a_own * dp_own, axis=-1, keepdims=True)
        p_mem, p_own = a_mem.astype(BF16), a_own.astype(BF16)
        ctx = dot(p_mem, mem_ref[rec, :, fv]) + dot(p_own, kv_ref[rec, :, fv])
        ctx_ref[:, f] = ctx.astype(BF16)
        ds_mem = (a_mem * (dp_mem - inner) * SCALE).astype(BF16)
        p_ref[h] = p_own
        ds_ref[h, :, :SEG] = ds_mem
        ds_ref[h, :, SEG:] = (a_own * (dp_own - inner) * SCALE).astype(BF16)
        dmem_ref[:, f] = dot(ds_mem, cq, TN).astype(BF16)
        dmem_ref[:, fv] = dot(p_mem, g, TN).astype(BF16)


def grad_kernel(
    rec, p_ref, ds_ref, cq_ref, cg_ref, kv_ref, mem_ref, pk_ref, wkv, wqo, np_ref, dq, dkv
):
    row = lax.broadcasted_iota(jnp.int32, (SEG, SEG), 0)
    col = lax.broadcasted_iota(jnp.int32, (SEG, SEG), 1)
    flip = jnp.where(row + col == SEG - 1, 1.0, 0.0).astype(BF16)
    for h in range(HEADS):
        f, fv = head(h), head(HEADS + h)
        ds = ds_ref[h]
        rel = pltpu.roll(dot(flip, ds), 0, 1, stride=1, stride_axis=0).astype(BF16)
        rel = dot(flip, rel).astype(BF16)
        total = dot(ds[:, :SEG], mem_ref[rec, :, f]) + dot(ds[:, SEG:], kv_ref[rec, :, f])
        dq[:, f] = (total + dot(rel, pk_ref[:, f])).astype(BF16)
        dkv[:, f] = dot(ds[:, SEG:], cq_ref[rec, :, f], TN).astype(BF16)
        dkv[:, fv] = dot(p_ref[h], cg_ref[rec, :, f], TN).astype(BF16)
    np_ref[...] = dot(dq[...], wqo[:, :HALF], NT) + dot(dkv[...], wkv[...], NT)


def returned_kernel(np_ref, ret_ref, wkv, out_ref):
    out_ref[...] = (np_ref[...] + dot(ret_ref[...], wkv[...], NT)).astype(out_ref.dtype)


def partial_output_kernel(ctx_ref, wqo, out_ref):
    out_ref[...] = dot(ctx_ref[...], wqo[:, HALF:], NT).astype(BF16)


def output_kernel(x_ref, ctx_ref, wqo, lo_ret, out_ref, held):
    z, _, _ = place()
    held[...] = dot(ctx_ref[...], wqo[:, HALF:], NT)
    for r in range(ZS):
        cols, there = slice(r * BLK, (r + 1) * BLK), plane_columns(z, r)
        total = held[:, cols] + lo_ret[:, cols].astype(F32)
        out_ref[0, :, there] = (x_ref[0, :, there].astype(F32) + total).astype(BF16)


def finish_kernel(x_ref, gain_ref, cot_ref, np_own, np_ret, grad_ref, total):
    z, _, _ = place()
    for r in range(ZS):
        cols = slice(r * BLK, (r + 1) * BLK)
        total[:, plane_columns(z, r)] = np_own[:, cols] + np_ret[:, cols].astype(F32)
    x = x_ref[0].astype(F32)
    center = jnp.mean(x, axis=-1, keepdims=True)
    moved = x - center
    spread = jnp.mean(jnp.square(moved), axis=-1, keepdims=True)
    rstd = lax.rsqrt(spread + epsilon)
    hat = moved * rstd
    g = total[...] * lanes(gain_ref)
    mean_g = jnp.mean(g, axis=-1, keepdims=True)
    mean_gh = jnp.mean(g * hat, axis=-1, keepdims=True)
    grad = (rstd * (g - mean_g - hat * mean_gh)).astype(BF16)
    grad_ref[0] = cot_ref[...] + grad


def call(kernel, outs, scratch=(), in_specs=None, mib=24):
    return pl.pallas_call(
        kernel,
        out_shape=outs,
        in_specs=in_specs,
        out_specs=jax.tree.map(lambda _: VM, outs),
        scratch_shapes=list(scratch),
        compiler_params=pltpu.CompilerParams(vmem_limit_bytes=mib * 1024 * 1024),
        cost_estimate=pl.CostEstimate(
            flops=0, bytes_accessed=1024, transcendentals=0
        ),
    )


def shape(*dims, dtype=BF16):
    return jax.ShapeDtypeStruct(dims, dtype)


VM = pl.BlockSpec(memory_space=pltpu.VMEM)
SM = pl.BlockSpec(memory_space=pltpu.SMEM)
ANY = pl.BlockSpec(memory_space=pl.ANY)


def moved_by(f):
    route = []
    for z in range(ZS):
        for y in range(2):
            for c in range(2):
                zz, yy, cc = f(z, y, c)
                route.append((4 * z + 2 * y + c, 4 * zz + 2 * yy + cc))
    return lambda block: lax.ppermute(block, "tm", route)


up = moved_by(lambda z, y, c: ((z + 1) % ZS, y, c))
down = moved_by(lambda z, y, c: ((z - 1) % ZS, y, c))
across = moved_by(lambda z, y, c: (z, 1 - y, c))
sibling = moved_by(lambda z, y, c: (z, y, 1 - c))


def after(block, *earlier):
    return lax.optimization_barrier((block, *earlier))[0]


def other(block):
    return lax.ppermute(block, "grp", [(0, 1), (1, 0)])


def split_heads(
    inputs,
    norm_gain,
    query_weight,
    key_weight,
    value_weight,
    output_weight,
    content_bias,
    position_bias,
    position_keys,
    start_flags,
    cotangent,
):
    cot = cotangent[0]
    gain = norm_gain.reshape(D // 128, 128)
    w0, normed, pk = call(
        prepare_kernel,
        (shape(4, ROWS, HALF), shape(SEG + 16, D), shape(2 * SEG, HALF)),
        [
            pltpu.VMEM((SEG, D), BF16),
            pltpu.VMEM((SEG, D), BF16),
            pltpu.VMEM((D // 128, 128), F32),
            pltpu.VMEM((2 * SEG, HALF), BF16),
            pltpu.SemaphoreType.DMA((7,)),
        ],
        [ANY] * 7 + [SM],
        62,
    )(
        key_weight, value_weight, query_weight, output_weight, inputs, gain, position_keys,
        start_flags,
    )
    normed_oth = other(normed)
    w1 = up(w0)
    w0y = across(w0)
    w3 = down(w0)
    w0_near, normed = call(
        stage_kernel, (shape(4, ROWS, HALF), shape(SEG + 16, D)), (), [VM] * 2
    )(w0, normed)
    w1 = after(w1, w0_near)
    cot_oth = other(after(cot, w1))
    w1y = across(w1)
    w2 = up(w1)
    w3y = across(w3)
    w2y_kv = up(after(w1y, w3)[:2])
    w2y_qo = across(after(w2, w3)[2:])
    here = [w0_near, w0y, w1, w1y, w2, w2y_kv, w3, w3y]
    there = [sibling(p) for p in [w0] + here[1:]]
    w2y_qo_there = sibling(w2y_qo)
    kv_pieces = []
    for r in range(ZS):
        kv_pieces += here[2 * r : 2 * r + 2] + there[2 * r : 2 * r + 2]
    qo_pieces = list(kv_pieces)
    qo_pieces[9], qo_pieces[11] = w2y_qo, w2y_qo_there

    half = shape(SEG, 2 * HALF)
    wkv, kv, xs, flags = call(
        key_value_kernel,
        (
            shape(D, 2 * HALF),
            shape(2, SEG, 2 * HALF),
            shape(2 * SEG, D),
            shape(2, 16, DH),
        ),
        [pltpu.SemaphoreType.DMA((32,))],
        [VM, VM] + [ANY] * 16,
    )(after(normed, w2y_qo, cot_oth), normed_oth, *kv_pieces)
    steps = lax.axis_size("tm")
    onward = [(i, i + 1) for i in range(steps - 1)]
    back = [(i + 1, i) for i in range(steps - 1)]
    mem = lax.ppermute(kv, "tm", onward)
    blocks = shape(2, HEADS, SEG, SEG, dtype=F32)
    wqo, cq, cg, rel, s_own, dp_own = call(
        query_kernel,
        (shape(D, 2 * HALF), shape(2, SEG, HALF), shape(2, SEG, HALF), blocks, blocks, blocks),
        [pltpu.VMEM((2 * SEG, D), BF16), pltpu.SemaphoreType.DMA((32,))],
        [VM] * 7 + [ANY] * 16,
    )(
        xs, cot, cot_oth, content_bias.reshape(H, DH), position_bias.reshape(H, DH),
        kv, pk, *qo_pieces,
    )

    def memory(rec, kv_rows, mem_rows):
        return call(
            functools.partial(memory_kernel, rec),
            (shape(HEADS, SEG, SEG), shape(HEADS, SEG, 2 * SEG), half, shape(SEG, HALF)),
            (),
            [VM] * 8,
        )(flags, cq, cg, rel, s_own, dp_own, kv_rows, mem_rows)

    def grads(rec, p, ds, kv_rows, mem_rows):
        return call(
            functools.partial(grad_kernel, rec),
            shape(SEG, D, dtype=F32),
            [pltpu.VMEM((SEG, HALF), BF16), pltpu.VMEM((SEG, 2 * HALF), BF16)],
            [VM] * 9,
        )(p, ds, cq, cg, kv_rows, mem_rows, pk, wkv, wqo)

    p_oth, ds_oth, dmem_oth, ctx_oth = memory(1, kv, mem)
    lo_oth = call(partial_output_kernel, shape(SEG, D), (), [VM] * 2)(ctx_oth, wqo)
    lo_ret = other(lo_oth)
    ret_oth = lax.ppermute(dmem_oth, "tm", back)
    p, ds, dmem, ctx = memory(0, kv, after(mem, lo_oth))
    ret = lax.ppermute(after(dmem, lo_ret), "tm", back)
    partial_oth = grads(1, after(p_oth, dmem), ds_oth, kv, mem)
    np_oth = call(returned_kernel, shape(SEG, D), (), [VM] * 3)(partial_oth, ret_oth, wkv)
    np_ret = other(np_oth)
    partial = grads(0, after(p, np_oth), ds, kv, mem)
    np_own = call(returned_kernel, shape(SEG, D, dtype=F32), (), [VM] * 3)(partial, ret, wkv)
    layer_out = call(
        output_kernel, shape(1, SEG, D), [pltpu.VMEM((SEG, D), F32)], [VM] * 4
    )(inputs, after(ctx, np_own), wqo, lo_ret)
    input_grad = call(
        finish_kernel, shape(1, SEG, D), [pltpu.VMEM((SEG, D), F32)], [VM] * 5
    )(inputs, gain, cot, after(np_own, layer_out), np_ret)
    return (layer_out, input_grad)


def from_behind(block, axis, distance):
    devices = range(lax.axis_size(axis))
    route = [(i - distance, i) for i in devices if i - distance in devices]
    return lax.ppermute(block, axis, route)


def normalize_project(
    inputs, norm_gain, query_weight, key_weight, value_weight, content_bias, position_bias
):
    widened = inputs.astype(jnp.float32)
    center = jnp.mean(widened, axis=-1, keepdims=True)
    spread = jnp.mean(jnp.square(widened - center), axis=-1, keepdims=True)
    normed = ((widened - center) * lax.rsqrt(spread + epsilon) * norm_gain).astype(jnp.bfloat16)
    projected = jnp.dot(normed, query_weight, preferred_element_type=jnp.float32)
    content_query = (projected + content_bias).astype(jnp.bfloat16)
    position_query = (projected + position_bias).astype(jnp.bfloat16)
    key_rows = jnp.dot(normed, key_weight, preferred_element_type=jnp.float32).astype(jnp.bfloat16)
    value_rows = jnp.dot(normed, value_weight, preferred_element_type=jnp.float32).astype(
        jnp.bfloat16
    )
    return (content_query, position_query, key_rows, value_rows)


def attend(
    content_query,
    position_query,
    key_rows,
    value_rows,
    memory_keys,
    memory_values,
    position_keys,
    keep_memory,
):
    length = content_query.shape[0]
    all_keys = jnp.concatenate([memory_keys, key_rows], axis=0).reshape(2 * length, H, DH)
    all_values = jnp.concatenate([memory_values, value_rows], axis=0).reshape(2 * length, H, DH)
    content = content_query.reshape(length, H, DH)
    located = position_query.reshape(length, H, DH)
    distance_keys = position_keys[::-1].reshape(2 * length, H, DH)
    direct = jnp.einsum("ihd,jhd->hij", content, all_keys, preferred_element_type=jnp.float32)
    relative = jnp.einsum(
        "ihd,jhd->hij", located, distance_keys, preferred_element_type=jnp.float32
    )
    padded = jnp.pad(relative, ((0, 0), (0, 0), (0, 1)))
    skewed = padded.reshape(H, length * (2 * length + 1))[
        :, length - 1 : length - 1 + 2 * length * length
    ]
    skewed = skewed.reshape(H, length, 2 * length)
    scores = (direct + skewed) * DH ** (-0.5)
    key_index = lax.broadcasted_iota(jnp.int32, (length, 2 * length), 1)
    query_index = lax.broadcasted_iota(jnp.int32, (length, 2 * length), 0)
    allowed = (key_index <= query_index + length) & (keep_memory | (key_index >= length))
    scores = jnp.where(allowed[None], scores, -jnp.inf)
    row_peak = lax.stop_gradient(jnp.max(scores, axis=-1, keepdims=True))
    raised = jnp.exp(scores - row_peak)
    attention = (raised / jnp.sum(raised, axis=-1, keepdims=True)).astype(jnp.bfloat16)
    gathered = jnp.einsum("hij,jhd->ihd", attention, all_values, preferred_element_type=jnp.float32)
    return gathered.reshape(length, H * DH).astype(jnp.bfloat16)


def finish(inputs, context, output_weight):
    update = lax.dot_general(
        context,
        output_weight,
        (((context.ndim - 1,), (1,)), ((), ())),
        preferred_element_type=jnp.float32,
    )
    return (inputs.astype(jnp.float32) + update).astype(jnp.bfloat16)


def shards(
    inputs,
    norm_gain,
    query_weight,
    key_weight,
    value_weight,
    output_weight,
    content_bias,
    position_bias,
    position_keys,
    start_flags,
    cotangent,
):
    partial_weights = (
        lax.all_gather(query_weight, "grp", axis=1, tiled=True),
        lax.all_gather(key_weight, "grp", axis=1, tiled=True),
        lax.all_gather(value_weight, "grp", axis=1, tiled=True),
        lax.all_gather(output_weight, "grp", axis=1, tiled=True),
    )
    full_weights = (
        lax.all_gather(partial_weights[0], "tm", axis=0, tiled=True),
        lax.all_gather(partial_weights[1], "tm", axis=0, tiled=True),
        lax.all_gather(partial_weights[2], "tm", axis=0, tiled=True),
        lax.all_gather(partial_weights[3], "tm", axis=0, tiled=True),
    )
    query_full, key_full, value_full, output_full = full_weights
    own_inputs = inputs[0]
    own_cotangent = cotangent[0]
    keep_memory = start_flags[0, 0] == 0

    def project(local_inputs):
        return normalize_project(
            local_inputs, norm_gain, query_full, key_full, value_full, content_bias, position_bias
        )

    projections, project_back = jax.vjp(project, own_inputs)
    content_query, position_query, key_rows, value_rows = projections
    memory_keys, memory_values = from_behind((key_rows, value_rows), "tm", 1)

    def attend_local(
        local_content, local_position, local_keys, local_values, prior_keys, prior_values
    ):
        return attend(
            local_content,
            local_position,
            local_keys,
            local_values,
            prior_keys,
            prior_values,
            position_keys,
            keep_memory,
        )

    context, attend_back = jax.vjp(
        attend_local,
        content_query,
        position_query,
        key_rows,
        value_rows,
        memory_keys,
        memory_values,
    )

    def combine(local_inputs, local_context):
        return finish(local_inputs, local_context, output_full)

    layer_out, finish_back = jax.vjp(combine, own_inputs, context)
    residual_grad, context_grad = finish_back(own_cotangent)
    attend_grads = attend_back(context_grad)
    returned_keys, returned_values = from_behind((attend_grads[4], attend_grads[5]), "tm", -1)
    key_grad = attend_grads[2] + returned_keys
    value_grad = attend_grads[3] + returned_values
    (norm_grad,) = project_back((attend_grads[0], attend_grads[1], key_grad, value_grad))
    input_grad = residual_grad + norm_grad
    return (layer_out[None], input_grad[None])


def solution(mesh):
    in_specs = (
        P("grp", "tm", None),
        P(),
        P("tm", "grp"),
        P("tm", "grp"),
        P("tm", "grp"),
        P("tm", "grp"),
        P(),
        P(),
        P(),
        P("grp", "tm"),
        P("grp", "tm", None),
    )
    out_specs = (P("grp", "tm", None), P("grp", "tm", None))
    split = dict(mesh.shape) == {"grp": 2, "tm": 4 * ZS}
    body = split_heads if split else shards
    return jax.shard_map(body, mesh=mesh, in_specs=in_specs, out_specs=out_specs, check_vma=False)
```

```python
import functools

import jax
import jax.numpy as jnp
from jax import lax
from jax.experimental import pallas as pl
from jax.experimental.pallas import tpu as pltpu
from jax.sharding import PartitionSpec as P

H = 6
DH = 128
epsilon = 1e-05

F32 = jnp.float32
BF16 = jnp.bfloat16
SEG = 128
D = 1536
HALF = 384
HEADS = HALF // DH
ROWS = 96
ZS = 4
BLK = 4 * ROWS
NT = (((1,), (1,)), ((), ()))
TN = (((0,), (0,)), ((), ()))


def dot(a, b, dims=(((1,), (0,)), ((), ()))):
    return lax.dot_general(a, b, dims, preferred_element_type=F32)


def place():
    t = lax.axis_index("tm")
    return t // 4, (t // 2) % 2, t % 2


def plane_columns(z, r):
    return pl.ds(pl.multiple_of(lax.rem(z - r + ZS, ZS) * BLK, 128), BLK)


def lanes(ref):
    return jnp.concatenate([ref[i : i + 1, :] for i in range(ref.shape[0])], axis=1)


def prepare_kernel(
    k_ref, v_ref, q_ref, o_ref, x_ref, gain_ref, pk_ref, flag_ref,
    shard, out_ref, pk_out, held, x_in, gain_in, pk_in, sems,
):
    z, _, _ = place()
    own = pl.ds(pl.multiple_of(lax.axis_index("grp") * HALF, 128), HALF)
    copies = [
        pltpu.make_async_copy(x_ref.at[0], x_in, sems.at[0]),
        pltpu.make_async_copy(gain_ref, gain_in, sems.at[1]),
        pltpu.make_async_copy(pk_ref.at[:, own], pk_in, sems.at[2]),
    ] + [
        pltpu.make_async_copy(ref, shard.at[i], sems.at[3 + i])
        for i, ref in enumerate((k_ref, v_ref, q_ref, o_ref))
    ]
    for copy in copies:
        copy.start()
    for copy in copies:
        copy.wait()
    x = x_in[...].astype(F32)
    center = jnp.mean(x, axis=-1, keepdims=True)
    moved = x - center
    spread = jnp.mean(jnp.square(moved), axis=-1, keepdims=True)
    held[...] = (moved * lax.rsqrt(spread + epsilon) * lanes(gain_in)).astype(BF16)
    for r in range(ZS):
        out_ref[0:SEG, r * BLK : (r + 1) * BLK] = held[:, plane_columns(z, r)]
    flag = flag_ref[0, 0].astype(F32)
    out_ref[SEG:, :] = jnp.full((16, D), flag, F32).astype(BF16)
    row = lax.broadcasted_iota(jnp.int32, (2 * SEG, 2 * SEG), 0)
    col = lax.broadcasted_iota(jnp.int32, (2 * SEG, 2 * SEG), 1)
    flip = jnp.where(row + col == 2 * SEG - 1, 1.0, 0.0).astype(BF16)
    pk_out[...] = dot(flip, pk_in[...]).astype(BF16)


def stage_kernel(shard_ref, normed_ref, shard, normed):
    shard[...] = shard_ref[...]
    normed[...] = normed_ref[...]


def shard_rows(r, j):
    _, y, c = place()
    yy = 1 - y if j % 2 else y
    cc = 1 - c if j // 2 else c
    return pl.ds(pl.multiple_of(r * BLK + (2 * yy + cc) * ROWS, 16), ROWS)


def fetch(pieces, first, weights, sems):
    copies = []
    for n in range(4 * ZS):
        for w in range(2):
            copies.append(
                pltpu.make_async_copy(
                    pieces[n].at[first[n] + w],
                    weights.at[shard_rows(n // 4, n % 4), pl.ds(w * HALF, HALF)],
                    sems.at[2 * n + w],
                )
            )
    for copy in copies:
        copy.start()
    return copies


def accumulate(x, weights, copies, columns):
    total = None
    for half in range(2):
        for copy in copies[half * 16 : half * 16 + 16]:
            copy.wait()
        rows = slice(half * 2 * BLK, (half + 1) * 2 * BLK)
        part = dot(x[:, rows], weights[rows, columns])
        total = part if total is None else total + part
    return total


def key_value_kernel(own_ref, oth_ref, *rest):
    pieces, (weights, kv_ref, xs, flags, sems) = rest[:16], rest[16:]
    copies = fetch(pieces, (0,) * 16, weights, sems)
    flags[0] = own_ref[SEG:, :DH]
    flags[1] = oth_ref[SEG:, :DH]
    xs[0:SEG, :] = own_ref[0:SEG, :]
    xs[SEG:, :] = oth_ref[0:SEG, :]
    total = accumulate(xs, weights, copies, slice(0, 2 * HALF))
    kv_ref[0] = total[:SEG].astype(BF16)
    kv_ref[1] = total[SEG:].astype(BF16)


SCALE = DH**-0.5
QO_PLACES = (2,) * 9 + (0,) + (2,) + (0,) + (2,) * 4


def head(i):
    return slice(i * DH, (i + 1) * DH)


def own_half(ref):
    g = lax.axis_index("grp")
    parts = [jnp.where(g == 0, ref[h : h + 1], ref[HEADS + h : HEADS + h + 1]) for h in range(HEADS)]
    return jnp.concatenate(parts, axis=1)


def query_kernel(xs, cot_own, cot_oth, cb_ref, pb_ref, kv_ref, pk_ref, *rest):
    pieces = rest[:16]
    weights, cq_ref, cg_ref, rel_ref, own_ref, dp_ref = rest[16:22]
    cots, sems = rest[22:]
    z, _, _ = place()
    copies = fetch(pieces, QO_PLACES, weights, sems)
    for r in range(ZS):
        cots[0:SEG, r * BLK : (r + 1) * BLK] = cot_own[:, plane_columns(z, r)]
        cots[SEG:, r * BLK : (r + 1) * BLK] = cot_oth[:, plane_columns(z, r)]
    q = accumulate(xs, weights, copies, slice(0, HALF))
    cq = (q + own_half(cb_ref)).astype(BF16)
    pq = (q + own_half(pb_ref)).astype(BF16)
    cg = dot(cots[...], weights[:, HALF:]).astype(BF16)
    row = lax.broadcasted_iota(jnp.int32, (SEG, SEG), 0)
    col = lax.broadcasted_iota(jnp.int32, (SEG, SEG), 1)
    for rec in range(2):
        rows = slice(rec * SEG, (rec + 1) * SEG)
        cq_ref[rec] = cq[rows]
        cg_ref[rec] = cg[rows]
        for h in range(HEADS):
            f, fv = head(h), head(HEADS + h)
            rel = dot(pq[rows, f], pk_ref[:, f], NT)
            rel = pltpu.roll(rel, SEG + 1, 1, stride=1, stride_axis=0)
            rel_ref[rec, h] = rel[:, :SEG]
            s_own = (dot(cq[rows, f], kv_ref[rec, :, f], NT) + rel[:, SEG:]) * SCALE
            own_ref[rec, h] = jnp.where(col <= row, s_own, -jnp.inf)
            dp_ref[rec, h] = dot(cg[rows, f], kv_ref[rec, :, fv], NT)


def memory_kernel(
    rec, flags, cq_ref, cg_ref, rel_ref, own_ref, dp_ref, kv_ref, mem_ref,
    p_ref, ds_ref, dmem_ref, ctx_ref,
):
    flag = flags[rec, 0:1, :].astype(F32)
    for h in range(HEADS):
        f, fv = head(h), head(HEADS + h)
        cq, g = cq_ref[rec, :, f], cg_ref[rec, :, f]
        s_own = own_ref[rec, h]
        s_mem = (dot(cq, mem_ref[rec, :, f], NT) + rel_ref[rec, h]) * SCALE
        s_mem = jnp.where(flag == 0, s_mem, -jnp.inf)
        dp_mem = dot(g, mem_ref[rec, :, fv], NT)
        peak = jnp.max(jnp.maximum(s_mem, s_own), axis=-1, keepdims=True)
        e_mem = jnp.exp(s_mem - peak)
        e_own = jnp.exp(s_own - peak)
        norm = 1.0 / jnp.sum(e_mem + e_own, axis=-1, keepdims=True)
        a_mem, a_own = e_mem * norm, e_own * norm
        dp_own = dp_ref[rec, h]
        inner = jnp.sum(a_mem * dp_mem + a_own * dp_own, axis=-1, keepdims=True)
        p_mem, p_own = a_mem.astype(BF16), a_own.astype(BF16)
        ctx = dot(p_mem, mem_ref[rec, :, fv]) + dot(p_own, kv_ref[rec, :, fv])
        ctx_ref[:, f] = ctx.astype(BF16)
        ds_mem = (a_mem * (dp_mem - inner) * SCALE).astype(BF16)
        p_ref[h] = p_own
        ds_ref[h, :, :SEG] = ds_mem
        ds_ref[h, :, SEG:] = (a_own * (dp_own - inner) * SCALE).astype(BF16)
        dmem_ref[:, f] = dot(ds_mem, cq, TN).astype(BF16)
        dmem_ref[:, fv] = dot(p_mem, g, TN).astype(BF16)


def grad_kernel(
    rec, p_ref, ds_ref, cq_ref, cg_ref, kv_ref, mem_ref, pk_ref, wkv, wqo, np_ref, dq, dkv
):
    row = lax.broadcasted_iota(jnp.int32, (SEG, SEG), 0)
    col = lax.broadcasted_iota(jnp.int32, (SEG, SEG), 1)
    flip = jnp.where(row + col == SEG - 1, 1.0, 0.0).astype(BF16)
    for h in range(HEADS):
        f, fv = head(h), head(HEADS + h)
        ds = ds_ref[h]
        rel = pltpu.roll(dot(flip, ds), 0, 1, stride=1, stride_axis=0).astype(BF16)
        rel = dot(flip, rel).astype(BF16)
        total = dot(ds[:, :SEG], mem_ref[rec, :, f]) + dot(ds[:, SEG:], kv_ref[rec, :, f])
        dq[:, f] = (total + dot(rel, pk_ref[:, f])).astype(BF16)
        dkv[:, f] = dot(ds[:, SEG:], cq_ref[rec, :, f], TN).astype(BF16)
        dkv[:, fv] = dot(p_ref[h], cg_ref[rec, :, f], TN).astype(BF16)
    np_ref[...] = dot(dq[...], wqo[:, :HALF], NT) + dot(dkv[...], wkv[...], NT)


def returned_kernel(np_ref, ret_ref, wkv, out_ref):
    out_ref[...] = (np_ref[...] + dot(ret_ref[...], wkv[...], NT)).astype(out_ref.dtype)


def partial_output_kernel(ctx_ref, wqo, out_ref):
    out_ref[...] = dot(ctx_ref[...], wqo[:, HALF:], NT).astype(BF16)


def output_kernel(x_ref, ctx_ref, wqo, lo_ret, out_ref, held):
    z, _, _ = place()
    held[...] = dot(ctx_ref[...], wqo[:, HALF:], NT)
    for r in range(ZS):
        cols, there = slice(r * BLK, (r + 1) * BLK), plane_columns(z, r)
        total = held[:, cols] + lo_ret[:, cols].astype(F32)
        out_ref[0, :, there] = (x_ref[0, :, there].astype(F32) + total).astype(BF16)


def hat_kernel(x_ref, gain_ref, cot_ref, hat_ref, rstd_ref, gain_out, cot_out, held):
    z, _, _ = place()
    x = x_ref[0].astype(F32)
    center = jnp.mean(x, axis=-1, keepdims=True)
    moved = x - center
    spread = jnp.mean(jnp.square(moved), axis=-1, keepdims=True)
    rstd = lax.rsqrt(spread + epsilon)
    held[0:SEG, :] = moved * rstd
    held[SEG:, :] = jnp.broadcast_to(lanes(gain_ref), (8, D))
    rstd_ref[...] = jnp.broadcast_to(rstd, (SEG, 128))
    for r in range(ZS):
        cols, there = slice(r * BLK, (r + 1) * BLK), plane_columns(z, r)
        hat_ref[:, cols] = held[0:SEG, there]
        gain_out[:, cols] = held[SEG:, there]
        cot_out[:, cols] = cot_ref[:, there]


def finish_kernel(hat_ref, rstd_ref, gain_ref, cot_ref, np_own, np_ret, grad_ref):
    z, _, _ = place()
    step = 32
    for i in range(0, SEG, step):
        rows = slice(i, i + step)
        hat, rstd = hat_ref[rows, :], rstd_ref[rows, 0:1]
        g = (np_own[rows, :] + np_ret[rows, :].astype(F32)) * gain_ref[0:1, :]
        mean_g = jnp.mean(g, axis=-1, keepdims=True)
        mean_gh = jnp.mean(g * hat, axis=-1, keepdims=True)
        grad = (rstd * (g - mean_g - hat * mean_gh)).astype(BF16)
        total = cot_ref[rows, :] + grad
        for r in range(ZS):
            grad_ref[0, rows, plane_columns(z, r)] = total[:, r * BLK : (r + 1) * BLK]


def call(kernel, outs, scratch=(), in_specs=None, mib=24):
    return pl.pallas_call(
        kernel,
        out_shape=outs,
        in_specs=in_specs,
        out_specs=jax.tree.map(lambda _: VM, outs),
        scratch_shapes=list(scratch),
        compiler_params=pltpu.CompilerParams(vmem_limit_bytes=mib * 1024 * 1024),
        cost_estimate=pl.CostEstimate(
            flops=0, bytes_accessed=1024, transcendentals=0
        ),
    )


def shape(*dims, dtype=BF16):
    return jax.ShapeDtypeStruct(dims, dtype)


VM = pl.BlockSpec(memory_space=pltpu.VMEM)
SM = pl.BlockSpec(memory_space=pltpu.SMEM)
ANY = pl.BlockSpec(memory_space=pl.ANY)


def moved_by(f):
    route = []
    for z in range(ZS):
        for y in range(2):
            for c in range(2):
                zz, yy, cc = f(z, y, c)
                route.append((4 * z + 2 * y + c, 4 * zz + 2 * yy + cc))
    return lambda block: lax.ppermute(block, "tm", route)


up = moved_by(lambda z, y, c: ((z + 1) % ZS, y, c))
down = moved_by(lambda z, y, c: ((z - 1) % ZS, y, c))
across = moved_by(lambda z, y, c: (z, 1 - y, c))
sibling = moved_by(lambda z, y, c: (z, y, 1 - c))


def after(block, *earlier):
    return lax.optimization_barrier((block, *earlier))[0]


def other(block):
    return lax.ppermute(block, "grp", [(0, 1), (1, 0)])


def split_heads(
    inputs,
    norm_gain,
    query_weight,
    key_weight,
    value_weight,
    output_weight,
    content_bias,
    position_bias,
    position_keys,
    start_flags,
    cotangent,
):
    cot = cotangent[0]
    gain = norm_gain.reshape(D // 128, 128)
    w0, normed, pk = call(
        prepare_kernel,
        (shape(4, ROWS, HALF), shape(SEG + 16, D), shape(2 * SEG, HALF)),
        [
            pltpu.VMEM((SEG, D), BF16),
            pltpu.VMEM((SEG, D), BF16),
            pltpu.VMEM((D // 128, 128), F32),
            pltpu.VMEM((2 * SEG, HALF), BF16),
            pltpu.SemaphoreType.DMA((7,)),
        ],
        [ANY] * 7 + [SM],
        62,
    )(
        key_weight, value_weight, query_weight, output_weight, inputs, gain, position_keys,
        start_flags,
    )
    normed_oth = other(normed)
    w1 = up(w0)
    w0y = across(w0)
    w3 = down(w0)
    w0_near, normed = call(
        stage_kernel, (shape(4, ROWS, HALF), shape(SEG + 16, D)), (), [VM] * 2
    )(w0, normed)
    w1 = after(w1, w0_near)
    cot_oth = other(after(cot, w1))
    w1y = across(w1)
    w2 = up(w1)
    w3y = across(w3)
    w2y_kv = up(after(w1y, w3)[:2])
    w2y_qo = across(after(w2, w3)[2:])
    here = [w0_near, w0y, w1, w1y, w2, w2y_kv, w3, w3y]
    there = [sibling(p) for p in [w0] + here[1:]]
    w2y_qo_there = sibling(w2y_qo)
    kv_pieces = []
    for r in range(ZS):
        kv_pieces += here[2 * r : 2 * r + 2] + there[2 * r : 2 * r + 2]
    qo_pieces = list(kv_pieces)
    qo_pieces[9], qo_pieces[11] = w2y_qo, w2y_qo_there

    half = shape(SEG, 2 * HALF)
    wkv, kv, xs, flags = call(
        key_value_kernel,
        (
            shape(D, 2 * HALF),
            shape(2, SEG, 2 * HALF),
            shape(2 * SEG, D),
            shape(2, 16, DH),
        ),
        [pltpu.SemaphoreType.DMA((32,))],
        [VM, VM] + [ANY] * 16,
    )(after(normed, w2y_qo, cot_oth), normed_oth, *kv_pieces)
    steps = lax.axis_size("tm")
    onward = [(i, i + 1) for i in range(steps - 1)]
    back = [(i + 1, i) for i in range(steps - 1)]
    mem = lax.ppermute(kv, "tm", onward)
    blocks = shape(2, HEADS, SEG, SEG, dtype=F32)
    wqo, cq, cg, rel, s_own, dp_own = call(
        query_kernel,
        (shape(D, 2 * HALF), shape(2, SEG, HALF), shape(2, SEG, HALF), blocks, blocks, blocks),
        [pltpu.VMEM((2 * SEG, D), BF16), pltpu.SemaphoreType.DMA((32,))],
        [VM] * 7 + [ANY] * 16,
    )(
        xs, cot, cot_oth, content_bias.reshape(H, DH), position_bias.reshape(H, DH),
        kv, pk, *qo_pieces,
    )

    def memory(rec, kv_rows, mem_rows):
        return call(
            functools.partial(memory_kernel, rec),
            (shape(HEADS, SEG, SEG), shape(HEADS, SEG, 2 * SEG), half, shape(SEG, HALF)),
            (),
            [VM] * 8,
        )(flags, cq, cg, rel, s_own, dp_own, kv_rows, mem_rows)

    def grads(rec, p, ds, kv_rows, mem_rows):
        return call(
            functools.partial(grad_kernel, rec),
            shape(SEG, D, dtype=F32),
            [pltpu.VMEM((SEG, HALF), BF16), pltpu.VMEM((SEG, 2 * HALF), BF16)],
            [VM] * 9,
        )(p, ds, cq, cg, kv_rows, mem_rows, pk, wkv, wqo)

    p_oth, ds_oth, dmem_oth, ctx_oth = memory(1, kv, mem)
    lo_oth = call(partial_output_kernel, shape(SEG, D), (), [VM] * 2)(ctx_oth, wqo)
    lo_ret = other(lo_oth)
    ret_oth = lax.ppermute(dmem_oth, "tm", back)
    p, ds, dmem, ctx = memory(0, kv, after(mem, lo_oth))
    ret = lax.ppermute(after(dmem, lo_ret), "tm", back)
    partial_oth = grads(1, after(p_oth, dmem), ds_oth, kv, mem)
    np_oth = call(returned_kernel, shape(SEG, D), (), [VM] * 3)(partial_oth, ret_oth, wkv)
    np_ret = other(np_oth)
    partial = grads(0, after(p, np_oth), ds, kv, mem)
    layer_out = call(
        output_kernel, shape(1, SEG, D), [pltpu.VMEM((SEG, D), F32)], [VM] * 4
    )(inputs, after(ctx, partial), wqo, lo_ret)
    np_own = call(returned_kernel, shape(SEG, D, dtype=F32), (), [VM] * 3)(
        after(partial, layer_out), ret, wkv
    )
    hat = call(
        hat_kernel,
        (
            shape(SEG, D, dtype=F32),
            shape(SEG, 128, dtype=F32),
            shape(8, D, dtype=F32),
            shape(SEG, D),
        ),
        [pltpu.VMEM((SEG + 8, D), F32)],
        [VM] * 3,
    )(inputs, gain, after(cot, partial))
    input_grad = call(finish_kernel, shape(1, SEG, D), (), [VM] * 6)(
        *hat, after(np_own, hat[0]), np_ret
    )
    return (layer_out, input_grad)


def from_behind(block, axis, distance):
    devices = range(lax.axis_size(axis))
    route = [(i - distance, i) for i in devices if i - distance in devices]
    return lax.ppermute(block, axis, route)


def normalize_project(
    inputs, norm_gain, query_weight, key_weight, value_weight, content_bias, position_bias
):
    widened = inputs.astype(jnp.float32)
    center = jnp.mean(widened, axis=-1, keepdims=True)
    spread = jnp.mean(jnp.square(widened - center), axis=-1, keepdims=True)
    normed = ((widened - center) * lax.rsqrt(spread + epsilon) * norm_gain).astype(jnp.bfloat16)
    projected = jnp.dot(normed, query_weight, preferred_element_type=jnp.float32)
    content_query = (projected + content_bias).astype(jnp.bfloat16)
    position_query = (projected + position_bias).astype(jnp.bfloat16)
    key_rows = jnp.dot(normed, key_weight, preferred_element_type=jnp.float32).astype(jnp.bfloat16)
    value_rows = jnp.dot(normed, value_weight, preferred_element_type=jnp.float32).astype(
        jnp.bfloat16
    )
    return (content_query, position_query, key_rows, value_rows)


def attend(
    content_query,
    position_query,
    key_rows,
    value_rows,
    memory_keys,
    memory_values,
    position_keys,
    keep_memory,
):
    length = content_query.shape[0]
    all_keys = jnp.concatenate([memory_keys, key_rows], axis=0).reshape(2 * length, H, DH)
    all_values = jnp.concatenate([memory_values, value_rows], axis=0).reshape(2 * length, H, DH)
    content = content_query.reshape(length, H, DH)
    located = position_query.reshape(length, H, DH)
    distance_keys = position_keys[::-1].reshape(2 * length, H, DH)
    direct = jnp.einsum("ihd,jhd->hij", content, all_keys, preferred_element_type=jnp.float32)
    relative = jnp.einsum(
        "ihd,jhd->hij", located, distance_keys, preferred_element_type=jnp.float32
    )
    padded = jnp.pad(relative, ((0, 0), (0, 0), (0, 1)))
    skewed = padded.reshape(H, length * (2 * length + 1))[
        :, length - 1 : length - 1 + 2 * length * length
    ]
    skewed = skewed.reshape(H, length, 2 * length)
    scores = (direct + skewed) * DH ** (-0.5)
    key_index = lax.broadcasted_iota(jnp.int32, (length, 2 * length), 1)
    query_index = lax.broadcasted_iota(jnp.int32, (length, 2 * length), 0)
    allowed = (key_index <= query_index + length) & (keep_memory | (key_index >= length))
    scores = jnp.where(allowed[None], scores, -jnp.inf)
    row_peak = lax.stop_gradient(jnp.max(scores, axis=-1, keepdims=True))
    raised = jnp.exp(scores - row_peak)
    attention = (raised / jnp.sum(raised, axis=-1, keepdims=True)).astype(jnp.bfloat16)
    gathered = jnp.einsum("hij,jhd->ihd", attention, all_values, preferred_element_type=jnp.float32)
    return gathered.reshape(length, H * DH).astype(jnp.bfloat16)


def finish(inputs, context, output_weight):
    update = lax.dot_general(
        context,
        output_weight,
        (((context.ndim - 1,), (1,)), ((), ())),
        preferred_element_type=jnp.float32,
    )
    return (inputs.astype(jnp.float32) + update).astype(jnp.bfloat16)


def shards(
    inputs,
    norm_gain,
    query_weight,
    key_weight,
    value_weight,
    output_weight,
    content_bias,
    position_bias,
    position_keys,
    start_flags,
    cotangent,
):
    partial_weights = (
        lax.all_gather(query_weight, "grp", axis=1, tiled=True),
        lax.all_gather(key_weight, "grp", axis=1, tiled=True),
        lax.all_gather(value_weight, "grp", axis=1, tiled=True),
        lax.all_gather(output_weight, "grp", axis=1, tiled=True),
    )
    full_weights = (
        lax.all_gather(partial_weights[0], "tm", axis=0, tiled=True),
        lax.all_gather(partial_weights[1], "tm", axis=0, tiled=True),
        lax.all_gather(partial_weights[2], "tm", axis=0, tiled=True),
        lax.all_gather(partial_weights[3], "tm", axis=0, tiled=True),
    )
    query_full, key_full, value_full, output_full = full_weights
    own_inputs = inputs[0]
    own_cotangent = cotangent[0]
    keep_memory = start_flags[0, 0] == 0

    def project(local_inputs):
        return normalize_project(
            local_inputs, norm_gain, query_full, key_full, value_full, content_bias, position_bias
        )

    projections, project_back = jax.vjp(project, own_inputs)
    content_query, position_query, key_rows, value_rows = projections
    memory_keys, memory_values = from_behind((key_rows, value_rows), "tm", 1)

    def attend_local(
        local_content, local_position, local_keys, local_values, prior_keys, prior_values
    ):
        return attend(
            local_content,
            local_position,
            local_keys,
            local_values,
            prior_keys,
            prior_values,
            position_keys,
            keep_memory,
        )

    context, attend_back = jax.vjp(
        attend_local,
        content_query,
        position_query,
        key_rows,
        value_rows,
        memory_keys,
        memory_values,
    )

    def combine(local_inputs, local_context):
        return finish(local_inputs, local_context, output_full)

    layer_out, finish_back = jax.vjp(combine, own_inputs, context)
    residual_grad, context_grad = finish_back(own_cotangent)
    attend_grads = attend_back(context_grad)
    returned_keys, returned_values = from_behind((attend_grads[4], attend_grads[5]), "tm", -1)
    key_grad = attend_grads[2] + returned_keys
    value_grad = attend_grads[3] + returned_values
    (norm_grad,) = project_back((attend_grads[0], attend_grads[1], key_grad, value_grad))
    input_grad = residual_grad + norm_grad
    return (layer_out[None], input_grad[None])


def solution(mesh):
    in_specs = (
        P("grp", "tm", None),
        P(),
        P("tm", "grp"),
        P("tm", "grp"),
        P("tm", "grp"),
        P("tm", "grp"),
        P(),
        P(),
        P(),
        P("grp", "tm"),
        P("grp", "tm", None),
    )
    out_specs = (P("grp", "tm", None), P("grp", "tm", None))
    split = dict(mesh.shape) == {"grp": 2, "tm": 4 * ZS}
    body = split_heads if split else shards
    return jax.shard_map(body, mesh=mesh, in_specs=in_specs, out_specs=out_specs, check_vma=False)
```

```python
import functools

import jax
import jax.numpy as jnp
from jax import lax
from jax.experimental import pallas as pl
from jax.experimental.pallas import tpu as pltpu
from jax.sharding import PartitionSpec as P

H = 6
DH = 128
epsilon = 1e-05

F32 = jnp.float32
BF16 = jnp.bfloat16
SEG = 128
D = 1536
HALF = 384
HEADS = HALF // DH
ROWS = 96
ZS = 4
BLK = 4 * ROWS
NT = (((1,), (1,)), ((), ()))
TN = (((0,), (0,)), ((), ()))


def dot(a, b, dims=(((1,), (0,)), ((), ()))):
    return lax.dot_general(a, b, dims, preferred_element_type=F32)


def place():
    t = lax.axis_index("tm")
    return t // 4, (t // 2) % 2, t % 2


def plane_columns(z, r):
    return pl.ds(pl.multiple_of(lax.rem(z - r + ZS, ZS) * BLK, 128), BLK)


def lanes(ref):
    return jnp.concatenate([ref[i : i + 1, :] for i in range(ref.shape[0])], axis=1)


def prepare_kernel(
    k_ref, v_ref, q_ref, o_ref, x_ref, gain_ref, pk_ref, flag_ref,
    shard, out_ref, pk_out, held, x_in, gain_in, pk_in, sems,
):
    z, _, _ = place()
    own = pl.ds(pl.multiple_of(lax.axis_index("grp") * HALF, 128), HALF)
    copies = [
        pltpu.make_async_copy(x_ref.at[0], x_in, sems.at[0]),
        pltpu.make_async_copy(gain_ref, gain_in, sems.at[1]),
        pltpu.make_async_copy(pk_ref.at[:, own], pk_in, sems.at[2]),
    ] + [
        pltpu.make_async_copy(ref, shard.at[i], sems.at[3 + i])
        for i, ref in enumerate((k_ref, v_ref, q_ref, o_ref))
    ]
    for copy in copies:
        copy.start()
    for copy in copies:
        copy.wait()
    x = x_in[...].astype(F32)
    center = jnp.mean(x, axis=-1, keepdims=True)
    moved = x - center
    spread = jnp.mean(jnp.square(moved), axis=-1, keepdims=True)
    held[...] = (moved * lax.rsqrt(spread + epsilon) * lanes(gain_in)).astype(BF16)
    for r in range(ZS):
        out_ref[0:SEG, r * BLK : (r + 1) * BLK] = held[:, plane_columns(z, r)]
    flag = flag_ref[0, 0].astype(F32)
    out_ref[SEG:, :] = jnp.full((16, D), flag, F32).astype(BF16)
    row = lax.broadcasted_iota(jnp.int32, (2 * SEG, 2 * SEG), 0)
    col = lax.broadcasted_iota(jnp.int32, (2 * SEG, 2 * SEG), 1)
    flip = jnp.where(row + col == 2 * SEG - 1, 1.0, 0.0).astype(BF16)
    pk_out[...] = dot(flip, pk_in[...]).astype(BF16)


def stage_kernel(shard_ref, normed_ref, shard, normed):
    shard[...] = shard_ref[...]
    normed[...] = normed_ref[...]


def shard_rows(r, j):
    _, y, c = place()
    yy = 1 - y if j % 2 else y
    cc = 1 - c if j // 2 else c
    return pl.ds(pl.multiple_of(r * BLK + (2 * yy + cc) * ROWS, 16), ROWS)


def fetch(pieces, first, weights, sems):
    copies = []
    for n in range(4 * ZS):
        for w in range(2):
            copies.append(
                pltpu.make_async_copy(
                    pieces[n].at[first[n] + w],
                    weights.at[shard_rows(n // 4, n % 4), pl.ds(w * HALF, HALF)],
                    sems.at[2 * n + w],
                )
            )
    for copy in copies:
        copy.start()
    return copies


def accumulate(x, weights, copies, columns):
    total = None
    for half in range(2):
        for copy in copies[half * 16 : half * 16 + 16]:
            copy.wait()
        rows = slice(half * 2 * BLK, (half + 1) * 2 * BLK)
        part = dot(x[:, rows], weights[rows, columns])
        total = part if total is None else total + part
    return total


def key_value_kernel(own_ref, oth_ref, *rest):
    pieces, (weights, kv_own, kv_oth, xs, flags, sems) = rest[:16], rest[16:]
    copies = fetch(pieces, (0,) * 16, weights, sems)
    flags[0] = own_ref[SEG:, :DH]
    flags[1] = oth_ref[SEG:, :DH]
    xs[0:SEG, :] = own_ref[0:SEG, :]
    xs[SEG:, :] = oth_ref[0:SEG, :]
    total = accumulate(xs, weights, copies, slice(0, 2 * HALF))
    kv_own[...] = total[:SEG].astype(BF16)
    kv_oth[...] = total[SEG:].astype(BF16)


SCALE = DH**-0.5
QO_PLACES = (2,) * 9 + (0,) + (2,) + (0,) + (2,) * 4


def head(i):
    return slice(i * DH, (i + 1) * DH)


def own_half(ref):
    g = lax.axis_index("grp")
    parts = [jnp.where(g == 0, ref[h : h + 1], ref[HEADS + h : HEADS + h + 1]) for h in range(HEADS)]
    return jnp.concatenate(parts, axis=1)


def query_kernel(xs, cot_own, cot_oth, cb_ref, pb_ref, kv_own, kv_oth, pk_ref, *rest):
    pieces = rest[:16]
    weights, cq_ref, cg_ref, rel_ref, own_ref, dp_ref = rest[16:22]
    cots, sems = rest[22:]
    z, _, _ = place()
    copies = fetch(pieces, QO_PLACES, weights, sems)
    for r in range(ZS):
        cots[0:SEG, r * BLK : (r + 1) * BLK] = cot_own[:, plane_columns(z, r)]
        cots[SEG:, r * BLK : (r + 1) * BLK] = cot_oth[:, plane_columns(z, r)]
    q = accumulate(xs, weights, copies, slice(0, HALF))
    cq = (q + own_half(cb_ref)).astype(BF16)
    pq = (q + own_half(pb_ref)).astype(BF16)
    cg = dot(cots[...], weights[:, HALF:]).astype(BF16)
    row = lax.broadcasted_iota(jnp.int32, (SEG, SEG), 0)
    col = lax.broadcasted_iota(jnp.int32, (SEG, SEG), 1)
    every = [(rec, h) for rec in range(2) for h in range(HEADS)]
    rows = [slice(rec * SEG, (rec + 1) * SEG) for rec in range(2)]
    kv = (kv_own, kv_oth)
    rel = [dot(pq[rows[rec], head(h)], pk_ref[:, head(h)], NT) for rec, h in every]
    own = [dot(cq[rows[rec], head(h)], kv[rec][:, head(h)], NT) for rec, h in every]
    for rec, h in every:
        dp_ref[rec, h] = dot(cg[rows[rec], head(h)], kv[rec][:, head(HEADS + h)], NT)
    for n, (rec, h) in enumerate(every):
        turned = pltpu.roll(rel[n], SEG + 1, 1, stride=1, stride_axis=0)
        rel_ref[rec, h] = turned[:, :SEG]
        s_own = (own[n] + turned[:, SEG:]) * SCALE
        own_ref[rec, h] = jnp.where(col <= row, s_own, -jnp.inf)
    for rec in range(2):
        cq_ref[rec] = cq[rows[rec]]
        cg_ref[rec] = cg[rows[rec]]


def memory_kernel(
    rec, flags, cq_ref, cg_ref, rel_ref, own_ref, dp_ref, kv_ref, mem_ref,
    p_ref, ds_ref, dmem_ref, ctx_ref,
):
    flag = flags[rec, 0:1, :].astype(F32)
    heads = range(HEADS)
    s_mem = [dot(cq_ref[rec, :, head(h)], mem_ref[:, head(h)], NT) for h in heads]
    dp_mem = [dot(cg_ref[rec, :, head(h)], mem_ref[:, head(HEADS + h)], NT) for h in heads]
    parts = []
    for h in heads:
        s = jnp.where(flag == 0, (s_mem[h] + rel_ref[rec, h]) * SCALE, -jnp.inf)
        s_own, dp_own = own_ref[rec, h], dp_ref[rec, h]
        peak = jnp.max(jnp.maximum(s, s_own), axis=-1, keepdims=True)
        e_mem, e_own = jnp.exp(s - peak), jnp.exp(s_own - peak)
        norm = 1.0 / jnp.sum(e_mem + e_own, axis=-1, keepdims=True)
        inner = jnp.sum(e_mem * dp_mem[h] + e_own * dp_own, axis=-1, keepdims=True) * norm
        a_mem, a_own = e_mem * norm, e_own * norm
        p_mem, p_own = a_mem.astype(BF16), a_own.astype(BF16)
        ds_mem = (a_mem * (dp_mem[h] - inner) * SCALE).astype(BF16)
        ds_own = (a_own * (dp_own - inner) * SCALE).astype(BF16)
        p_ref[h] = p_own
        ds_ref[:, 2 * SEG * h : 2 * SEG * h + SEG] = ds_mem
        ds_ref[:, 2 * SEG * h + SEG : 2 * SEG * (h + 1)] = ds_own
        parts.append((p_mem, p_own, ds_mem))
    for h in heads:
        f, fv = head(h), head(HEADS + h)
        p_mem, p_own, ds_mem = parts[h]
        dmem_ref[:, f] = dot(ds_mem, cq_ref[rec, :, f], TN).astype(BF16)
        dmem_ref[:, fv] = dot(p_mem, cg_ref[rec, :, f], TN).astype(BF16)
        ctx = dot(p_mem, mem_ref[:, fv]) + dot(p_own, kv_ref[:, fv])
        ctx_ref[:, f] = ctx.astype(BF16)


def grad_kernel(
    rec, p_ref, ds_ref, cq_ref, cg_ref, kv_ref, mem_ref, pk_ref, wqo, np_ref, dkv, dq
):
    row = lax.broadcasted_iota(jnp.int32, (SEG, SEG), 0)
    col = lax.broadcasted_iota(jnp.int32, (SEG, SEG), 1)
    flip = jnp.where(row + col == SEG - 1, 1.0, 0.0).astype(BF16)
    both = [slice(2 * SEG * h, 2 * SEG * (h + 1)) for h in range(HEADS)]
    rel = dot(flip, ds_ref[...])
    rel = [pltpu.roll(rel[:, w], 0, 1, stride=1, stride_axis=0).astype(BF16) for w in both]
    rel = dot(flip, jnp.concatenate(rel, axis=1)).astype(BF16)
    for h, w in enumerate(both):
        f, fv = head(h), head(HEADS + h)
        ds_mem, ds_own = ds_ref[:, w][:, :SEG], ds_ref[:, w][:, SEG:]
        dkv[:, f] = dot(ds_own, cq_ref[rec, :, f], TN).astype(BF16)
        dkv[:, fv] = dot(p_ref[h], cg_ref[rec, :, f], TN).astype(BF16)
        total = dot(ds_mem, mem_ref[:, f]) + dot(ds_own, kv_ref[:, f])
        dq[:, f] = (total + dot(rel[:, w], pk_ref[:, f])).astype(BF16)
    np_ref[...] = dot(dq[...], wqo[:, :HALF], NT)


def returned_kernel(np_ref, dkv_ref, ret_ref, wkv, out_ref):
    dkv = (dkv_ref[...].astype(F32) + ret_ref[...].astype(F32)).astype(BF16)
    out_ref[...] = (np_ref[...] + dot(dkv, wkv[...], NT)).astype(out_ref.dtype)


def partial_output_kernel(ctx_ref, wqo, out_ref):
    out_ref[...] = dot(ctx_ref[...], wqo[:, HALF:], NT).astype(BF16)


def output_kernel(x_ref, ctx_ref, wqo, lo_ret, out_ref):
    z, _, _ = place()
    total = dot(ctx_ref[...], wqo[:, HALF:], NT)
    for r in range(ZS):
        cols, there = slice(r * BLK, (r + 1) * BLK), plane_columns(z, r)
        part = total[:, cols] + lo_ret[:, cols].astype(F32)
        out_ref[0, :, there] = (x_ref[0, :, there].astype(F32) + part).astype(BF16)


def hat_kernel(x_ref, gain_ref, cot_ref, hat_ref, rstd_ref, gain_out, cot_out, held):
    z, _, _ = place()
    x = x_ref[0].astype(F32)
    center = jnp.mean(x, axis=-1, keepdims=True)
    moved = x - center
    spread = jnp.mean(jnp.square(moved), axis=-1, keepdims=True)
    rstd = lax.rsqrt(spread + epsilon)
    held[0:SEG, :] = moved * rstd
    held[SEG:, :] = jnp.broadcast_to(lanes(gain_ref), (8, D))
    rstd_ref[...] = jnp.broadcast_to(rstd, (SEG, 128))
    for r in range(ZS):
        cols, there = slice(r * BLK, (r + 1) * BLK), plane_columns(z, r)
        hat_ref[:, cols] = held[0:SEG, there]
        gain_out[:, cols] = held[SEG:, there]
        cot_out[:, cols] = cot_ref[:, there]


def finish_kernel(hat_ref, rstd_ref, gain_ref, cot_ref, np_own, np_ret, grad_ref):
    z, _, _ = place()
    step = 32
    for i in range(0, SEG, step):
        rows = slice(i, i + step)
        hat, rstd = hat_ref[rows, :], rstd_ref[rows, 0:1]
        g = (np_own[rows, :] + np_ret[rows, :].astype(F32)) * gain_ref[0:1, :]
        mean_g = jnp.mean(g, axis=-1, keepdims=True)
        mean_gh = jnp.mean(g * hat, axis=-1, keepdims=True)
        grad = (rstd * (g - mean_g - hat * mean_gh)).astype(BF16)
        total = cot_ref[rows, :] + grad
        for r in range(ZS):
            grad_ref[0, rows, plane_columns(z, r)] = total[:, r * BLK : (r + 1) * BLK]


def call(kernel, outs, scratch=(), in_specs=None, mib=24):
    return pl.pallas_call(
        kernel,
        out_shape=outs,
        in_specs=in_specs,
        out_specs=jax.tree.map(lambda _: VM, outs),
        scratch_shapes=list(scratch),
        compiler_params=pltpu.CompilerParams(vmem_limit_bytes=mib * 1024 * 1024),
        cost_estimate=pl.CostEstimate(
            flops=0, bytes_accessed=1024, transcendentals=0
        ),
    )


def shape(*dims, dtype=BF16):
    return jax.ShapeDtypeStruct(dims, dtype)


VM = pl.BlockSpec(memory_space=pltpu.VMEM)
SM = pl.BlockSpec(memory_space=pltpu.SMEM)
ANY = pl.BlockSpec(memory_space=pl.ANY)


def moved_by(f):
    route = []
    for z in range(ZS):
        for y in range(2):
            for c in range(2):
                zz, yy, cc = f(z, y, c)
                route.append((4 * z + 2 * y + c, 4 * zz + 2 * yy + cc))
    return lambda block: lax.ppermute(block, "tm", route)


up = moved_by(lambda z, y, c: ((z + 1) % ZS, y, c))
down = moved_by(lambda z, y, c: ((z - 1) % ZS, y, c))
across = moved_by(lambda z, y, c: (z, 1 - y, c))
sibling = moved_by(lambda z, y, c: (z, y, 1 - c))


def after(block, *earlier):
    return lax.optimization_barrier((block, *earlier))[0]


def other(block):
    return lax.ppermute(block, "grp", [(0, 1), (1, 0)])


def split_heads(
    inputs,
    norm_gain,
    query_weight,
    key_weight,
    value_weight,
    output_weight,
    content_bias,
    position_bias,
    position_keys,
    start_flags,
    cotangent,
):
    cot = cotangent[0]
    gain = norm_gain.reshape(D // 128, 128)
    w0, normed, pk = call(
        prepare_kernel,
        (shape(4, ROWS, HALF), shape(SEG + 16, D), shape(2 * SEG, HALF)),
        [
            pltpu.VMEM((SEG, D), BF16),
            pltpu.VMEM((SEG, D), BF16),
            pltpu.VMEM((D // 128, 128), F32),
            pltpu.VMEM((2 * SEG, HALF), BF16),
            pltpu.SemaphoreType.DMA((7,)),
        ],
        [ANY] * 7 + [SM],
        62,
    )(
        key_weight, value_weight, query_weight, output_weight, inputs, gain, position_keys,
        start_flags,
    )
    normed_oth = other(normed)
    w1 = up(w0)
    w0y = across(w0)
    w3 = down(w0)
    w0_near, normed = call(
        stage_kernel, (shape(4, ROWS, HALF), shape(SEG + 16, D)), (), [VM] * 2
    )(w0, normed)
    w1 = after(w1, w0_near)
    cot_oth = other(after(cot, w1))
    w1y = across(w1)
    w2 = up(w1)
    w3y = across(w3)
    w2y_kv = up(after(w1y, w3)[:2])
    w2y_qo = across(after(w2, w3)[2:])
    here = [w0_near, w0y, w1, w1y, w2, w2y_kv, w3, w3y]
    there = [sibling(p) for p in [w0] + here[1:]]
    w2y_qo_there = sibling(w2y_qo)
    kv_pieces = []
    for r in range(ZS):
        kv_pieces += here[2 * r : 2 * r + 2] + there[2 * r : 2 * r + 2]
    qo_pieces = list(kv_pieces)
    qo_pieces[9], qo_pieces[11] = w2y_qo, w2y_qo_there

    half = shape(SEG, 2 * HALF)
    wkv, kv, kv_oth, xs, flags = call(
        key_value_kernel,
        (
            shape(D, 2 * HALF),
            half,
            half,
            shape(2 * SEG, D),
            shape(2, 16, DH),
        ),
        [pltpu.SemaphoreType.DMA((32,))],
        [VM, VM] + [ANY] * 16,
    )(after(normed, w2y_qo, cot_oth), normed_oth, *kv_pieces)
    steps = lax.axis_size("tm")
    onward = [(i, i + 1) for i in range(steps - 1)]
    back = [(i + 1, i) for i in range(steps - 1)]
    mem_oth = lax.ppermute(kv_oth, "tm", onward)
    mem = lax.ppermute(kv, "tm", onward)
    blocks = shape(2, HEADS, SEG, SEG, dtype=F32)
    wqo, cq, cg, rel, s_own, dp_own = call(
        query_kernel,
        (shape(D, 2 * HALF), shape(2, SEG, HALF), shape(2, SEG, HALF), blocks, blocks, blocks),
        [pltpu.VMEM((2 * SEG, D), BF16), pltpu.SemaphoreType.DMA((32,))],
        [VM] * 8 + [ANY] * 16,
    )(
        xs, cot, cot_oth, content_bias.reshape(H, DH), position_bias.reshape(H, DH),
        kv, kv_oth, pk, *qo_pieces,
    )

    def memory(rec, kv_rows, mem_rows):
        return call(
            functools.partial(memory_kernel, rec),
            (shape(HEADS, SEG, SEG), shape(SEG, HEADS * 2 * SEG), half, shape(SEG, HALF)),
            (),
            [VM] * 8,
        )(flags, cq, cg, rel, s_own, dp_own, kv_rows, mem_rows)

    def grads(rec, p, ds, kv_rows, mem_rows):
        return call(
            functools.partial(grad_kernel, rec),
            (shape(SEG, D, dtype=F32), half),
            [pltpu.VMEM((SEG, HALF), BF16)],
            [VM] * 8,
        )(p, ds, cq, cg, kv_rows, mem_rows, pk, wqo)

    p_oth, ds_oth, dmem_oth, ctx_oth = memory(1, kv_oth, mem_oth)
    lo_oth = call(partial_output_kernel, shape(SEG, D), (), [VM] * 2)(ctx_oth, wqo)
    lo_ret = other(lo_oth)
    ret_oth = lax.ppermute(dmem_oth, "tm", back)
    partial_oth, dkv_oth = grads(1, after(p_oth, lo_oth), ds_oth, kv_oth, mem_oth)
    np_oth = call(returned_kernel, shape(SEG, D), (), [VM] * 4)(
        partial_oth, dkv_oth, ret_oth, wkv
    )
    np_ret = other(np_oth)
    p, ds, dmem, ctx = memory(0, kv, after(mem, np_oth))
    ret = lax.ppermute(after(dmem, lo_ret), "tm", back)
    partial, dkv = grads(0, after(p, dmem), ds, kv, mem)
    layer_out = call(
        output_kernel, shape(1, SEG, D), (), [VM] * 4
    )(inputs, after(ctx, partial), wqo, lo_ret)
    np_own = call(returned_kernel, shape(SEG, D, dtype=F32), (), [VM] * 4)(
        after(partial, layer_out), dkv, ret, wkv
    )
    hat = call(
        hat_kernel,
        (
            shape(SEG, D, dtype=F32),
            shape(SEG, 128, dtype=F32),
            shape(8, D, dtype=F32),
            shape(SEG, D),
        ),
        [pltpu.VMEM((SEG + 8, D), F32)],
        [VM] * 3,
    )(inputs, gain, after(cot, partial))
    input_grad = call(finish_kernel, shape(1, SEG, D), (), [VM] * 6)(
        *hat, after(np_own, hat[0]), np_ret
    )
    return (layer_out, input_grad)


def from_behind(block, axis, distance):
    devices = range(lax.axis_size(axis))
    route = [(i - distance, i) for i in devices if i - distance in devices]
    return lax.ppermute(block, axis, route)


def normalize_project(
    inputs, norm_gain, query_weight, key_weight, value_weight, content_bias, position_bias
):
    widened = inputs.astype(jnp.float32)
    center = jnp.mean(widened, axis=-1, keepdims=True)
    spread = jnp.mean(jnp.square(widened - center), axis=-1, keepdims=True)
    normed = ((widened - center) * lax.rsqrt(spread + epsilon) * norm_gain).astype(jnp.bfloat16)
    projected = jnp.dot(normed, query_weight, preferred_element_type=jnp.float32)
    content_query = (projected + content_bias).astype(jnp.bfloat16)
    position_query = (projected + position_bias).astype(jnp.bfloat16)
    key_rows = jnp.dot(normed, key_weight, preferred_element_type=jnp.float32).astype(jnp.bfloat16)
    value_rows = jnp.dot(normed, value_weight, preferred_element_type=jnp.float32).astype(
        jnp.bfloat16
    )
    return (content_query, position_query, key_rows, value_rows)


def attend(
    content_query,
    position_query,
    key_rows,
    value_rows,
    memory_keys,
    memory_values,
    position_keys,
    keep_memory,
):
    length = content_query.shape[0]
    all_keys = jnp.concatenate([memory_keys, key_rows], axis=0).reshape(2 * length, H, DH)
    all_values = jnp.concatenate([memory_values, value_rows], axis=0).reshape(2 * length, H, DH)
    content = content_query.reshape(length, H, DH)
    located = position_query.reshape(length, H, DH)
    distance_keys = position_keys[::-1].reshape(2 * length, H, DH)
    direct = jnp.einsum("ihd,jhd->hij", content, all_keys, preferred_element_type=jnp.float32)
    relative = jnp.einsum(
        "ihd,jhd->hij", located, distance_keys, preferred_element_type=jnp.float32
    )
    padded = jnp.pad(relative, ((0, 0), (0, 0), (0, 1)))
    skewed = padded.reshape(H, length * (2 * length + 1))[
        :, length - 1 : length - 1 + 2 * length * length
    ]
    skewed = skewed.reshape(H, length, 2 * length)
    scores = (direct + skewed) * DH ** (-0.5)
    key_index = lax.broadcasted_iota(jnp.int32, (length, 2 * length), 1)
    query_index = lax.broadcasted_iota(jnp.int32, (length, 2 * length), 0)
    allowed = (key_index <= query_index + length) & (keep_memory | (key_index >= length))
    scores = jnp.where(allowed[None], scores, -jnp.inf)
    row_peak = lax.stop_gradient(jnp.max(scores, axis=-1, keepdims=True))
    raised = jnp.exp(scores - row_peak)
    attention = (raised / jnp.sum(raised, axis=-1, keepdims=True)).astype(jnp.bfloat16)
    gathered = jnp.einsum("hij,jhd->ihd", attention, all_values, preferred_element_type=jnp.float32)
    return gathered.reshape(length, H * DH).astype(jnp.bfloat16)


def finish(inputs, context, output_weight):
    update = lax.dot_general(
        context,
        output_weight,
        (((context.ndim - 1,), (1,)), ((), ())),
        preferred_element_type=jnp.float32,
    )
    return (inputs.astype(jnp.float32) + update).astype(jnp.bfloat16)


def shards(
    inputs,
    norm_gain,
    query_weight,
    key_weight,
    value_weight,
    output_weight,
    content_bias,
    position_bias,
    position_keys,
    start_flags,
    cotangent,
):
    partial_weights = (
        lax.all_gather(query_weight, "grp", axis=1, tiled=True),
        lax.all_gather(key_weight, "grp", axis=1, tiled=True),
        lax.all_gather(value_weight, "grp", axis=1, tiled=True),
        lax.all_gather(output_weight, "grp", axis=1, tiled=True),
    )
    full_weights = (
        lax.all_gather(partial_weights[0], "tm", axis=0, tiled=True),
        lax.all_gather(partial_weights[1], "tm", axis=0, tiled=True),
        lax.all_gather(partial_weights[2], "tm", axis=0, tiled=True),
        lax.all_gather(partial_weights[3], "tm", axis=0, tiled=True),
    )
    query_full, key_full, value_full, output_full = full_weights
    own_inputs = inputs[0]
    own_cotangent = cotangent[0]
    keep_memory = start_flags[0, 0] == 0

    def project(local_inputs):
        return normalize_project(
            local_inputs, norm_gain, query_full, key_full, value_full, content_bias, position_bias
        )

    projections, project_back = jax.vjp(project, own_inputs)
    content_query, position_query, key_rows, value_rows = projections
    memory_keys, memory_values = from_behind((key_rows, value_rows), "tm", 1)

    def attend_local(
        local_content, local_position, local_keys, local_values, prior_keys, prior_values
    ):
        return attend(
            local_content,
            local_position,
            local_keys,
            local_values,
            prior_keys,
            prior_values,
            position_keys,
            keep_memory,
        )

    context, attend_back = jax.vjp(
        attend_local,
        content_query,
        position_query,
        key_rows,
        value_rows,
        memory_keys,
        memory_values,
    )

    def combine(local_inputs, local_context):
        return finish(local_inputs, local_context, output_full)

    layer_out, finish_back = jax.vjp(combine, own_inputs, context)
    residual_grad, context_grad = finish_back(own_cotangent)
    attend_grads = attend_back(context_grad)
    returned_keys, returned_values = from_behind((attend_grads[4], attend_grads[5]), "tm", -1)
    key_grad = attend_grads[2] + returned_keys
    value_grad = attend_grads[3] + returned_values
    (norm_grad,) = project_back((attend_grads[0], attend_grads[1], key_grad, value_grad))
    input_grad = residual_grad + norm_grad
    return (layer_out[None], input_grad[None])


def solution(mesh):
    in_specs = (
        P("grp", "tm", None),
        P(),
        P("tm", "grp"),
        P("tm", "grp"),
        P("tm", "grp"),
        P("tm", "grp"),
        P(),
        P(),
        P(),
        P("grp", "tm"),
        P("grp", "tm", None),
    )
    out_specs = (P("grp", "tm", None), P("grp", "tm", None))
    split = dict(mesh.shape) == {"grp": 2, "tm": 4 * ZS}
    body = split_heads if split else shards
    return jax.shard_map(body, mesh=mesh, in_specs=in_specs, out_specs=out_specs, check_vma=False)
```

```python
import functools

import jax
import jax.numpy as jnp
from jax import lax
from jax.experimental import pallas as pl
from jax.experimental.pallas import tpu as pltpu
from jax.sharding import PartitionSpec as P

H = 6
DH = 128
epsilon = 1e-05

F32 = jnp.float32
BF16 = jnp.bfloat16
SEG = 128
D = 1536
HALF = 384
HEADS = HALF // DH
ROWS = 96
ZS = 4
BLK = 4 * ROWS
NT = (((1,), (1,)), ((), ()))
TN = (((0,), (0,)), ((), ()))


def dot(a, b, dims=(((1,), (0,)), ((), ()))):
    return lax.dot_general(a, b, dims, preferred_element_type=F32)


def place():
    t = lax.axis_index("tm")
    return t // 4, (t // 2) % 2, t % 2


def plane_columns(z, r):
    return pl.ds(pl.multiple_of(lax.rem(z - r + ZS, ZS) * BLK, 128), BLK)


def lanes(ref):
    return jnp.concatenate([ref[i : i + 1, :] for i in range(ref.shape[0])], axis=1)


def prepare_kernel(
    k_ref, v_ref, q_ref, o_ref, x_ref, gain_ref, pk_ref, flag_ref,
    shard, out_ref, pk_out, held, x_in, gain_in, pk_in, sems,
):
    z, _, _ = place()
    own = pl.ds(pl.multiple_of(lax.axis_index("grp") * HALF, 128), HALF)
    copies = [
        pltpu.make_async_copy(x_ref.at[0], x_in, sems.at[0]),
        pltpu.make_async_copy(gain_ref, gain_in, sems.at[1]),
        pltpu.make_async_copy(pk_ref.at[:, own], pk_in, sems.at[2]),
    ] + [
        pltpu.make_async_copy(ref, shard.at[i], sems.at[3 + i])
        for i, ref in enumerate((k_ref, v_ref, q_ref, o_ref))
    ]
    for copy in copies:
        copy.start()
    for copy in copies:
        copy.wait()
    x = x_in[...].astype(F32)
    center = jnp.mean(x, axis=-1, keepdims=True)
    moved = x - center
    spread = jnp.mean(jnp.square(moved), axis=-1, keepdims=True)
    held[...] = (moved * lax.rsqrt(spread + epsilon) * lanes(gain_in)).astype(BF16)
    for r in range(ZS):
        out_ref[0:SEG, r * BLK : (r + 1) * BLK] = held[:, plane_columns(z, r)]
    flag = flag_ref[0, 0].astype(F32)
    out_ref[SEG:, :] = jnp.full((16, D), flag, F32).astype(BF16)
    row = lax.broadcasted_iota(jnp.int32, (2 * SEG, 2 * SEG), 0)
    col = lax.broadcasted_iota(jnp.int32, (2 * SEG, 2 * SEG), 1)
    flip = jnp.where(row + col == 2 * SEG - 1, 1.0, 0.0).astype(BF16)
    pk_out[...] = dot(flip, pk_in[...]).astype(BF16)


def stage_kernel(shard_ref, normed_ref, shard, normed):
    shard[...] = shard_ref[...]
    normed[...] = normed_ref[...]


def shard_rows(r, j):
    _, y, c = place()
    yy = 1 - y if j % 2 else y
    cc = 1 - c if j // 2 else c
    return pl.ds(pl.multiple_of(r * BLK + (2 * yy + cc) * ROWS, 16), ROWS)


def fetch(pieces, first, weights, sems):
    copies = []
    for n in range(4 * ZS):
        for w in range(2):
            copies.append(
                pltpu.make_async_copy(
                    pieces[n].at[first[n] + w],
                    weights.at[shard_rows(n // 4, n % 4), pl.ds(w * HALF, HALF)],
                    sems.at[2 * n + w],
                )
            )
    for copy in copies:
        copy.start()
    return copies


def accumulate(x, weights, copies, columns):
    for copy in copies:
        copy.wait()
    return dot(x[...], weights[:, columns])


def key_value_kernel(own_ref, oth_ref, *rest):
    pieces, (weights, kv_own, kv_oth, xs, flags, sems) = rest[:16], rest[16:]
    copies = fetch(pieces, (0,) * 16, weights, sems)
    flags[0] = own_ref[SEG:, :DH]
    flags[1] = oth_ref[SEG:, :DH]
    xs[0:SEG, :] = own_ref[0:SEG, :]
    xs[SEG:, :] = oth_ref[0:SEG, :]
    total = accumulate(xs, weights, copies, slice(0, 2 * HALF))
    kv_own[...] = total[:SEG].astype(BF16)
    kv_oth[...] = total[SEG:].astype(BF16)


SCALE = DH**-0.5
QO_PLACES = (2,) * 9 + (0,) + (2,) + (0,) + (2,) * 4


def head(i):
    return slice(i * DH, (i + 1) * DH)


def own_half(ref):
    g = lax.axis_index("grp")
    parts = [jnp.where(g == 0, ref[h : h + 1], ref[HEADS + h : HEADS + h + 1]) for h in range(HEADS)]
    return jnp.concatenate(parts, axis=1)


def query_kernel(xs, cot_own, cot_oth, cb_ref, pb_ref, kv_own, kv_oth, pk_ref, *rest):
    pieces = rest[:16]
    weights, cq_ref, cg_ref, rel_ref, own_ref, dp_ref = rest[16:22]
    cots, sems = rest[22:]
    z, _, _ = place()
    copies = fetch(pieces, QO_PLACES, weights, sems)
    for r in range(ZS):
        cots[0:SEG, r * BLK : (r + 1) * BLK] = cot_own[:, plane_columns(z, r)]
        cots[SEG:, r * BLK : (r + 1) * BLK] = cot_oth[:, plane_columns(z, r)]
    q = accumulate(xs, weights, copies, slice(0, HALF))
    cq = (q + own_half(cb_ref)).astype(BF16)
    pq = (q + own_half(pb_ref)).astype(BF16)
    cg = dot(cots[...], weights[:, HALF:]).astype(BF16)
    row = lax.broadcasted_iota(jnp.int32, (SEG, SEG), 0)
    col = lax.broadcasted_iota(jnp.int32, (SEG, SEG), 1)
    every = [(rec, h) for rec in range(2) for h in range(HEADS)]
    rows = [slice(rec * SEG, (rec + 1) * SEG) for rec in range(2)]
    kv = (kv_own, kv_oth)
    rel = [dot(pq[rows[rec], head(h)], pk_ref[:, head(h)], NT) for rec, h in every]
    own = [dot(cq[rows[rec], head(h)], kv[rec][:, head(h)], NT) for rec, h in every]
    for rec, h in every:
        dp_ref[rec, h] = dot(cg[rows[rec], head(h)], kv[rec][:, head(HEADS + h)], NT)
    for n, (rec, h) in enumerate(every):
        turned = pltpu.roll(rel[n], SEG + 1, 1, stride=1, stride_axis=0)
        rel_ref[rec, h] = turned[:, :SEG]
        s_own = (own[n] + turned[:, SEG:]) * SCALE
        own_ref[rec, h] = jnp.where(col <= row, s_own, -jnp.inf)
    for rec in range(2):
        cq_ref[rec] = cq[rows[rec]]
        cg_ref[rec] = cg[rows[rec]]


def memory_kernel(
    rec, flags, cq_ref, cg_ref, rel_ref, own_ref, dp_ref, kv_ref, mem_ref,
    p_ref, ds_ref, dmem_ref, ctx_ref,
):
    flag = flags[rec, 0:1, :].astype(F32)
    heads = range(HEADS)
    s_mem = [dot(cq_ref[rec, :, head(h)], mem_ref[:, head(h)], NT) for h in heads]
    dp_mem = [dot(cg_ref[rec, :, head(h)], mem_ref[:, head(HEADS + h)], NT) for h in heads]
    parts = []
    for h in heads:
        s = jnp.where(flag == 0, (s_mem[h] + rel_ref[rec, h]) * SCALE, -jnp.inf)
        s_own, dp_own = own_ref[rec, h], dp_ref[rec, h]
        peak = jnp.max(jnp.maximum(s, s_own), axis=-1, keepdims=True)
        e_mem, e_own = jnp.exp(s - peak), jnp.exp(s_own - peak)
        norm = 1.0 / jnp.sum(e_mem + e_own, axis=-1, keepdims=True)
        inner = jnp.sum(e_mem * dp_mem[h] + e_own * dp_own, axis=-1, keepdims=True) * norm
        a_mem, a_own = e_mem * norm, e_own * norm
        p_mem, p_own = a_mem.astype(BF16), a_own.astype(BF16)
        ds_mem = (a_mem * (dp_mem[h] - inner) * SCALE).astype(BF16)
        ds_own = (a_own * (dp_own - inner) * SCALE).astype(BF16)
        p_ref[h] = p_own
        ds_ref[:, 2 * SEG * h : 2 * SEG * h + SEG] = ds_mem
        ds_ref[:, 2 * SEG * h + SEG : 2 * SEG * (h + 1)] = ds_own
        parts.append((p_mem, p_own, ds_mem))
    for h in heads:
        f, fv = head(h), head(HEADS + h)
        p_mem, p_own, ds_mem = parts[h]
        dmem_ref[:, f] = dot(ds_mem, cq_ref[rec, :, f], TN).astype(BF16)
        dmem_ref[:, fv] = dot(p_mem, cg_ref[rec, :, f], TN).astype(BF16)
        ctx = dot(p_mem, mem_ref[:, fv]) + dot(p_own, kv_ref[:, fv])
        ctx_ref[:, f] = ctx.astype(BF16)


def grad_kernel(
    rec, p_ref, ds_ref, cq_ref, cg_ref, kv_ref, mem_ref, pk_ref, wqo, np_ref, dkv, dq
):
    row = lax.broadcasted_iota(jnp.int32, (SEG, SEG), 0)
    col = lax.broadcasted_iota(jnp.int32, (SEG, SEG), 1)
    flip = jnp.where(row + col == SEG - 1, 1.0, 0.0).astype(BF16)
    both = [slice(2 * SEG * h, 2 * SEG * (h + 1)) for h in range(HEADS)]
    rel = dot(flip, ds_ref[...])
    rel = [pltpu.roll(rel[:, w], 0, 1, stride=1, stride_axis=0).astype(BF16) for w in both]
    rel = dot(flip, jnp.concatenate(rel, axis=1)).astype(BF16)
    for h, w in enumerate(both):
        f, fv = head(h), head(HEADS + h)
        ds_mem, ds_own = ds_ref[:, w][:, :SEG], ds_ref[:, w][:, SEG:]
        dkv[:, f] = dot(ds_own, cq_ref[rec, :, f], TN).astype(BF16)
        dkv[:, fv] = dot(p_ref[h], cg_ref[rec, :, f], TN).astype(BF16)
        total = dot(ds_mem, mem_ref[:, f]) + dot(ds_own, kv_ref[:, f])
        dq[:, f] = (total + dot(rel[:, w], pk_ref[:, f])).astype(BF16)
    np_ref[...] = dot(dq[...], wqo[:, :HALF], NT)


def returned_kernel(np_ref, dkv_ref, ret_ref, wkv, out_ref):
    dkv = (dkv_ref[...].astype(F32) + ret_ref[...].astype(F32)).astype(BF16)
    out_ref[...] = (np_ref[...] + dot(dkv, wkv[...], NT)).astype(out_ref.dtype)


def partial_output_kernel(ctx_ref, wqo, out_ref):
    out_ref[...] = dot(ctx_ref[...], wqo[:, HALF:], NT).astype(BF16)


def output_kernel(x_ref, ctx_ref, wqo, lo_ret, out_ref):
    z, _, _ = place()
    total = dot(ctx_ref[...], wqo[:, HALF:], NT)
    for r in range(ZS):
        cols, there = slice(r * BLK, (r + 1) * BLK), plane_columns(z, r)
        part = total[:, cols] + lo_ret[:, cols].astype(F32)
        out_ref[0, :, there] = (x_ref[0, :, there].astype(F32) + part).astype(BF16)


def hat_kernel(x_ref, gain_ref, cot_ref, hat_ref, rstd_ref, gain_out, cot_out, held):
    z, _, _ = place()
    x = x_ref[0].astype(F32)
    center = jnp.mean(x, axis=-1, keepdims=True)
    moved = x - center
    spread = jnp.mean(jnp.square(moved), axis=-1, keepdims=True)
    rstd = lax.rsqrt(spread + epsilon)
    held[0:SEG, :] = moved * rstd
    held[SEG:, :] = jnp.broadcast_to(lanes(gain_ref), (8, D))
    rstd_ref[...] = jnp.broadcast_to(rstd, (SEG, 128))
    for r in range(ZS):
        cols, there = slice(r * BLK, (r + 1) * BLK), plane_columns(z, r)
        hat_ref[:, cols] = held[0:SEG, there]
        gain_out[:, cols] = held[SEG:, there]
        cot_out[:, cols] = cot_ref[:, there]


def finish_kernel(hat_ref, rstd_ref, gain_ref, cot_ref, np_own, np_ret, grad_ref):
    z, _, _ = place()
    step = 32
    for i in range(0, SEG, step):
        rows = slice(i, i + step)
        hat, rstd = hat_ref[rows, :], rstd_ref[rows, 0:1]
        g = (np_own[rows, :] + np_ret[rows, :].astype(F32)) * gain_ref[0:1, :]
        mean_g = jnp.mean(g, axis=-1, keepdims=True)
        mean_gh = jnp.mean(g * hat, axis=-1, keepdims=True)
        grad = (rstd * (g - mean_g - hat * mean_gh)).astype(BF16)
        total = cot_ref[rows, :] + grad
        for r in range(ZS):
            grad_ref[0, rows, plane_columns(z, r)] = total[:, r * BLK : (r + 1) * BLK]


def call(kernel, outs, scratch=(), in_specs=None, mib=24):
    return pl.pallas_call(
        kernel,
        out_shape=outs,
        in_specs=in_specs,
        out_specs=jax.tree.map(lambda _: VM, outs),
        scratch_shapes=list(scratch),
        compiler_params=pltpu.CompilerParams(vmem_limit_bytes=mib * 1024 * 1024),
        cost_estimate=pl.CostEstimate(
            flops=0, bytes_accessed=1024, transcendentals=0
        ),
    )


def shape(*dims, dtype=BF16):
    return jax.ShapeDtypeStruct(dims, dtype)


VM = pl.BlockSpec(memory_space=pltpu.VMEM)
SM = pl.BlockSpec(memory_space=pltpu.SMEM)
ANY = pl.BlockSpec(memory_space=pl.ANY)


def moved_by(f):
    route = []
    for z in range(ZS):
        for y in range(2):
            for c in range(2):
                zz, yy, cc = f(z, y, c)
                route.append((4 * z + 2 * y + c, 4 * zz + 2 * yy + cc))
    return lambda block: lax.ppermute(block, "tm", route)


up = moved_by(lambda z, y, c: ((z + 1) % ZS, y, c))
down = moved_by(lambda z, y, c: ((z - 1) % ZS, y, c))
across = moved_by(lambda z, y, c: (z, 1 - y, c))
sibling = moved_by(lambda z, y, c: (z, y, 1 - c))


def after(block, *earlier):
    return lax.optimization_barrier((block, *earlier))[0]


def other(block):
    return lax.ppermute(block, "grp", [(0, 1), (1, 0)])


def split_heads(
    inputs,
    norm_gain,
    query_weight,
    key_weight,
    value_weight,
    output_weight,
    content_bias,
    position_bias,
    position_keys,
    start_flags,
    cotangent,
):
    cot = cotangent[0]
    gain = norm_gain.reshape(D // 128, 128)
    w0, normed, pk = call(
        prepare_kernel,
        (shape(4, ROWS, HALF), shape(SEG + 16, D), shape(2 * SEG, HALF)),
        [
            pltpu.VMEM((SEG, D), BF16),
            pltpu.VMEM((SEG, D), BF16),
            pltpu.VMEM((D // 128, 128), F32),
            pltpu.VMEM((2 * SEG, HALF), BF16),
            pltpu.SemaphoreType.DMA((7,)),
        ],
        [ANY] * 7 + [SM],
        62,
    )(
        key_weight, value_weight, query_weight, output_weight, inputs, gain, position_keys,
        start_flags,
    )
    normed_oth = other(normed)
    w1 = up(w0)
    w0y = across(w0)
    w3 = down(w0)
    w0_near, normed = call(
        stage_kernel, (shape(4, ROWS, HALF), shape(SEG + 16, D)), (), [VM] * 2
    )(w0, normed)
    w1 = after(w1, w0_near)
    cot_oth = other(after(cot, w1))
    w1y = across(w1)
    w2 = up(w1)
    w3y = across(w3)
    w2y_kv = up(after(w1y, w3)[:2])
    w2y_qo = across(after(w2, w3)[2:])
    here = [w0_near, w0y, w1, w1y, w2, w2y_kv, w3, w3y]
    there = [sibling(p) for p in [w0] + here[1:]]
    w2y_qo_there = sibling(w2y_qo)
    kv_pieces = []
    for r in range(ZS):
        kv_pieces += here[2 * r : 2 * r + 2] + there[2 * r : 2 * r + 2]
    qo_pieces = list(kv_pieces)
    qo_pieces[9], qo_pieces[11] = w2y_qo, w2y_qo_there

    half = shape(SEG, 2 * HALF)
    wkv, kv, kv_oth, xs, flags = call(
        key_value_kernel,
        (
            shape(D, 2 * HALF),
            half,
            half,
            shape(2 * SEG, D),
            shape(2, 16, DH),
        ),
        [pltpu.SemaphoreType.DMA((32,))],
        [VM, VM] + [ANY] * 16,
    )(after(normed, w2y_qo, cot_oth), normed_oth, *kv_pieces)
    steps = lax.axis_size("tm")
    onward = [(i, i + 1) for i in range(steps - 1)]
    back = [(i + 1, i) for i in range(steps - 1)]
    mem_oth = lax.ppermute(kv_oth, "tm", onward)
    mem = lax.ppermute(kv, "tm", onward)
    blocks = shape(2, HEADS, SEG, SEG, dtype=F32)
    wqo, cq, cg, rel, s_own, dp_own = call(
        query_kernel,
        (shape(D, 2 * HALF), shape(2, SEG, HALF), shape(2, SEG, HALF), blocks, blocks, blocks),
        [pltpu.VMEM((2 * SEG, D), BF16), pltpu.SemaphoreType.DMA((32,))],
        [VM] * 8 + [ANY] * 16,
    )(
        xs, cot, cot_oth, content_bias.reshape(H, DH), position_bias.reshape(H, DH),
        kv, kv_oth, pk, *qo_pieces,
    )

    def memory(rec, kv_rows, mem_rows):
        return call(
            functools.partial(memory_kernel, rec),
            (shape(HEADS, SEG, SEG), shape(SEG, HEADS * 2 * SEG), half, shape(SEG, HALF)),
            (),
            [VM] * 8,
        )(flags, cq, cg, rel, s_own, dp_own, kv_rows, mem_rows)

    def grads(rec, p, ds, kv_rows, mem_rows):
        return call(
            functools.partial(grad_kernel, rec),
            (shape(SEG, D, dtype=F32), half),
            [pltpu.VMEM((SEG, HALF), BF16)],
            [VM] * 8,
        )(p, ds, cq, cg, kv_rows, mem_rows, pk, wqo)

    p_oth, ds_oth, dmem_oth, ctx_oth = memory(1, kv_oth, mem_oth)
    lo_oth = call(partial_output_kernel, shape(SEG, D), (), [VM] * 2)(ctx_oth, wqo)
    lo_ret = other(lo_oth)
    ret_oth = lax.ppermute(dmem_oth, "tm", back)
    partial_oth, dkv_oth = grads(1, after(p_oth, lo_oth), ds_oth, kv_oth, mem_oth)
    np_oth = call(returned_kernel, shape(SEG, D), (), [VM] * 4)(
        partial_oth, dkv_oth, ret_oth, wkv
    )
    np_ret = other(np_oth)
    hat = call(
        hat_kernel,
        (
            shape(SEG, D, dtype=F32),
            shape(SEG, 128, dtype=F32),
            shape(8, D, dtype=F32),
            shape(SEG, D),
        ),
        [pltpu.VMEM((SEG + 8, D), F32)],
        [VM] * 3,
    )(inputs, gain, after(cot, np_oth))
    p, ds, dmem, ctx = memory(0, kv, after(mem, np_oth, hat[0]))
    ret = lax.ppermute(after(dmem, lo_ret), "tm", back)
    partial, dkv = grads(0, after(p, dmem), ds, kv, mem)
    layer_out = call(
        output_kernel, shape(1, SEG, D), (), [VM] * 4
    )(inputs, after(ctx, partial), wqo, lo_ret)
    np_own = call(returned_kernel, shape(SEG, D, dtype=F32), (), [VM] * 4)(
        after(partial, layer_out), dkv, ret, wkv
    )
    input_grad = call(finish_kernel, shape(1, SEG, D), (), [VM] * 6)(
        *hat, after(np_own, hat[0]), np_ret
    )
    return (layer_out, input_grad)


def from_behind(block, axis, distance):
    devices = range(lax.axis_size(axis))
    route = [(i - distance, i) for i in devices if i - distance in devices]
    return lax.ppermute(block, axis, route)


def normalize_project(
    inputs, norm_gain, query_weight, key_weight, value_weight, content_bias, position_bias
):
    widened = inputs.astype(jnp.float32)
    center = jnp.mean(widened, axis=-1, keepdims=True)
    spread = jnp.mean(jnp.square(widened - center), axis=-1, keepdims=True)
    normed = ((widened - center) * lax.rsqrt(spread + epsilon) * norm_gain).astype(jnp.bfloat16)
    projected = jnp.dot(normed, query_weight, preferred_element_type=jnp.float32)
    content_query = (projected + content_bias).astype(jnp.bfloat16)
    position_query = (projected + position_bias).astype(jnp.bfloat16)
    key_rows = jnp.dot(normed, key_weight, preferred_element_type=jnp.float32).astype(jnp.bfloat16)
    value_rows = jnp.dot(normed, value_weight, preferred_element_type=jnp.float32).astype(
        jnp.bfloat16
    )
    return (content_query, position_query, key_rows, value_rows)


def attend(
    content_query,
    position_query,
    key_rows,
    value_rows,
    memory_keys,
    memory_values,
    position_keys,
    keep_memory,
):
    length = content_query.shape[0]
    all_keys = jnp.concatenate([memory_keys, key_rows], axis=0).reshape(2 * length, H, DH)
    all_values = jnp.concatenate([memory_values, value_rows], axis=0).reshape(2 * length, H, DH)
    content = content_query.reshape(length, H, DH)
    located = position_query.reshape(length, H, DH)
    distance_keys = position_keys[::-1].reshape(2 * length, H, DH)
    direct = jnp.einsum("ihd,jhd->hij", content, all_keys, preferred_element_type=jnp.float32)
    relative = jnp.einsum(
        "ihd,jhd->hij", located, distance_keys, preferred_element_type=jnp.float32
    )
    padded = jnp.pad(relative, ((0, 0), (0, 0), (0, 1)))
    skewed = padded.reshape(H, length * (2 * length + 1))[
        :, length - 1 : length - 1 + 2 * length * length
    ]
    skewed = skewed.reshape(H, length, 2 * length)
    scores = (direct + skewed) * DH ** (-0.5)
    key_index = lax.broadcasted_iota(jnp.int32, (length, 2 * length), 1)
    query_index = lax.broadcasted_iota(jnp.int32, (length, 2 * length), 0)
    allowed = (key_index <= query_index + length) & (keep_memory | (key_index >= length))
    scores = jnp.where(allowed[None], scores, -jnp.inf)
    row_peak = lax.stop_gradient(jnp.max(scores, axis=-1, keepdims=True))
    raised = jnp.exp(scores - row_peak)
    attention = (raised / jnp.sum(raised, axis=-1, keepdims=True)).astype(jnp.bfloat16)
    gathered = jnp.einsum("hij,jhd->ihd", attention, all_values, preferred_element_type=jnp.float32)
    return gathered.reshape(length, H * DH).astype(jnp.bfloat16)


def finish(inputs, context, output_weight):
    update = lax.dot_general(
        context,
        output_weight,
        (((context.ndim - 1,), (1,)), ((), ())),
        preferred_element_type=jnp.float32,
    )
    return (inputs.astype(jnp.float32) + update).astype(jnp.bfloat16)


def shards(
    inputs,
    norm_gain,
    query_weight,
    key_weight,
    value_weight,
    output_weight,
    content_bias,
    position_bias,
    position_keys,
    start_flags,
    cotangent,
):
    partial_weights = (
        lax.all_gather(query_weight, "grp", axis=1, tiled=True),
        lax.all_gather(key_weight, "grp", axis=1, tiled=True),
        lax.all_gather(value_weight, "grp", axis=1, tiled=True),
        lax.all_gather(output_weight, "grp", axis=1, tiled=True),
    )
    full_weights = (
        lax.all_gather(partial_weights[0], "tm", axis=0, tiled=True),
        lax.all_gather(partial_weights[1], "tm", axis=0, tiled=True),
        lax.all_gather(partial_weights[2], "tm", axis=0, tiled=True),
        lax.all_gather(partial_weights[3], "tm", axis=0, tiled=True),
    )
    query_full, key_full, value_full, output_full = full_weights
    own_inputs = inputs[0]
    own_cotangent = cotangent[0]
    keep_memory = start_flags[0, 0] == 0

    def project(local_inputs):
        return normalize_project(
            local_inputs, norm_gain, query_full, key_full, value_full, content_bias, position_bias
        )

    projections, project_back = jax.vjp(project, own_inputs)
    content_query, position_query, key_rows, value_rows = projections
    memory_keys, memory_values = from_behind((key_rows, value_rows), "tm", 1)

    def attend_local(
        local_content, local_position, local_keys, local_values, prior_keys, prior_values
    ):
        return attend(
            local_content,
            local_position,
            local_keys,
            local_values,
            prior_keys,
            prior_values,
            position_keys,
            keep_memory,
        )

    context, attend_back = jax.vjp(
        attend_local,
        content_query,
        position_query,
        key_rows,
        value_rows,
        memory_keys,
        memory_values,
    )

    def combine(local_inputs, local_context):
        return finish(local_inputs, local_context, output_full)

    layer_out, finish_back = jax.vjp(combine, own_inputs, context)
    residual_grad, context_grad = finish_back(own_cotangent)
    attend_grads = attend_back(context_grad)
    returned_keys, returned_values = from_behind((attend_grads[4], attend_grads[5]), "tm", -1)
    key_grad = attend_grads[2] + returned_keys
    value_grad = attend_grads[3] + returned_values
    (norm_grad,) = project_back((attend_grads[0], attend_grads[1], key_grad, value_grad))
    input_grad = residual_grad + norm_grad
    return (layer_out[None], input_grad[None])


def solution(mesh):
    in_specs = (
        P("grp", "tm", None),
        P(),
        P("tm", "grp"),
        P("tm", "grp"),
        P("tm", "grp"),
        P("tm", "grp"),
        P(),
        P(),
        P(),
        P("grp", "tm"),
        P("grp", "tm", None),
    )
    out_specs = (P("grp", "tm", None), P("grp", "tm", None))
    split = dict(mesh.shape) == {"grp": 2, "tm": 4 * ZS}
    body = split_heads if split else shards
    return jax.shard_map(body, mesh=mesh, in_specs=in_specs, out_specs=out_specs, check_vma=False)
```

```python
import functools

import jax
import jax.numpy as jnp
from jax import lax
from jax.experimental import pallas as pl
from jax.experimental.pallas import tpu as pltpu
from jax.sharding import PartitionSpec as P

H = 6
DH = 128
epsilon = 1e-05

F32 = jnp.float32
BF16 = jnp.bfloat16
SEG = 128
D = 1536
HALF = 384
HEADS = HALF // DH
ROWS = 96
ZS = 4
BLK = 4 * ROWS
NT = (((1,), (1,)), ((), ()))
TN = (((0,), (0,)), ((), ()))


def dot(a, b, dims=(((1,), (0,)), ((), ()))):
    return lax.dot_general(a, b, dims, preferred_element_type=F32)


def place():
    t = lax.axis_index("tm")
    return t // 4, (t // 2) % 2, t % 2


def plane_columns(z, r):
    return pl.ds(pl.multiple_of(lax.rem(z - r + ZS, ZS) * BLK, 128), BLK)


def lanes(ref):
    return jnp.concatenate([ref[i : i + 1, :] for i in range(ref.shape[0])], axis=1)


def prepare_kernel(
    k_ref, v_ref, q_ref, o_ref, x_ref, gain_ref, pk_ref, flag_ref,
    shard, out_ref, pk_out, held, x_in, gain_in, pk_in, sems,
):
    z, _, _ = place()
    own = pl.ds(pl.multiple_of(lax.axis_index("grp") * HALF, 128), HALF)
    copies = [
        pltpu.make_async_copy(x_ref.at[0], x_in, sems.at[0]),
        pltpu.make_async_copy(gain_ref, gain_in, sems.at[1]),
        pltpu.make_async_copy(pk_ref.at[:, own], pk_in, sems.at[2]),
    ] + [
        pltpu.make_async_copy(ref, shard.at[i], sems.at[3 + i])
        for i, ref in enumerate((k_ref, v_ref, q_ref, o_ref))
    ]
    for copy in copies:
        copy.start()
    for copy in copies:
        copy.wait()
    x = x_in[...].astype(F32)
    center = jnp.mean(x, axis=-1, keepdims=True)
    moved = x - center
    spread = jnp.mean(jnp.square(moved), axis=-1, keepdims=True)
    held[...] = (moved * lax.rsqrt(spread + epsilon) * lanes(gain_in)).astype(BF16)
    for r in range(ZS):
        out_ref[0:SEG, r * BLK : (r + 1) * BLK] = held[:, plane_columns(z, r)]
    flag = flag_ref[0, 0].astype(F32)
    out_ref[SEG:, :] = jnp.full((16, D), flag, F32).astype(BF16)
    row = lax.broadcasted_iota(jnp.int32, (2 * SEG, 2 * SEG), 0)
    col = lax.broadcasted_iota(jnp.int32, (2 * SEG, 2 * SEG), 1)
    flip = jnp.where(row + col == 2 * SEG - 1, 1.0, 0.0).astype(BF16)
    pk_out[...] = dot(flip, pk_in[...]).astype(BF16)


def stage_kernel(shard_ref, normed_ref, shard, normed):
    shard[...] = shard_ref[...]
    normed[...] = normed_ref[...]


def shard_rows(r, j):
    _, y, c = place()
    yy = 1 - y if j % 2 else y
    cc = 1 - c if j // 2 else c
    return pl.ds(pl.multiple_of(r * BLK + (2 * yy + cc) * ROWS, 16), ROWS)


def fetch(pieces, first, weights, sems):
    copies = []
    for n in range(4 * ZS):
        for w in range(2):
            copies.append(
                pltpu.make_async_copy(
                    pieces[n].at[first[n] + w],
                    weights.at[shard_rows(n // 4, n % 4), pl.ds(w * HALF, HALF)],
                    sems.at[2 * n + w],
                )
            )
    for copy in copies:
        copy.start()
    return copies


def accumulate(x, weights, copies, columns):
    for copy in copies:
        copy.wait()
    return dot(x[...], weights[:, columns])


def key_value_kernel(own_ref, oth_ref, *rest):
    pieces, (weights, kv_own, kv_oth, xs, flags, sems) = rest[:16], rest[16:]
    copies = fetch(pieces, (0,) * 16, weights, sems)
    flags[0] = own_ref[SEG:, :DH]
    flags[1] = oth_ref[SEG:, :DH]
    xs[0:SEG, :] = own_ref[0:SEG, :]
    xs[SEG:, :] = oth_ref[0:SEG, :]
    total = accumulate(xs, weights, copies, slice(0, 2 * HALF))
    kv_own[...] = total[:SEG].astype(BF16)
    kv_oth[...] = total[SEG:].astype(BF16)


SCALE = DH**-0.5
QO_PLACES = (2,) * 9 + (0,) + (2,) + (0,) + (2,) * 4


def head(i):
    return slice(i * DH, (i + 1) * DH)


def own_half(ref):
    g = lax.axis_index("grp")
    parts = [jnp.where(g == 0, ref[h : h + 1], ref[HEADS + h : HEADS + h + 1]) for h in range(HEADS)]
    return jnp.concatenate(parts, axis=1)


def query_kernel(xs, cot_own, cot_oth, cb_ref, pb_ref, kv_own, kv_oth, pk_ref, *rest):
    pieces = rest[:16]
    weights, cq_ref, cg_ref, rel_ref, own_ref, dp_ref = rest[16:22]
    cots, sems = rest[22:]
    z, _, _ = place()
    copies = fetch(pieces, QO_PLACES, weights, sems)
    for r in range(ZS):
        cots[0:SEG, r * BLK : (r + 1) * BLK] = cot_own[:, plane_columns(z, r)]
        cots[SEG:, r * BLK : (r + 1) * BLK] = cot_oth[:, plane_columns(z, r)]
    q = accumulate(xs, weights, copies, slice(0, HALF))
    cq = (q + own_half(cb_ref)).astype(BF16)
    pq = (q + own_half(pb_ref)).astype(BF16)
    cg = dot(cots[...], weights[:, HALF:]).astype(BF16)
    row = lax.broadcasted_iota(jnp.int32, (SEG, SEG), 0)
    col = lax.broadcasted_iota(jnp.int32, (SEG, SEG), 1)
    every = [(rec, h) for rec in range(2) for h in range(HEADS)]
    rows = [slice(rec * SEG, (rec + 1) * SEG) for rec in range(2)]
    kv = (kv_own, kv_oth)
    rel = [dot(pq[rows[rec], head(h)], pk_ref[:, head(h)], NT) for rec, h in every]
    own = [dot(cq[rows[rec], head(h)], kv[rec][:, head(h)], NT) for rec, h in every]
    for rec, h in every:
        dp_ref[rec, h] = dot(cg[rows[rec], head(h)], kv[rec][:, head(HEADS + h)], NT)
    for n, (rec, h) in enumerate(every):
        turned = pltpu.roll(rel[n], SEG + 1, 1, stride=1, stride_axis=0)
        rel_ref[rec, h] = turned[:, :SEG]
        s_own = (own[n] + turned[:, SEG:]) * SCALE
        own_ref[rec, h] = jnp.where(col <= row, s_own, -jnp.inf)
    for rec in range(2):
        cq_ref[rec] = cq[rows[rec]]
        cg_ref[rec] = cg[rows[rec]]


def memory_kernel(
    rec, flags, cq_ref, cg_ref, rel_ref, own_ref, dp_ref, kv_ref, mem_ref, *rest
):
    if rec == 0:
        p_ref, ds_ref, dmem_ref, ctx_ref = rest
    else:
        wqo, p_ref, ds_ref, dmem_ref, lo_ref, ctx_ref = rest
    flag = flags[rec, 0:1, :].astype(F32)
    heads = range(HEADS)
    s_mem = [dot(cq_ref[rec, :, head(h)], mem_ref[:, head(h)], NT) for h in heads]
    dp_mem = [dot(cg_ref[rec, :, head(h)], mem_ref[:, head(HEADS + h)], NT) for h in heads]
    parts = []
    for h in heads:
        s = jnp.where(flag == 0, (s_mem[h] + rel_ref[rec, h]) * SCALE, -jnp.inf)
        s_own, dp_own = own_ref[rec, h], dp_ref[rec, h]
        peak = jnp.max(jnp.maximum(s, s_own), axis=-1, keepdims=True)
        e_mem, e_own = jnp.exp(s - peak), jnp.exp(s_own - peak)
        norm = 1.0 / jnp.sum(e_mem + e_own, axis=-1, keepdims=True)
        inner = jnp.sum(e_mem * dp_mem[h] + e_own * dp_own, axis=-1, keepdims=True) * norm
        a_mem, a_own = e_mem * norm, e_own * norm
        p_mem, p_own = a_mem.astype(BF16), a_own.astype(BF16)
        ds_mem = (a_mem * (dp_mem[h] - inner) * SCALE).astype(BF16)
        ds_own = (a_own * (dp_own - inner) * SCALE).astype(BF16)
        p_ref[h] = p_own
        ds_ref[:, 2 * SEG * h : 2 * SEG * h + SEG] = ds_mem
        ds_ref[:, 2 * SEG * h + SEG : 2 * SEG * (h + 1)] = ds_own
        parts.append((p_mem, p_own, ds_mem))
    for h in heads:
        f, fv = head(h), head(HEADS + h)
        p_mem, p_own, ds_mem = parts[h]
        dmem_ref[:, f] = dot(ds_mem, cq_ref[rec, :, f], TN).astype(BF16)
        dmem_ref[:, fv] = dot(p_mem, cg_ref[rec, :, f], TN).astype(BF16)
        ctx = dot(p_mem, mem_ref[:, fv]) + dot(p_own, kv_ref[:, fv])
        ctx_ref[:, f] = ctx.astype(BF16)
    if rec == 1:
        lo_ref[...] = dot(ctx_ref[...], wqo[:, HALF:], NT).astype(BF16)


def grad_kernel(
    rec, p_ref, ds_ref, cq_ref, cg_ref, kv_ref, mem_ref, pk_ref, wqo, np_ref, dkv, dq
):
    row = lax.broadcasted_iota(jnp.int32, (SEG, SEG), 0)
    col = lax.broadcasted_iota(jnp.int32, (SEG, SEG), 1)
    flip = jnp.where(row + col == SEG - 1, 1.0, 0.0).astype(BF16)
    both = [slice(2 * SEG * h, 2 * SEG * (h + 1)) for h in range(HEADS)]
    rel = dot(flip, ds_ref[...])
    rel = [pltpu.roll(rel[:, w], 0, 1, stride=1, stride_axis=0).astype(BF16) for w in both]
    rel = dot(flip, jnp.concatenate(rel, axis=1)).astype(BF16)
    for h, w in enumerate(both):
        f, fv = head(h), head(HEADS + h)
        ds_mem, ds_own = ds_ref[:, w][:, :SEG], ds_ref[:, w][:, SEG:]
        dkv[:, f] = dot(ds_own, cq_ref[rec, :, f], TN).astype(BF16)
        dkv[:, fv] = dot(p_ref[h], cg_ref[rec, :, f], TN).astype(BF16)
        total = dot(ds_mem, mem_ref[:, f]) + dot(ds_own, kv_ref[:, f])
        dq[:, f] = (total + dot(rel[:, w], pk_ref[:, f])).astype(BF16)
    np_ref[...] = dot(dq[...], wqo[:, :HALF], NT)


def returned_kernel(np_ref, dkv_ref, ret_ref, wkv, out_ref):
    dkv = (dkv_ref[...].astype(F32) + ret_ref[...].astype(F32)).astype(BF16)
    out_ref[...] = (np_ref[...] + dot(dkv, wkv[...], NT)).astype(out_ref.dtype)


def own_kernel(
    x_ref, ctx_ref, lo_ret, p_ref, ds_ref, cq_ref, cg_ref, kv_ref, mem_ref, pk_ref, wqo,
    np_ref, dkv, out_ref, dq,
):
    z, _, _ = place()
    grad_kernel(0, p_ref, ds_ref, cq_ref, cg_ref, kv_ref, mem_ref, pk_ref, wqo, np_ref, dkv, dq)
    total = dot(ctx_ref[...], wqo[:, HALF:], NT)
    for r in range(ZS):
        cols, there = slice(r * BLK, (r + 1) * BLK), plane_columns(z, r)
        part = total[:, cols] + lo_ret[:, cols].astype(F32)
        out_ref[0, :, there] = (x_ref[0, :, there].astype(F32) + part).astype(BF16)


def hat_kernel(x_ref, gain_ref, cot_ref, hat_ref, rstd_ref, gain_out, cot_out, held):
    z, _, _ = place()
    x = x_ref[0].astype(F32)
    center = jnp.mean(x, axis=-1, keepdims=True)
    moved = x - center
    spread = jnp.mean(jnp.square(moved), axis=-1, keepdims=True)
    rstd = lax.rsqrt(spread + epsilon)
    held[0:SEG, :] = moved * rstd
    held[SEG:, :] = jnp.broadcast_to(lanes(gain_ref), (8, D))
    rstd_ref[...] = jnp.broadcast_to(rstd, (SEG, 128))
    for r in range(ZS):
        cols, there = slice(r * BLK, (r + 1) * BLK), plane_columns(z, r)
        hat_ref[:, cols] = held[0:SEG, there]
        gain_out[:, cols] = held[SEG:, there]
        cot_out[:, cols] = cot_ref[:, there]


def finish_kernel(hat_ref, rstd_ref, gain_ref, cot_ref, np_own, np_ret, grad_ref):
    z, _, _ = place()
    step = 32
    for i in range(0, SEG, step):
        rows = slice(i, i + step)
        hat, rstd = hat_ref[rows, :], rstd_ref[rows, 0:1]
        g = (np_own[rows, :] + np_ret[rows, :].astype(F32)) * gain_ref[0:1, :]
        mean_g = jnp.mean(g, axis=-1, keepdims=True)
        mean_gh = jnp.mean(g * hat, axis=-1, keepdims=True)
        grad = (rstd * (g - mean_g - hat * mean_gh)).astype(BF16)
        total = cot_ref[rows, :] + grad
        for r in range(ZS):
            grad_ref[0, rows, plane_columns(z, r)] = total[:, r * BLK : (r + 1) * BLK]


def call(kernel, outs, scratch=(), in_specs=None, mib=24):
    return pl.pallas_call(
        kernel,
        out_shape=outs,
        in_specs=in_specs,
        out_specs=jax.tree.map(lambda _: VM, outs),
        scratch_shapes=list(scratch),
        compiler_params=pltpu.CompilerParams(vmem_limit_bytes=mib * 1024 * 1024),
        cost_estimate=pl.CostEstimate(
            flops=0, bytes_accessed=1024, transcendentals=0
        ),
    )


def shape(*dims, dtype=BF16):
    return jax.ShapeDtypeStruct(dims, dtype)


VM = pl.BlockSpec(memory_space=pltpu.VMEM)
SM = pl.BlockSpec(memory_space=pltpu.SMEM)
ANY = pl.BlockSpec(memory_space=pl.ANY)


def moved_by(f):
    route = []
    for z in range(ZS):
        for y in range(2):
            for c in range(2):
                zz, yy, cc = f(z, y, c)
                route.append((4 * z + 2 * y + c, 4 * zz + 2 * yy + cc))
    return lambda block: lax.ppermute(block, "tm", route)


up = moved_by(lambda z, y, c: ((z + 1) % ZS, y, c))
down = moved_by(lambda z, y, c: ((z - 1) % ZS, y, c))
across = moved_by(lambda z, y, c: (z, 1 - y, c))
sibling = moved_by(lambda z, y, c: (z, y, 1 - c))


def after(block, *earlier):
    return lax.optimization_barrier((block, *earlier))[0]


def other(block):
    return lax.ppermute(block, "grp", [(0, 1), (1, 0)])


def split_heads(
    inputs,
    norm_gain,
    query_weight,
    key_weight,
    value_weight,
    output_weight,
    content_bias,
    position_bias,
    position_keys,
    start_flags,
    cotangent,
):
    cot = cotangent[0]
    gain = norm_gain.reshape(D // 128, 128)
    w0, normed, pk = call(
        prepare_kernel,
        (shape(4, ROWS, HALF), shape(SEG + 16, D), shape(2 * SEG, HALF)),
        [
            pltpu.VMEM((SEG, D), BF16),
            pltpu.VMEM((SEG, D), BF16),
            pltpu.VMEM((D // 128, 128), F32),
            pltpu.VMEM((2 * SEG, HALF), BF16),
            pltpu.SemaphoreType.DMA((7,)),
        ],
        [ANY] * 7 + [SM],
        62,
    )(
        key_weight, value_weight, query_weight, output_weight, inputs, gain, position_keys,
        start_flags,
    )
    normed_oth = other(normed)
    w1 = up(w0)
    w0y = across(w0)
    w3 = down(w0)
    w0_near, normed = call(
        stage_kernel, (shape(4, ROWS, HALF), shape(SEG + 16, D)), (), [VM] * 2
    )(w0, normed)
    w1 = after(w1, w0_near)
    cot_oth = other(after(cot, w1))
    w1y = across(w1)
    w2 = up(w1)
    w3y = across(w3)
    w2y_kv = up(after(w1y, w3)[:2])
    w2y_qo = across(after(w2, w3)[2:])
    here = [w0_near, w0y, w1, w1y, w2, w2y_kv, w3, w3y]
    there = [sibling(p) for p in [w0] + here[1:]]
    w2y_qo_there = sibling(w2y_qo)
    kv_pieces = []
    for r in range(ZS):
        kv_pieces += here[2 * r : 2 * r + 2] + there[2 * r : 2 * r + 2]
    qo_pieces = list(kv_pieces)
    qo_pieces[9], qo_pieces[11] = w2y_qo, w2y_qo_there

    half = shape(SEG, 2 * HALF)
    wkv, kv, kv_oth, xs, flags = call(
        key_value_kernel,
        (
            shape(D, 2 * HALF),
            half,
            half,
            shape(2 * SEG, D),
            shape(2, 16, DH),
        ),
        [pltpu.SemaphoreType.DMA((32,))],
        [VM, VM] + [ANY] * 16,
    )(after(normed, w2y_qo, cot_oth), normed_oth, *kv_pieces)
    steps = lax.axis_size("tm")
    onward = [(i, i + 1) for i in range(steps - 1)]
    back = [(i + 1, i) for i in range(steps - 1)]
    mem_oth = lax.ppermute(kv_oth, "tm", onward)
    mem = lax.ppermute(kv, "tm", onward)
    blocks = shape(2, HEADS, SEG, SEG, dtype=F32)
    wqo, cq, cg, rel, s_own, dp_own = call(
        query_kernel,
        (shape(D, 2 * HALF), shape(2, SEG, HALF), shape(2, SEG, HALF), blocks, blocks, blocks),
        [pltpu.VMEM((2 * SEG, D), BF16), pltpu.SemaphoreType.DMA((32,))],
        [VM] * 8 + [ANY] * 16,
    )(
        xs, cot, cot_oth, content_bias.reshape(H, DH), position_bias.reshape(H, DH),
        kv, kv_oth, pk, *qo_pieces,
    )

    def memory(rec, *rows):
        last = shape(SEG, D) if rec else shape(SEG, HALF)
        return call(
            functools.partial(memory_kernel, rec),
            (shape(HEADS, SEG, SEG), shape(SEG, HEADS * 2 * SEG), half, last),
            [pltpu.VMEM((SEG, HALF), BF16)] if rec else (),
            [VM] * (6 + len(rows)),
        )(flags, cq, cg, rel, s_own, dp_own, *rows)

    def grads(rec, p, ds, kv_rows, mem_rows):
        return call(
            functools.partial(grad_kernel, rec),
            (shape(SEG, D, dtype=F32), half),
            [pltpu.VMEM((SEG, HALF), BF16)],
            [VM] * 8,
        )(p, ds, cq, cg, kv_rows, mem_rows, pk, wqo)

    p_oth, ds_oth, dmem_oth, lo_oth = memory(1, kv_oth, mem_oth, wqo)
    lo_ret = other(lo_oth)
    ret_oth = lax.ppermute(dmem_oth, "tm", back)
    partial_oth, dkv_oth = grads(1, after(p_oth, lo_oth), ds_oth, kv_oth, mem_oth)
    np_oth = call(returned_kernel, shape(SEG, D), (), [VM] * 4)(
        partial_oth, dkv_oth, ret_oth, wkv
    )
    np_ret = other(np_oth)
    hat = call(
        hat_kernel,
        (
            shape(SEG, D, dtype=F32),
            shape(SEG, 128, dtype=F32),
            shape(8, D, dtype=F32),
            shape(SEG, D),
        ),
        [pltpu.VMEM((SEG + 8, D), F32)],
        [VM] * 3,
    )(inputs, gain, after(cot, np_oth))
    p, ds, dmem, ctx = memory(0, kv, after(mem, np_oth, hat[0]))
    ret = lax.ppermute(after(dmem, lo_ret), "tm", back)
    partial, dkv, layer_out = call(
        own_kernel,
        (shape(SEG, D, dtype=F32), half, shape(1, SEG, D)),
        [pltpu.VMEM((SEG, HALF), BF16)],
        [VM] * 11,
    )(inputs, ctx, lo_ret, after(p, dmem), ds, cq, cg, kv, mem, pk, wqo)
    np_own = call(returned_kernel, shape(SEG, D, dtype=F32), (), [VM] * 4)(
        partial, dkv, ret, wkv
    )
    input_grad = call(finish_kernel, shape(1, SEG, D), (), [VM] * 6)(
        *hat, after(np_own, hat[0]), np_ret
    )
    return (layer_out, input_grad)


def from_behind(block, axis, distance):
    devices = range(lax.axis_size(axis))
    route = [(i - distance, i) for i in devices if i - distance in devices]
    return lax.ppermute(block, axis, route)


def normalize_project(
    inputs, norm_gain, query_weight, key_weight, value_weight, content_bias, position_bias
):
    widened = inputs.astype(jnp.float32)
    center = jnp.mean(widened, axis=-1, keepdims=True)
    spread = jnp.mean(jnp.square(widened - center), axis=-1, keepdims=True)
    normed = ((widened - center) * lax.rsqrt(spread + epsilon) * norm_gain).astype(jnp.bfloat16)
    projected = jnp.dot(normed, query_weight, preferred_element_type=jnp.float32)
    content_query = (projected + content_bias).astype(jnp.bfloat16)
    position_query = (projected + position_bias).astype(jnp.bfloat16)
    key_rows = jnp.dot(normed, key_weight, preferred_element_type=jnp.float32).astype(jnp.bfloat16)
    value_rows = jnp.dot(normed, value_weight, preferred_element_type=jnp.float32).astype(
        jnp.bfloat16
    )
    return (content_query, position_query, key_rows, value_rows)


def attend(
    content_query,
    position_query,
    key_rows,
    value_rows,
    memory_keys,
    memory_values,
    position_keys,
    keep_memory,
):
    length = content_query.shape[0]
    all_keys = jnp.concatenate([memory_keys, key_rows], axis=0).reshape(2 * length, H, DH)
    all_values = jnp.concatenate([memory_values, value_rows], axis=0).reshape(2 * length, H, DH)
    content = content_query.reshape(length, H, DH)
    located = position_query.reshape(length, H, DH)
    distance_keys = position_keys[::-1].reshape(2 * length, H, DH)
    direct = jnp.einsum("ihd,jhd->hij", content, all_keys, preferred_element_type=jnp.float32)
    relative = jnp.einsum(
        "ihd,jhd->hij", located, distance_keys, preferred_element_type=jnp.float32
    )
    padded = jnp.pad(relative, ((0, 0), (0, 0), (0, 1)))
    skewed = padded.reshape(H, length * (2 * length + 1))[
        :, length - 1 : length - 1 + 2 * length * length
    ]
    skewed = skewed.reshape(H, length, 2 * length)
    scores = (direct + skewed) * DH ** (-0.5)
    key_index = lax.broadcasted_iota(jnp.int32, (length, 2 * length), 1)
    query_index = lax.broadcasted_iota(jnp.int32, (length, 2 * length), 0)
    allowed = (key_index <= query_index + length) & (keep_memory | (key_index >= length))
    scores = jnp.where(allowed[None], scores, -jnp.inf)
    row_peak = lax.stop_gradient(jnp.max(scores, axis=-1, keepdims=True))
    raised = jnp.exp(scores - row_peak)
    attention = (raised / jnp.sum(raised, axis=-1, keepdims=True)).astype(jnp.bfloat16)
    gathered = jnp.einsum("hij,jhd->ihd", attention, all_values, preferred_element_type=jnp.float32)
    return gathered.reshape(length, H * DH).astype(jnp.bfloat16)


def finish(inputs, context, output_weight):
    update = lax.dot_general(
        context,
        output_weight,
        (((context.ndim - 1,), (1,)), ((), ())),
        preferred_element_type=jnp.float32,
    )
    return (inputs.astype(jnp.float32) + update).astype(jnp.bfloat16)


def shards(
    inputs,
    norm_gain,
    query_weight,
    key_weight,
    value_weight,
    output_weight,
    content_bias,
    position_bias,
    position_keys,
    start_flags,
    cotangent,
):
    partial_weights = (
        lax.all_gather(query_weight, "grp", axis=1, tiled=True),
        lax.all_gather(key_weight, "grp", axis=1, tiled=True),
        lax.all_gather(value_weight, "grp", axis=1, tiled=True),
        lax.all_gather(output_weight, "grp", axis=1, tiled=True),
    )
    full_weights = (
        lax.all_gather(partial_weights[0], "tm", axis=0, tiled=True),
        lax.all_gather(partial_weights[1], "tm", axis=0, tiled=True),
        lax.all_gather(partial_weights[2], "tm", axis=0, tiled=True),
        lax.all_gather(partial_weights[3], "tm", axis=0, tiled=True),
    )
    query_full, key_full, value_full, output_full = full_weights
    own_inputs = inputs[0]
    own_cotangent = cotangent[0]
    keep_memory = start_flags[0, 0] == 0

    def project(local_inputs):
        return normalize_project(
            local_inputs, norm_gain, query_full, key_full, value_full, content_bias, position_bias
        )

    projections, project_back = jax.vjp(project, own_inputs)
    content_query, position_query, key_rows, value_rows = projections
    memory_keys, memory_values = from_behind((key_rows, value_rows), "tm", 1)

    def attend_local(
        local_content, local_position, local_keys, local_values, prior_keys, prior_values
    ):
        return attend(
            local_content,
            local_position,
            local_keys,
            local_values,
            prior_keys,
            prior_values,
            position_keys,
            keep_memory,
        )

    context, attend_back = jax.vjp(
        attend_local,
        content_query,
        position_query,
        key_rows,
        value_rows,
        memory_keys,
        memory_values,
    )

    def combine(local_inputs, local_context):
        return finish(local_inputs, local_context, output_full)

    layer_out, finish_back = jax.vjp(combine, own_inputs, context)
    residual_grad, context_grad = finish_back(own_cotangent)
    attend_grads = attend_back(context_grad)
    returned_keys, returned_values = from_behind((attend_grads[4], attend_grads[5]), "tm", -1)
    key_grad = attend_grads[2] + returned_keys
    value_grad = attend_grads[3] + returned_values
    (norm_grad,) = project_back((attend_grads[0], attend_grads[1], key_grad, value_grad))
    input_grad = residual_grad + norm_grad
    return (layer_out[None], input_grad[None])


def solution(mesh):
    in_specs = (
        P("grp", "tm", None),
        P(),
        P("tm", "grp"),
        P("tm", "grp"),
        P("tm", "grp"),
        P("tm", "grp"),
        P(),
        P(),
        P(),
        P("grp", "tm"),
        P("grp", "tm", None),
    )
    out_specs = (P("grp", "tm", None), P("grp", "tm", None))
    split = dict(mesh.shape) == {"grp": 2, "tm": 4 * ZS}
    body = split_heads if split else shards
    return jax.shard_map(body, mesh=mesh, in_specs=in_specs, out_specs=out_specs, check_vma=False)
```

```python
import functools

import jax
import jax.numpy as jnp
from jax import lax
from jax.experimental import pallas as pl
from jax.experimental.pallas import tpu as pltpu
from jax.sharding import PartitionSpec as P

H = 6
DH = 128
epsilon = 1e-05

F32 = jnp.float32
BF16 = jnp.bfloat16
SEG = 128
D = 1536
HALF = 384
HEADS = HALF // DH
ROWS = 96
ZS = 4
BLK = 4 * ROWS
NT = (((1,), (1,)), ((), ()))
TN = (((0,), (0,)), ((), ()))


def dot(a, b, dims=(((1,), (0,)), ((), ()))):
    return lax.dot_general(a, b, dims, preferred_element_type=F32)


def place():
    t = lax.axis_index("tm")
    return t // 4, (t // 2) % 2, t % 2


def plane_columns(z, r):
    return pl.ds(pl.multiple_of(lax.rem(z - r + ZS, ZS) * BLK, 128), BLK)


def lanes(ref):
    return jnp.concatenate([ref[i : i + 1, :] for i in range(ref.shape[0])], axis=1)


def prepare_kernel(
    k_ref, v_ref, q_ref, o_ref, x_ref, gain_ref, pk_ref, flag_ref,
    shard, out_ref, pk_out, held, x_in, gain_in, pk_in, sems,
):
    z, _, _ = place()
    own = pl.ds(pl.multiple_of(lax.axis_index("grp") * HALF, 128), HALF)
    copies = [
        pltpu.make_async_copy(x_ref.at[0], x_in, sems.at[0]),
        pltpu.make_async_copy(gain_ref, gain_in, sems.at[1]),
        pltpu.make_async_copy(pk_ref.at[:, own], pk_in, sems.at[2]),
    ] + [
        pltpu.make_async_copy(ref, shard.at[i], sems.at[3 + i])
        for i, ref in enumerate((k_ref, v_ref, q_ref, o_ref))
    ]
    for copy in copies:
        copy.start()
    for copy in copies:
        copy.wait()
    x = x_in[...].astype(F32)
    center = jnp.mean(x, axis=-1, keepdims=True)
    moved = x - center
    spread = jnp.mean(jnp.square(moved), axis=-1, keepdims=True)
    held[...] = (moved * lax.rsqrt(spread + epsilon) * lanes(gain_in)).astype(BF16)
    for r in range(ZS):
        out_ref[0:SEG, r * BLK : (r + 1) * BLK] = held[:, plane_columns(z, r)]
    flag = flag_ref[0, 0].astype(F32)
    out_ref[SEG:, :] = jnp.full((16, D), flag, F32).astype(BF16)
    row = lax.broadcasted_iota(jnp.int32, (2 * SEG, 2 * SEG), 0)
    col = lax.broadcasted_iota(jnp.int32, (2 * SEG, 2 * SEG), 1)
    flip = jnp.where(row + col == 2 * SEG - 1, 1.0, 0.0).astype(BF16)
    pk_out[...] = dot(flip, pk_in[...]).astype(BF16)


def stage_kernel(shard_ref, normed_ref, shard, normed):
    shard[...] = shard_ref[...]
    normed[...] = normed_ref[...]


def shard_rows(r, j):
    _, y, c = place()
    yy = 1 - y if j % 2 else y
    cc = 1 - c if j // 2 else c
    return pl.ds(pl.multiple_of(r * BLK + (2 * yy + cc) * ROWS, 16), ROWS)


def fetch(pieces, first, weights, sems):
    copies = []
    for n in range(4 * ZS):
        for w in range(2):
            copies.append(
                pltpu.make_async_copy(
                    pieces[n].at[first[n] + w],
                    weights.at[shard_rows(n // 4, n % 4), pl.ds(w * HALF, HALF)],
                    sems.at[2 * n + w],
                )
            )
    for copy in copies:
        copy.start()
    return copies


def accumulate(x, weights, copies, columns):
    for copy in copies:
        copy.wait()
    return dot(x[...], weights[:, columns])


def key_value_kernel(own_ref, oth_ref, *rest):
    pieces, (weights, kv_own, kv_oth, xs, flags, sems) = rest[:16], rest[16:]
    copies = fetch(pieces, (0,) * 16, weights, sems)
    flags[0] = own_ref[SEG:, :DH]
    flags[1] = oth_ref[SEG:, :DH]
    xs[0:SEG, :] = own_ref[0:SEG, :]
    xs[SEG:, :] = oth_ref[0:SEG, :]
    total = accumulate(xs, weights, copies, slice(0, 2 * HALF))
    kv_own[...] = total[:SEG].astype(BF16)
    kv_oth[...] = total[SEG:].astype(BF16)


SCALE = DH**-0.5
QO_PLACES = (2,) * 9 + (0,) + (2,) + (0,) + (2,) * 4


def head(i):
    return slice(i * DH, (i + 1) * DH)


def own_half(ref):
    g = lax.axis_index("grp")
    parts = [jnp.where(g == 0, ref[h : h + 1], ref[HEADS + h : HEADS + h + 1]) for h in range(HEADS)]
    return jnp.concatenate(parts, axis=1)


def query_kernel(xs, cot_own, cot_oth, cb_ref, pb_ref, kv_own, kv_oth, pk_ref, *rest):
    pieces = rest[:16]
    weights, cq_ref, cg_ref, rel_ref, own_ref, dp_ref = rest[16:22]
    cots, sems = rest[22:]
    z, _, _ = place()
    copies = fetch(pieces, QO_PLACES, weights, sems)
    for r in range(ZS):
        cots[0:SEG, r * BLK : (r + 1) * BLK] = cot_own[:, plane_columns(z, r)]
        cots[SEG:, r * BLK : (r + 1) * BLK] = cot_oth[:, plane_columns(z, r)]
    q = accumulate(xs, weights, copies, slice(0, HALF))
    cq = (q + own_half(cb_ref)).astype(BF16)
    pq = (q + own_half(pb_ref)).astype(BF16)
    cg = dot(cots[...], weights[:, HALF:]).astype(BF16)
    row = lax.broadcasted_iota(jnp.int32, (SEG, SEG), 0)
    col = lax.broadcasted_iota(jnp.int32, (SEG, SEG), 1)
    every = [(rec, h) for rec in range(2) for h in range(HEADS)]
    rows = [slice(rec * SEG, (rec + 1) * SEG) for rec in range(2)]
    kv = (kv_own, kv_oth)
    rel = [dot(pq[rows[rec], head(h)], pk_ref[:, head(h)], NT) for rec, h in every]
    own = [dot(cq[rows[rec], head(h)], kv[rec][:, head(h)], NT) for rec, h in every]
    for rec, h in every:
        dp_ref[rec, h] = dot(cg[rows[rec], head(h)], kv[rec][:, head(HEADS + h)], NT)
    for n, (rec, h) in enumerate(every):
        turned = pltpu.roll(rel[n], SEG + 1, 1, stride=1, stride_axis=0)
        rel_ref[rec, h] = turned[:, :SEG]
        s_own = (own[n] + turned[:, SEG:]) * SCALE
        own_ref[rec, h] = jnp.where(col <= row, s_own, -jnp.inf)
    for rec in range(2):
        cq_ref[rec] = cq[rows[rec]]
        cg_ref[rec] = cg[rows[rec]]


def memory_kernel(
    rec, flags, cq_ref, cg_ref, rel_ref, own_ref, dp_ref, kv_ref, mem_ref, *rest
):
    if rec == 0:
        p_ref, ds_ref, dmem_ref, ctx_ref = rest
    else:
        wqo, p_ref, ds_ref, dmem_ref, lo_ref, ctx_ref = rest
    flag = flags[rec, 0:1, :].astype(F32)
    heads = range(HEADS)
    s_mem = [dot(cq_ref[rec, :, head(h)], mem_ref[:, head(h)], NT) for h in heads]
    dp_mem = [dot(cg_ref[rec, :, head(h)], mem_ref[:, head(HEADS + h)], NT) for h in heads]
    parts = []
    for h in heads:
        s = jnp.where(flag == 0, (s_mem[h] + rel_ref[rec, h]) * SCALE, -jnp.inf)
        s_own, dp_own = own_ref[rec, h], dp_ref[rec, h]
        peak = jnp.max(jnp.maximum(s, s_own), axis=-1, keepdims=True)
        e_mem, e_own = jnp.exp(s - peak), jnp.exp(s_own - peak)
        norm = 1.0 / jnp.sum(e_mem + e_own, axis=-1, keepdims=True)
        inner = jnp.sum(e_mem * dp_mem[h] + e_own * dp_own, axis=-1, keepdims=True) * norm
        a_mem, a_own = e_mem * norm, e_own * norm
        p_mem, p_own = a_mem.astype(BF16), a_own.astype(BF16)
        ds_mem = (a_mem * (dp_mem[h] - inner) * SCALE).astype(BF16)
        ds_own = (a_own * (dp_own - inner) * SCALE).astype(BF16)
        p_ref[h] = p_own
        ds_ref[:, 2 * SEG * h : 2 * SEG * h + SEG] = ds_mem
        ds_ref[:, 2 * SEG * h + SEG : 2 * SEG * (h + 1)] = ds_own
        parts.append((p_mem, p_own, ds_mem))
    for h in heads:
        f, fv = head(h), head(HEADS + h)
        p_mem, p_own, ds_mem = parts[h]
        dmem_ref[:, f] = dot(ds_mem, cq_ref[rec, :, f], TN).astype(BF16)
        dmem_ref[:, fv] = dot(p_mem, cg_ref[rec, :, f], TN).astype(BF16)
        ctx = dot(p_mem, mem_ref[:, fv]) + dot(p_own, kv_ref[:, fv])
        ctx_ref[:, f] = ctx.astype(BF16)
    if rec == 1:
        lo_ref[...] = dot(ctx_ref[...], wqo[:, HALF:], NT).astype(BF16)


def grad_kernel(
    rec, p_ref, ds_ref, cq_ref, cg_ref, kv_ref, mem_ref, pk_ref, wqo, np_ref, dkv, dq
):
    row = lax.broadcasted_iota(jnp.int32, (SEG, SEG), 0)
    col = lax.broadcasted_iota(jnp.int32, (SEG, SEG), 1)
    flip = jnp.where(row + col == SEG - 1, 1.0, 0.0).astype(BF16)
    both = [slice(2 * SEG * h, 2 * SEG * (h + 1)) for h in range(HEADS)]
    rel = dot(flip, ds_ref[...])
    rel = [pltpu.roll(rel[:, w], 0, 1, stride=1, stride_axis=0).astype(BF16) for w in both]
    rel = dot(flip, jnp.concatenate(rel, axis=1)).astype(BF16)
    for h, w in enumerate(both):
        f, fv = head(h), head(HEADS + h)
        ds_mem, ds_own = ds_ref[:, w][:, :SEG], ds_ref[:, w][:, SEG:]
        dkv[:, f] = dot(ds_own, cq_ref[rec, :, f], TN).astype(BF16)
        dkv[:, fv] = dot(p_ref[h], cg_ref[rec, :, f], TN).astype(BF16)
        total = dot(ds_mem, mem_ref[:, f]) + dot(ds_own, kv_ref[:, f])
        dq[:, f] = (total + dot(rel[:, w], pk_ref[:, f])).astype(BF16)
    np_ref[...] = dot(dq[...], wqo[:, :HALF], NT)


def returned_kernel(np_ref, dkv_ref, ret_ref, wkv, out_ref):
    dkv = (dkv_ref[...].astype(F32) + ret_ref[...].astype(F32)).astype(BF16)
    out_ref[...] = (np_ref[...] + dot(dkv, wkv[...], NT)).astype(out_ref.dtype)


def own_kernel(
    x_ref, ctx_ref, lo_ret, p_ref, ds_ref, cq_ref, cg_ref, kv_ref, mem_ref, pk_ref, wqo,
    np_ref, dkv, out_ref, dq,
):
    z, _, _ = place()
    grad_kernel(0, p_ref, ds_ref, cq_ref, cg_ref, kv_ref, mem_ref, pk_ref, wqo, np_ref, dkv, dq)
    total = dot(ctx_ref[...], wqo[:, HALF:], NT)
    for r in range(ZS):
        cols, there = slice(r * BLK, (r + 1) * BLK), plane_columns(z, r)
        part = total[:, cols] + lo_ret[:, cols].astype(F32)
        out_ref[0, :, there] = (x_ref[0, :, there].astype(F32) + part).astype(BF16)


def hat_kernel(x_ref, gain_ref, cot_ref, hat_ref, rstd_ref, gain_out, cot_out, held):
    z, _, _ = place()
    x = x_ref[0].astype(F32)
    center = jnp.mean(x, axis=-1, keepdims=True)
    moved = x - center
    spread = jnp.mean(jnp.square(moved), axis=-1, keepdims=True)
    rstd = lax.rsqrt(spread + epsilon)
    held[0:SEG, :] = moved * rstd
    held[SEG:, :] = jnp.broadcast_to(lanes(gain_ref), (8, D))
    rstd_ref[...] = jnp.broadcast_to(rstd, (SEG, 128))
    for r in range(ZS):
        cols, there = slice(r * BLK, (r + 1) * BLK), plane_columns(z, r)
        hat_ref[:, cols] = held[0:SEG, there]
        gain_out[:, cols] = held[SEG:, there]
        cot_out[:, cols] = cot_ref[:, there]


def finish_kernel(hat_ref, rstd_ref, gain_ref, cot_ref, np_own, np_ret, grad_ref):
    z, _, _ = place()
    step = 16
    for i in range(0, SEG, step):
        rows = slice(i, i + step)
        hat, rstd = hat_ref[rows, :], rstd_ref[rows, 0:1]
        g = (np_own[rows, :] + np_ret[rows, :].astype(F32)) * gain_ref[0:1, :]
        mean_g = jnp.mean(g, axis=-1, keepdims=True)
        mean_gh = jnp.mean(g * hat, axis=-1, keepdims=True)
        grad = (rstd * (g - mean_g - hat * mean_gh)).astype(BF16)
        total = cot_ref[rows, :] + grad
        for r in range(ZS):
            grad_ref[0, rows, plane_columns(z, r)] = total[:, r * BLK : (r + 1) * BLK]


def call(kernel, outs, scratch=(), in_specs=None, mib=24):
    return pl.pallas_call(
        kernel,
        out_shape=outs,
        in_specs=in_specs,
        out_specs=jax.tree.map(lambda _: VM, outs),
        scratch_shapes=list(scratch),
        compiler_params=pltpu.CompilerParams(vmem_limit_bytes=mib * 1024 * 1024),
        cost_estimate=pl.CostEstimate(
            flops=0, bytes_accessed=1024, transcendentals=0
        ),
    )


def shape(*dims, dtype=BF16):
    return jax.ShapeDtypeStruct(dims, dtype)


VM = pl.BlockSpec(memory_space=pltpu.VMEM)
SM = pl.BlockSpec(memory_space=pltpu.SMEM)
ANY = pl.BlockSpec(memory_space=pl.ANY)


def moved_by(f):
    route = []
    for z in range(ZS):
        for y in range(2):
            for c in range(2):
                zz, yy, cc = f(z, y, c)
                route.append((4 * z + 2 * y + c, 4 * zz + 2 * yy + cc))
    return lambda block: lax.ppermute(block, "tm", route)


up = moved_by(lambda z, y, c: ((z + 1) % ZS, y, c))
down = moved_by(lambda z, y, c: ((z - 1) % ZS, y, c))
across = moved_by(lambda z, y, c: (z, 1 - y, c))
sibling = moved_by(lambda z, y, c: (z, y, 1 - c))


def after(block, *earlier):
    return lax.optimization_barrier((block, *earlier))[0]


def other(block):
    return lax.ppermute(block, "grp", [(0, 1), (1, 0)])


def split_heads(
    inputs,
    norm_gain,
    query_weight,
    key_weight,
    value_weight,
    output_weight,
    content_bias,
    position_bias,
    position_keys,
    start_flags,
    cotangent,
):
    cot = cotangent[0]
    gain = norm_gain.reshape(D // 128, 128)
    w0, normed, pk = call(
        prepare_kernel,
        (shape(4, ROWS, HALF), shape(SEG + 16, D), shape(2 * SEG, HALF)),
        [
            pltpu.VMEM((SEG, D), BF16),
            pltpu.VMEM((SEG, D), BF16),
            pltpu.VMEM((D // 128, 128), F32),
            pltpu.VMEM((2 * SEG, HALF), BF16),
            pltpu.SemaphoreType.DMA((7,)),
        ],
        [ANY] * 7 + [SM],
        62,
    )(
        key_weight, value_weight, query_weight, output_weight, inputs, gain, position_keys,
        start_flags,
    )
    normed_oth = other(normed)
    w1 = up(w0)
    w0y = across(w0)
    w3 = down(w0)
    w0_near, normed = call(
        stage_kernel, (shape(4, ROWS, HALF), shape(SEG + 16, D)), (), [VM] * 2
    )(w0, normed)
    w1 = after(w1, w0_near)
    cot_oth = other(after(cot, w1))
    w1y = across(w1)
    w2 = up(w1)
    w3y = across(w3)
    w2y_kv = up(after(w1y, w3)[:2])
    w2y_qo = across(after(w2, w3)[2:])
    here = [w0_near, w0y, w1, w1y, w2, w2y_kv, w3, w3y]
    there = [sibling(p) for p in [w0] + here[1:]]
    w2y_qo_there = sibling(w2y_qo)
    kv_pieces = []
    for r in range(ZS):
        kv_pieces += here[2 * r : 2 * r + 2] + there[2 * r : 2 * r + 2]
    qo_pieces = list(kv_pieces)
    qo_pieces[9], qo_pieces[11] = w2y_qo, w2y_qo_there

    half = shape(SEG, 2 * HALF)
    wkv, kv, kv_oth, xs, flags = call(
        key_value_kernel,
        (
            shape(D, 2 * HALF),
            half,
            half,
            shape(2 * SEG, D),
            shape(2, 16, DH),
        ),
        [pltpu.SemaphoreType.DMA((32,))],
        [VM, VM] + [ANY] * 16,
    )(after(normed, w2y_qo, cot_oth), normed_oth, *kv_pieces)
    steps = lax.axis_size("tm")
    onward = [(i, i + 1) for i in range(steps - 1)]
    back = [(i + 1, i) for i in range(steps - 1)]
    mem_oth = lax.ppermute(kv_oth, "tm", onward)
    mem = lax.ppermute(kv, "tm", onward)
    blocks = shape(2, HEADS, SEG, SEG, dtype=F32)
    wqo, cq, cg, rel, s_own, dp_own = call(
        query_kernel,
        (shape(D, 2 * HALF), shape(2, SEG, HALF), shape(2, SEG, HALF), blocks, blocks, blocks),
        [pltpu.VMEM((2 * SEG, D), BF16), pltpu.SemaphoreType.DMA((32,))],
        [VM] * 8 + [ANY] * 16,
    )(
        xs, cot, cot_oth, content_bias.reshape(H, DH), position_bias.reshape(H, DH),
        kv, kv_oth, pk, *qo_pieces,
    )

    def memory(rec, *rows):
        last = shape(SEG, D) if rec else shape(SEG, HALF)
        return call(
            functools.partial(memory_kernel, rec),
            (shape(HEADS, SEG, SEG), shape(SEG, HEADS * 2 * SEG), half, last),
            [pltpu.VMEM((SEG, HALF), BF16)] if rec else (),
            [VM] * (6 + len(rows)),
        )(flags, cq, cg, rel, s_own, dp_own, *rows)

    def grads(rec, p, ds, kv_rows, mem_rows):
        return call(
            functools.partial(grad_kernel, rec),
            (shape(SEG, D, dtype=F32), half),
            [pltpu.VMEM((SEG, HALF), BF16)],
            [VM] * 8,
        )(p, ds, cq, cg, kv_rows, mem_rows, pk, wqo)

    p_oth, ds_oth, dmem_oth, lo_oth = memory(1, kv_oth, mem_oth, wqo)
    lo_ret = other(lo_oth)
    ret_oth = lax.ppermute(dmem_oth, "tm", back)
    partial_oth, dkv_oth = grads(1, after(p_oth, lo_oth), ds_oth, kv_oth, mem_oth)
    np_oth = call(returned_kernel, shape(SEG, D), (), [VM] * 4)(
        partial_oth, dkv_oth, ret_oth, wkv
    )
    np_ret = other(np_oth)
    hat = call(
        hat_kernel,
        (
            shape(SEG, D, dtype=F32),
            shape(SEG, 128, dtype=F32),
            shape(8, D, dtype=F32),
            shape(SEG, D),
        ),
        [pltpu.VMEM((SEG + 8, D), F32)],
        [VM] * 3,
    )(inputs, gain, after(cot, np_oth))
    p, ds, dmem, ctx = memory(0, kv, after(mem, np_oth, hat[0]))
    ret = lax.ppermute(after(dmem, lo_ret), "tm", back)
    partial, dkv, layer_out = call(
        own_kernel,
        (shape(SEG, D, dtype=F32), half, shape(1, SEG, D)),
        [pltpu.VMEM((SEG, HALF), BF16)],
        [VM] * 11,
    )(inputs, ctx, lo_ret, after(p, dmem), ds, cq, cg, kv, mem, pk, wqo)
    np_own = call(returned_kernel, shape(SEG, D, dtype=F32), (), [VM] * 4)(
        partial, dkv, ret, wkv
    )
    input_grad = call(finish_kernel, shape(1, SEG, D), (), [VM] * 6)(
        *hat, after(np_own, hat[0]), np_ret
    )
    return (layer_out, input_grad)


def from_behind(block, axis, distance):
    devices = range(lax.axis_size(axis))
    route = [(i - distance, i) for i in devices if i - distance in devices]
    return lax.ppermute(block, axis, route)


def normalize_project(
    inputs, norm_gain, query_weight, key_weight, value_weight, content_bias, position_bias
):
    widened = inputs.astype(jnp.float32)
    center = jnp.mean(widened, axis=-1, keepdims=True)
    spread = jnp.mean(jnp.square(widened - center), axis=-1, keepdims=True)
    normed = ((widened - center) * lax.rsqrt(spread + epsilon) * norm_gain).astype(jnp.bfloat16)
    projected = jnp.dot(normed, query_weight, preferred_element_type=jnp.float32)
    content_query = (projected + content_bias).astype(jnp.bfloat16)
    position_query = (projected + position_bias).astype(jnp.bfloat16)
    key_rows = jnp.dot(normed, key_weight, preferred_element_type=jnp.float32).astype(jnp.bfloat16)
    value_rows = jnp.dot(normed, value_weight, preferred_element_type=jnp.float32).astype(
        jnp.bfloat16
    )
    return (content_query, position_query, key_rows, value_rows)


def attend(
    content_query,
    position_query,
    key_rows,
    value_rows,
    memory_keys,
    memory_values,
    position_keys,
    keep_memory,
):
    length = content_query.shape[0]
    all_keys = jnp.concatenate([memory_keys, key_rows], axis=0).reshape(2 * length, H, DH)
    all_values = jnp.concatenate([memory_values, value_rows], axis=0).reshape(2 * length, H, DH)
    content = content_query.reshape(length, H, DH)
    located = position_query.reshape(length, H, DH)
    distance_keys = position_keys[::-1].reshape(2 * length, H, DH)
    direct = jnp.einsum("ihd,jhd->hij", content, all_keys, preferred_element_type=jnp.float32)
    relative = jnp.einsum(
        "ihd,jhd->hij", located, distance_keys, preferred_element_type=jnp.float32
    )
    padded = jnp.pad(relative, ((0, 0), (0, 0), (0, 1)))
    skewed = padded.reshape(H, length * (2 * length + 1))[
        :, length - 1 : length - 1 + 2 * length * length
    ]
    skewed = skewed.reshape(H, length, 2 * length)
    scores = (direct + skewed) * DH ** (-0.5)
    key_index = lax.broadcasted_iota(jnp.int32, (length, 2 * length), 1)
    query_index = lax.broadcasted_iota(jnp.int32, (length, 2 * length), 0)
    allowed = (key_index <= query_index + length) & (keep_memory | (key_index >= length))
    scores = jnp.where(allowed[None], scores, -jnp.inf)
    row_peak = lax.stop_gradient(jnp.max(scores, axis=-1, keepdims=True))
    raised = jnp.exp(scores - row_peak)
    attention = (raised / jnp.sum(raised, axis=-1, keepdims=True)).astype(jnp.bfloat16)
    gathered = jnp.einsum("hij,jhd->ihd", attention, all_values, preferred_element_type=jnp.float32)
    return gathered.reshape(length, H * DH).astype(jnp.bfloat16)


def finish(inputs, context, output_weight):
    update = lax.dot_general(
        context,
        output_weight,
        (((context.ndim - 1,), (1,)), ((), ())),
        preferred_element_type=jnp.float32,
    )
    return (inputs.astype(jnp.float32) + update).astype(jnp.bfloat16)


def shards(
    inputs,
    norm_gain,
    query_weight,
    key_weight,
    value_weight,
    output_weight,
    content_bias,
    position_bias,
    position_keys,
    start_flags,
    cotangent,
):
    partial_weights = (
        lax.all_gather(query_weight, "grp", axis=1, tiled=True),
        lax.all_gather(key_weight, "grp", axis=1, tiled=True),
        lax.all_gather(value_weight, "grp", axis=1, tiled=True),
        lax.all_gather(output_weight, "grp", axis=1, tiled=True),
    )
    full_weights = (
        lax.all_gather(partial_weights[0], "tm", axis=0, tiled=True),
        lax.all_gather(partial_weights[1], "tm", axis=0, tiled=True),
        lax.all_gather(partial_weights[2], "tm", axis=0, tiled=True),
        lax.all_gather(partial_weights[3], "tm", axis=0, tiled=True),
    )
    query_full, key_full, value_full, output_full = full_weights
    own_inputs = inputs[0]
    own_cotangent = cotangent[0]
    keep_memory = start_flags[0, 0] == 0

    def project(local_inputs):
        return normalize_project(
            local_inputs, norm_gain, query_full, key_full, value_full, content_bias, position_bias
        )

    projections, project_back = jax.vjp(project, own_inputs)
    content_query, position_query, key_rows, value_rows = projections
    memory_keys, memory_values = from_behind((key_rows, value_rows), "tm", 1)

    def attend_local(
        local_content, local_position, local_keys, local_values, prior_keys, prior_values
    ):
        return attend(
            local_content,
            local_position,
            local_keys,
            local_values,
            prior_keys,
            prior_values,
            position_keys,
            keep_memory,
        )

    context, attend_back = jax.vjp(
        attend_local,
        content_query,
        position_query,
        key_rows,
        value_rows,
        memory_keys,
        memory_values,
    )

    def combine(local_inputs, local_context):
        return finish(local_inputs, local_context, output_full)

    layer_out, finish_back = jax.vjp(combine, own_inputs, context)
    residual_grad, context_grad = finish_back(own_cotangent)
    attend_grads = attend_back(context_grad)
    returned_keys, returned_values = from_behind((attend_grads[4], attend_grads[5]), "tm", -1)
    key_grad = attend_grads[2] + returned_keys
    value_grad = attend_grads[3] + returned_values
    (norm_grad,) = project_back((attend_grads[0], attend_grads[1], key_grad, value_grad))
    input_grad = residual_grad + norm_grad
    return (layer_out[None], input_grad[None])


def solution(mesh):
    in_specs = (
        P("grp", "tm", None),
        P(),
        P("tm", "grp"),
        P("tm", "grp"),
        P("tm", "grp"),
        P("tm", "grp"),
        P(),
        P(),
        P(),
        P("grp", "tm"),
        P("grp", "tm", None),
    )
    out_specs = (P("grp", "tm", None), P("grp", "tm", None))
    split = dict(mesh.shape) == {"grp": 2, "tm": 4 * ZS}
    body = split_heads if split else shards
    return jax.shard_map(body, mesh=mesh, in_specs=in_specs, out_specs=out_specs, check_vma=False)
```
